32 devices in a mesh: depth: 4 (over y, x), tile: 8 (over z, core).
Axes of the slice: x: 2, y: 2, z: 4, core: 2. Of those that a mesh axis runs over, the one named last changes fastest.
Arguments:
- field: float32 [64, 256, 1024], P('depth', None, 'tile'), may hold values from -6 to 6
- light_vectors: float32 [16, 3], replicated, may hold values from -4 to 4
- transfer: float32 [16, 4, 8], replicated, may hold values from 0.05 to 1
- light_index: int32 [4], replicated, may hold values from 0 to 15
- flips: int32 [8], P('tile'), may hold values from 0 to 1
Outputs:
- frames: float32 [4, 4, 256, 1024], P(None, None, 'depth', 'tile')
The draws below stay inside these ranges and needn't reach their ends.
All inputs are finite; a program needn't handle non-finite values.
Results may differ from the reference program's by a relative error of at most 0.0003.
Values sent between devices are 32-bit elements; how exact they have to be, the bound alone decides.
No kernel may reach another device: no remote copies, remote signals or barrier semaphores. Data moves between devices by JAX's collectives and lax.ppermute only.
A program may use at most 128 MiB of HBM per device.

```python
import jax
import jax.numpy as jnp
from jax import lax

BX = 128
BY = 256
PASSES = 4
LIGHTS = 16
KNOTS = 8
TILES = 8
NZ = 64
NX = 1024


def with_ends(values, key, least, top_value):
    index_at = [jax.random.randint(jax.random.fold_in(key, axis), (), 0, length) for axis, length in enumerate(values.shape)]
    main_axis = values.shape.index(max(values.shape))
    next_to = index_at[:main_axis] + [(index_at[main_axis] + 1) % values.shape[main_axis]] + index_at[main_axis + 1:]
    return values.at[tuple(index_at)].set(least).at[tuple(next_to)].set(top_value)


def levels(stream_key, shape, shards, least, largest):
    factor_of = 1.0
    for dim, blocks in shards:
        heights = jax.random.uniform(jax.random.fold_in(jax.random.fold_in(stream_key, 6), dim), (blocks,), jnp.float32, least / len(shards), largest / len(shards))
        factor_of = factor_of * jnp.repeat(jnp.exp(heights), shape[dim] // blocks).reshape((-1,) + (1,) * (len(shape) - 1 - dim))
    return factor_of


def bell_draw(own_key, shape, deviation, bound, split=(), kind=jnp.bfloat16):
    drawn = deviation * jax.random.normal(own_key, shape, jnp.float32)
    if split:
        drawn = drawn * levels(own_key, shape, split, -0.22, 0.18)
    return jnp.clip(drawn, -bound, bound).astype(kind)


def setup_inputs(seed: int = 0) -> dict:
    splits = jax.random.split(jax.random.key(seed), 6)
    field = bell_draw(splits[0], (NZ, BY, NX), 1.0, 6.0, ((0, 4), (2, 8)), jnp.float32)
    light_vectors = bell_draw(splits[1], (LIGHTS, 3), 1.0, 4.0, (), jnp.float32)
    transfer = jnp.clip(jax.random.uniform(splits[2], (LIGHTS, 4, KNOTS), jnp.float32, 0.05, 1.0), 0.05, 1.0)
    light_index = with_ends(jax.random.randint(splits[3], (PASSES,), 0, LIGHTS), jax.random.fold_in(splits[3], 1), 0, LIGHTS - 1).astype(jnp.int32)
    flips = with_ends(jax.random.randint(splits[4], (TILES,), 0, 2), jax.random.fold_in(splits[4], 1), 0, 1).astype(jnp.int32)
    return dict(field=field, light_vectors=light_vectors, transfer=transfer, light_index=light_index, flips=flips)


AMBIENT = 0.3

def shade_cells(values, grad_z, grad_y, grad_x, light_vec, curve, opacity_scale):
    knot_count = curve.shape[-1]
    position = jax.nn.sigmoid(values) * (knot_count - 1)
    mixed = [jnp.zeros_like(values) for channel in range(4)]
    for knot_index in range(knot_count):
        tent = jnp.maximum(0.0, 1.0 - jnp.abs(position - knot_index))
        mixed = [mixed[channel] + tent * curve[channel, knot_index] for channel in range(4)]
    facing = grad_x * light_vec[0] + grad_y * light_vec[1] + grad_z * light_vec[2]
    bright = AMBIENT + jnp.abs(facing) / jnp.sqrt(grad_x * grad_x + grad_y * grad_y + grad_z * grad_z + 1.0)
    opacity = mixed[3] * opacity_scale
    emitted = [mixed[channel] * bright * opacity for channel in range(3)]
    return (emitted, opacity)

def march(emitted, opacity, flip):
    log_keep = jnp.log1p(-opacity)
    running = jnp.cumsum(log_keep, axis=0)
    column_sum = running[-1]
    before = jnp.where(flip == 1, column_sum[None] - running, running - log_keep)
    carried = jnp.exp(before)
    colors = [lax.optimization_barrier(jnp.sum(carried * emitted[channel], axis=0)) for channel in range(3)]
    return jnp.stack(colors + [jnp.exp(column_sum)])

def reference(field, light_vectors, transfer, light_index, flips):
    scale = 2.0 / field.shape[0]
    padded = jnp.pad(field, ((1, 1), (1, 1), (1, 1)))

    def render_tile(tile_index):
        start = (tile_index * BX).astype(jnp.int32)
        block = lax.dynamic_slice_in_dim(padded, start, BX + 2, 2)
        center = block[1:-1, 1:-1, 1:-1]
        grad_z = (block[2:, 1:-1, 1:-1] - block[:-2, 1:-1, 1:-1]) * 0.5
        grad_y = (block[1:-1, 2:, 1:-1] - block[1:-1, :-2, 1:-1]) * 0.5
        grad_x = (block[1:-1, 1:-1, 2:] - block[1:-1, 1:-1, :-2]) * 0.5
        flip = flips[tile_index]
        images = []
        for pass_index in range(PASSES):
            chosen = light_index[pass_index]
            emitted, opacity = shade_cells(center, grad_z, grad_y, grad_x, light_vectors[chosen], transfer[chosen], scale)
            images.append(march(emitted, opacity, flip))
        return jnp.stack(images)
    tiled = lax.map(render_tile, jnp.arange(TILES, dtype=jnp.int32))
    images = jnp.transpose(tiled, (1, 2, 3, 0, 4)).reshape(PASSES, 4, BY, TILES * BX)
    return jnp.concatenate([images[:, :3], 1.0 - images[:, 3:]], axis=1)
```

```python
import functools

import jax
import jax.numpy as jnp
from jax import lax
from jax.experimental import pallas as pl
from jax.experimental.pallas import tpu as pltpu
from jax.sharding import PartitionSpec as P

AMBIENT = 0.3
OPACITY = 2.0
SUB = 8
VMEM = pltpu.VMEM
SMEM = pltpu.SMEM


def edge_kernel(parts, field_ref, out_ref):
    cells, _, cols = field_ref.shape
    rows = out_ref.shape[0]
    lane_pair = lax.broadcasted_iota(jnp.int32, (SUB, cols), 1) // 2

    def tile(i, carry):
        acc = jnp.zeros((SUB, cols), jnp.float32)
        for part in range(parts):
            for z in range(cells):
                slot = part * cells + z
                start = pl.multiple_of(part * rows + i * SUB, SUB)
                value = field_ref[z, pl.ds(start, SUB), :]
                moved = pltpu.roll(value, (2 * slot + 1) % cols, 1)
                acc = jnp.where(lane_pair == slot, moved, acc)
        out_ref[pl.ds(pl.multiple_of(i * SUB, SUB), SUB), :] = acc
        return carry

    lax.fori_loop(0, rows // SUB, tile, 0)


def pack_kernel(parts, field_ref, left_ref, right_ref, out_ref):
    cells, all_rows, cols = field_ref.shape
    rows = all_rows // parts
    tall = rows + 2
    lane = lax.broadcasted_iota(jnp.int32, (rows, cols), 1)
    sides = jnp.where(lane % 2 == 0, left_ref[...], right_ref[...])
    zero = jnp.zeros((1, cols), jnp.float32)
    for part in range(parts):
        low = part * rows
        out_ref[part, cells * tall :, :] = sides
        for z in range(cells):
            at = z * tall
            out_ref[part, at + 1 : at + 1 + rows, :] = field_ref[z, low : low + rows, :]
            above = field_ref[z, low - 1 : low, :] if part > 0 else zero
            below = field_ref[z, low + rows : low + rows + 1, :] if part < parts - 1 else zero
            out_ref[part, at : at + 1, :] = above
            out_ref[part, at + 1 + rows : at + 2 + rows, :] = below


def shade_kernel(parts, cells, passes, knots, unroll, scal_ref, lights_ref, curves_ref, bricks_ref, out_ref):
    cols = bricks_ref.shape[2]
    rows = out_ref.shape[2]
    tall = rows + 2
    depth = parts * cells
    me = scal_ref[0]
    flip = scal_ref[1]
    step = 1 - 2 * flip
    first = flip * (depth - 1)
    signed = step.astype(jnp.float32)
    scale = OPACITY / depth
    lane = lax.broadcasted_iota(jnp.int32, (SUB, cols), 1)
    is_first = lane == 0
    is_last = lane == cols - 1

    def bends(index, channel, factor):
        points = [curves_ref[index, channel * knots + k] * factor for k in range(knots)]
        slopes = [points[k + 1] - points[k] for k in range(knots - 1)]
        return [points[0], slopes[0]] + [slopes[k] - slopes[k - 1] for k in range(1, knots - 1)]

    chosen = [scal_ref[2 + p] for p in range(passes)]
    vectors = [[lights_ref[chosen[p], axis] for axis in range(3)] for p in range(passes)]
    for p in range(passes):
        vectors[p][2] = vectors[p][2] * signed
    curves = [bends(chosen[p], 3, scale) for p in range(passes)]

    def row_tile(i, carry):
        base = i * SUB
        lateral = jnp.zeros((SUB, cols), jnp.float32)
        for part in range(parts):
            got = bricks_ref[part, pl.ds(cells * tall + base, SUB), :]
            moved = pltpu.roll(got, (2 * cells * (part - me + parts)) % cols, 1)
            lateral = jnp.where(lane // (2 * cells) == part, moved, lateral)

        def load(z, shift):
            return bricks_ref[z // cells, pl.ds(z % cells * tall + base + shift, SUB), :]

        def one(s, state):
            before, here, keep, sums = state
            z = first + step * s
            follow = jnp.clip(z + step, 0, depth - 1)
            after = jnp.where(s < depth - 1, load(follow, 1), 0.0)
            edge = pltpu.roll(lateral, (cols - 1 - 2 * z) % cols, 1)
            grad_x = pltpu.roll(jnp.where(is_first, edge, here), cols - 1, 1) - pltpu.roll(
                jnp.where(is_last, edge, here), 1, 1
            )
            grad_y = load(z, 2) - load(z, 0)
            grad_z = after - before
            inverse = lax.rsqrt(grad_x * grad_x + grad_y * grad_y + grad_z * grad_z + 4.0)
            half = 0.5 * (knots - 1)
            position = half + half * jnp.tanh(0.5 * here)
            hinges = [position] + [jnp.maximum(position - k, 0.0) for k in range(1, knots - 1)]
            new_keep, new_sums = [], []
            for p in range(passes):
                opacity = curves[p][0] + curves[p][1] * hinges[0]
                for k in range(1, knots - 1):
                    opacity = opacity + curves[p][k + 1] * hinges[k]
                facing = grad_x * vectors[p][0] + grad_y * vectors[p][1] + grad_z * vectors[p][2]
                bright = AMBIENT + jnp.abs(facing) * inverse
                taken = keep[p] * opacity
                weight = taken * bright
                new_keep.append(keep[p] - taken)
                new_sums.append([sums[p][0] + weight] + [sums[p][k + 1] + weight * hinges[k] for k in range(knots - 1)])
            return here, after, new_keep, new_sums

        def group(g, state):
            for u in range(unroll):
                state = one(g * unroll + u, state)
            return state

        zero = jnp.zeros((SUB, cols), jnp.float32)
        start = (
            zero,
            load(first, 1),
            [jnp.ones((SUB, cols), jnp.float32)] * passes,
            [[zero] * knots] * passes,
        )
        _, _, keep, sums = lax.fori_loop(0, depth // unroll, group, start)
        at = pl.ds(pl.multiple_of(base, SUB), SUB)
        for p in range(passes):
            for channel in range(3):
                curve = bends(chosen[p], channel, 1.0)
                color = curve[0] * sums[p][0]
                for k in range(1, knots):
                    color = color + curve[k] * sums[p][k]
                out_ref[p, channel, at, :] = color
            out_ref[p, 3, at, :] = 1.0 - keep[p]
        return carry

    lax.fori_loop(0, rows // SUB, row_tile, 0)


def shift_along(block, axis, amount):
    count = lax.axis_size(axis)
    route = [(i, i + amount) for i in range(count) if 0 <= i + amount < count]
    return lax.ppermute(block, axis, route)


def on_device(field, light_vectors, transfer, light_index, flips):
    parts = lax.axis_size("depth")
    cells, all_rows, cols = field.shape
    rows = all_rows // parts
    passes = light_index.shape[0]
    lights, channels, knots = transfer.shape
    message = cells * (rows + 2) + rows

    edges = pl.pallas_call(
        functools.partial(edge_kernel, parts),
        out_shape=jax.ShapeDtypeStruct((rows, cols), jnp.float32),
        in_specs=[pl.BlockSpec(memory_space=VMEM)],
        out_specs=pl.BlockSpec(memory_space=VMEM),
        name="edges",
    )(field)
    left = shift_along(edges, "tile", 1)
    right = shift_along(edges, "tile", -1)
    packed = pl.pallas_call(
        functools.partial(pack_kernel, parts),
        out_shape=jax.ShapeDtypeStruct((parts, message, cols), jnp.float32),
        in_specs=[pl.BlockSpec(memory_space=VMEM)] * 3,
        out_specs=pl.BlockSpec(memory_space=VMEM),
        name="pack",
    )(field, left, right)
    bricks = lax.all_to_all(packed, "depth", 0, 0, tiled=True)
    scal = jnp.concatenate([lax.axis_index("depth").astype(jnp.int32)[None], flips, light_index])
    return pl.pallas_call(
        functools.partial(shade_kernel, parts, cells, passes, knots, 2),
        out_shape=jax.ShapeDtypeStruct((passes, channels, rows, cols), jnp.float32),
        in_specs=[pl.BlockSpec(memory_space=SMEM)] * 3 + [pl.BlockSpec(memory_space=VMEM)],
        out_specs=pl.BlockSpec(memory_space=VMEM),
        name="shade",
    )(scal, light_vectors, transfer.reshape(lights, channels * knots), bricks)


def solution(mesh):
    in_specs = (P("depth", None, "tile"), P(), P(), P(), P("tile"))
    out_specs = P(None, None, "depth", "tile")
    return jax.shard_map(
        on_device, mesh=mesh, in_specs=in_specs, out_specs=out_specs, check_vma=False
    )
```

```python
import functools

import jax
import jax.numpy as jnp
from jax import lax
from jax.experimental import pallas as pl
from jax.experimental.pallas import tpu as pltpu
from jax.sharding import PartitionSpec as P

AMBIENT = 0.3
OPACITY = 2.0
SUB = 8
VMEM = pltpu.VMEM
SMEM = pltpu.SMEM


def edge_kernel(parts, field_ref, out_ref):
    cells, _, cols = field_ref.shape
    rows = out_ref.shape[0]
    lane_pair = lax.broadcasted_iota(jnp.int32, (SUB, cols), 1) // 2

    def tile(i, carry):
        acc = jnp.zeros((SUB, cols), jnp.float32)
        for part in range(parts):
            for z in range(cells):
                slot = part * cells + z
                start = pl.multiple_of(part * rows + i * SUB, SUB)
                value = field_ref[z, pl.ds(start, SUB), :]
                moved = pltpu.roll(value, (2 * slot + 1) % cols, 1)
                acc = jnp.where(lane_pair == slot, moved, acc)
        out_ref[pl.ds(pl.multiple_of(i * SUB, SUB), SUB), :] = acc
        return carry

    lax.fori_loop(0, rows // SUB, tile, 0)


def pack_kernel(parts, field_ref, left_ref, right_ref, out_ref):
    cells, all_rows, cols = field_ref.shape
    rows = all_rows // parts
    tall = rows + 2
    lane = lax.broadcasted_iota(jnp.int32, (rows, cols), 1)
    sides = jnp.where(lane % 2 == 0, left_ref[...], right_ref[...])
    zero = jnp.zeros((1, cols), jnp.float32)
    for part in range(parts):
        low = part * rows
        out_ref[part, cells * tall :, :] = sides
        for z in range(cells):
            at = z * tall
            out_ref[part, at + 1 : at + 1 + rows, :] = field_ref[z, low : low + rows, :]
            above = field_ref[z, low - 1 : low, :] if part > 0 else zero
            below = field_ref[z, low + rows : low + rows + 1, :] if part < parts - 1 else zero
            out_ref[part, at : at + 1, :] = above
            out_ref[part, at + 1 + rows : at + 2 + rows, :] = below


def shade_kernel(parts, cells, passes, knots, unroll, scal_ref, lights_ref, curves_ref, bricks_ref, out_ref, cell_ref):
    cols = bricks_ref.shape[2]
    rows = out_ref.shape[2]
    tall = rows + 2
    depth = parts * cells
    me = scal_ref[0]
    flip = scal_ref[1]
    step = 1 - 2 * flip
    first = flip * (depth - 1)
    scale = OPACITY / depth
    lane = lax.broadcasted_iota(jnp.int32, (SUB, cols), 1)
    is_first = lane == 0
    is_last = lane == cols - 1

    def bends(index, channel, factor):
        points = [curves_ref[index, channel * knots + k] * factor for k in range(knots)]
        slopes = [points[k + 1] - points[k] for k in range(knots - 1)]
        return [points[0], slopes[0]] + [slopes[k] - slopes[k - 1] for k in range(1, knots - 1)]

    chosen = [scal_ref[2 + p] for p in range(passes)]
    vectors = [[lights_ref[chosen[p], axis] for axis in range(3)] for p in range(passes)]
    curves = [bends(chosen[p], 3, scale) for p in range(passes)]

    def row_tile(i, carry):
        base = i * SUB
        lateral = jnp.zeros((SUB, cols), jnp.float32)
        for part in range(parts):
            got = bricks_ref[part, pl.ds(cells * tall + base, SUB), :]
            moved = pltpu.roll(got, (2 * cells * (part - me + parts)) % cols, 1)
            lateral = jnp.where(lane // (2 * cells) == part, moved, lateral)

        def load(z, shift):
            return bricks_ref[z // cells, pl.ds(z % cells * tall + base + shift, SUB), :]

        def prepare(g, carry):
            low = g * unroll
            line = [jnp.where(low > 0, load(jnp.maximum(low - 1, 0), 1), 0.0)]
            line += [load(low + u, 1) for u in range(unroll)]
            line += [jnp.where(low + unroll < depth, load(jnp.minimum(low + unroll, depth - 1), 1), 0.0)]
            for u in range(unroll):
                z = low + u
                here = line[u + 1]
                edge = pltpu.roll(lateral, (cols - 1 - 2 * z) % cols, 1)
                grad_x = pltpu.roll(jnp.where(is_first, edge, here), cols - 1, 1) - pltpu.roll(
                    jnp.where(is_last, edge, here), 1, 1
                )
                grad_y = load(z, 2) - load(z, 0)
                grad_z = line[u + 2] - line[u]
                inverse = lax.rsqrt(grad_x * grad_x + grad_y * grad_y + grad_z * grad_z + 4.0)
                half = 0.5 * (knots - 1)
                position = half + half * jnp.tanh(0.5 * here)
                cell_ref[0, z] = grad_x * inverse
                cell_ref[1, z] = grad_y * inverse
                cell_ref[2, z] = grad_z * inverse
                cell_ref[3, z] = position
                for k in range(1, knots - 1):
                    cell_ref[3 + k, z] = jnp.maximum(position - k, 0.0)
            return carry

        lax.fori_loop(0, depth // unroll, prepare, 0)
        at = pl.ds(pl.multiple_of(base, SUB), SUB)
        zero = jnp.zeros((SUB, cols), jnp.float32)
        for p in range(passes):
            vector = [jnp.full((SUB, cols), v) for v in vectors[p]]
            curve = [jnp.full((SUB, cols), v) for v in curves[p]]

            def march(g, state):
                keep, sums = state
                for u in range(unroll):
                    z = first + step * (g * unroll + u)
                    hinges = [cell_ref[3 + k, z] for k in range(knots - 1)]
                    terms = [curve[0]] + [curve[k + 1] * hinges[k] for k in range(knots - 1)]
                    while len(terms) > 1:
                        terms = [sum(terms[j : j + 2][1:], terms[j]) for j in range(0, len(terms), 2)]
                    opacity = terms[0]
                    facing = cell_ref[0, z] * vector[0] + cell_ref[1, z] * vector[1] + cell_ref[2, z] * vector[2]
                    taken = keep * opacity
                    weight = taken * (AMBIENT + jnp.abs(facing))
                    keep = keep - taken
                    sums = [sums[0] + weight] + [sums[k + 1] + weight * hinges[k] for k in range(knots - 1)]
                return keep, sums

            keep, sums = lax.fori_loop(0, depth // unroll, march, (jnp.ones((SUB, cols), jnp.float32), [zero] * knots))
            for channel in range(3):
                tint = bends(chosen[p], channel, 1.0)
                color = tint[0] * sums[0]
                for k in range(1, knots):
                    color = color + tint[k] * sums[k]
                out_ref[p, channel, at, :] = color
            out_ref[p, 3, at, :] = 1.0 - keep
        return carry

    lax.fori_loop(0, rows // SUB, row_tile, 0)


def shift_along(block, axis, amount):
    count = lax.axis_size(axis)
    route = [(i, i + amount) for i in range(count) if 0 <= i + amount < count]
    return lax.ppermute(block, axis, route)


def on_device(field, light_vectors, transfer, light_index, flips):
    parts = lax.axis_size("depth")
    cells, all_rows, cols = field.shape
    rows = all_rows // parts
    passes = light_index.shape[0]
    lights, channels, knots = transfer.shape
    message = cells * (rows + 2) + rows

    edges = pl.pallas_call(
        functools.partial(edge_kernel, parts),
        out_shape=jax.ShapeDtypeStruct((rows, cols), jnp.float32),
        in_specs=[pl.BlockSpec(memory_space=VMEM)],
        out_specs=pl.BlockSpec(memory_space=VMEM),
        name="edges",
    )(field)
    left = shift_along(edges, "tile", 1)
    right = shift_along(edges, "tile", -1)
    packed = pl.pallas_call(
        functools.partial(pack_kernel, parts),
        out_shape=jax.ShapeDtypeStruct((parts, message, cols), jnp.float32),
        in_specs=[pl.BlockSpec(memory_space=VMEM)] * 3,
        out_specs=pl.BlockSpec(memory_space=VMEM),
        name="pack",
    )(field, left, right)
    bricks = lax.all_to_all(packed, "depth", 0, 0, tiled=True)
    scal = jnp.concatenate([lax.axis_index("depth").astype(jnp.int32)[None], flips, light_index])
    return pl.pallas_call(
        functools.partial(shade_kernel, parts, cells, passes, knots, 8),
        out_shape=jax.ShapeDtypeStruct((passes, channels, rows, cols), jnp.float32),
        in_specs=[pl.BlockSpec(memory_space=SMEM)] * 3 + [pl.BlockSpec(memory_space=VMEM)],
        out_specs=pl.BlockSpec(memory_space=VMEM),
        scratch_shapes=[VMEM((knots + 2, parts * cells, SUB, cols), jnp.float32)],
        name="shade",
    )(scal, light_vectors, transfer.reshape(lights, channels * knots), bricks)


def solution(mesh):
    in_specs = (P("depth", None, "tile"), P(), P(), P(), P("tile"))
    out_specs = P(None, None, "depth", "tile")
    return jax.shard_map(
        on_device, mesh=mesh, in_specs=in_specs, out_specs=out_specs, check_vma=False
    )
```

```python
import functools

import jax
import jax.numpy as jnp
from jax import lax
from jax.experimental import pallas as pl
from jax.experimental.pallas import tpu as pltpu
from jax.sharding import PartitionSpec as P

AMBIENT = 0.3
OPACITY = 2.0
SUB = 8
VMEM = pltpu.VMEM
SMEM = pltpu.SMEM


def edge_kernel(parts, field_ref, out_ref):
    cells, _, cols = field_ref.shape
    rows = out_ref.shape[0]
    lane_pair = lax.broadcasted_iota(jnp.int32, (SUB, cols), 1) // 2

    def tile(i, carry):
        acc = jnp.zeros((SUB, cols), jnp.float32)
        for part in range(parts):
            for z in range(cells):
                slot = part * cells + z
                start = pl.multiple_of(part * rows + i * SUB, SUB)
                value = field_ref[z, pl.ds(start, SUB), :]
                moved = pltpu.roll(value, (2 * slot + 1) % cols, 1)
                acc = jnp.where(lane_pair == slot, moved, acc)
        out_ref[pl.ds(pl.multiple_of(i * SUB, SUB), SUB), :] = acc
        return carry

    lax.fori_loop(0, rows // SUB, tile, 0)


def pack_kernel(parts, scal_ref, field_ref, *refs):
    outs, (extra_ref, sems) = refs[:parts], refs[parts:]
    cells, all_rows, cols = field_ref.shape
    rows = all_rows // parts
    me = scal_ref[0]
    copies = []
    for m in range(parts):
        low = pl.multiple_of((me ^ m) * rows, SUB)
        centre = outs[m].at[pl.ds(2 * cells, cells * rows), :].reshape(cells, rows, cols)
        copies.append(pltpu.make_async_copy(field_ref.at[:, pl.ds(low, rows), :], centre, sems.at[0, m]))
        copies[-1].start()
    for m in range(parts):
        part = me ^ m
        low = part * rows
        above = jnp.where(part > 0, 1.0, 0.0)
        below = jnp.where(part < parts - 1, 1.0, 0.0)
        for z in range(cells):
            extra_ref[m, z : z + 1, :] = field_ref[z, pl.ds(jnp.maximum(low - 1, 0), 1), :] * above
            extra_ref[m, cells + z : cells + z + 1, :] = (
                field_ref[z, pl.ds(jnp.minimum(low + rows, all_rows - 1), 1), :] * below
            )
        copies.append(pltpu.make_async_copy(extra_ref.at[m], outs[m].at[pl.ds(0, 2 * cells), :], sems.at[1, m]))
        copies[-1].start()
    for copy in copies:
        copy.wait()


def shade_kernel(parts, cells, passes, knots, unroll, scal_ref, lights_ref, curves_ref, lateral_ref, *refs):
    bricks, (out_ref, cell_ref, ends_ref) = refs[:parts], refs[parts:]
    cols = bricks[0].shape[1]
    rows = out_ref.shape[2]
    depth = parts * cells
    me = scal_ref[0]
    flip = scal_ref[1]
    step = 1 - 2 * flip
    first = flip * (depth - 1)
    scale = OPACITY / depth
    lane = lax.broadcasted_iota(jnp.int32, (SUB, cols), 1)
    sublane = lax.broadcasted_iota(jnp.int32, (SUB, cols), 0)
    is_first = lane == 0
    is_last = lane == cols - 1

    def bends(index, channel, factor):
        points = [curves_ref[index, channel * knots + k] * factor for k in range(knots)]
        slopes = [points[k + 1] - points[k] for k in range(knots - 1)]
        return [points[0], slopes[0]] + [slopes[k] - slopes[k - 1] for k in range(1, knots - 1)]

    chosen = [scal_ref[2 + p] for p in range(passes)]
    vectors = [[lights_ref[chosen[p], axis] for axis in range(3)] for p in range(passes)]
    curves = [bends(chosen[p], 3, scale) for p in range(passes)]

    ends_ref[0, 1] = jnp.zeros((rows, cols), jnp.float32)
    ends_ref[parts + 1, 0] = jnp.zeros((rows, cols), jnp.float32)
    for m in range(parts):
        ends_ref[(me ^ m) + 1, 0] = bricks[m][2 * cells : 2 * cells + rows, :]
        ends_ref[(me ^ m) + 1, 1] = bricks[m][(cells - 1) * rows + 2 * cells : cells * rows + 2 * cells, :]

    def row_tile(i, carry):
        base = pl.multiple_of(i * SUB, SUB)
        at = pl.ds(base, SUB)
        is_top = jnp.logical_and(sublane == 0, i == 0)
        is_bottom = jnp.logical_and(sublane == SUB - 1, i == rows // SUB - 1)
        for m in range(parts):
            part = me ^ m
            brick = bricks[m]
            sides = pltpu.roll(lateral_ref[part, at, :], (cols - 1 - 2 * cells * me) % cols, 1)
            line = [ends_ref[part, 1, at, :]]
            line += [brick[pl.ds(2 * cells + z * rows + base, SUB), :] for z in range(cells)]
            line += [ends_ref[part + 2, 0, at, :]]
            for z in range(cells):
                here = line[z + 1]
                start = 2 * cells + z * rows + base
                upper = jnp.where(is_top, brick[z : z + 1, :], brick[pl.ds(start - 1, SUB), :])
                lower = jnp.where(is_bottom, brick[cells + z : cells + z + 1, :], brick[pl.ds(start + 1, SUB), :])
                edge = pltpu.roll(sides, (cols - 2 * z) % cols, 1) if z else sides
                grad_x = pltpu.roll(jnp.where(is_first, edge, here), cols - 1, 1) - pltpu.roll(
                    jnp.where(is_last, edge, here), 1, 1
                )
                grad_y = lower - upper
                grad_z = line[z + 2] - line[z]
                inverse = lax.rsqrt(grad_x * grad_x + grad_y * grad_y + grad_z * grad_z + 4.0)
                half = 0.5 * (knots - 1)
                position = half + half * jnp.tanh(0.5 * here)
                spot = part * cells + z
                cell_ref[0, spot] = grad_x * inverse
                cell_ref[1, spot] = grad_y * inverse
                cell_ref[2, spot] = grad_z * inverse
                cell_ref[3, spot] = position
                for k in range(1, knots - 1):
                    cell_ref[3 + k, spot] = jnp.maximum(position - k, 0.0)

        zero = jnp.zeros((SUB, cols), jnp.float32)
        for p in range(passes):
            vector = [jnp.full((SUB, cols), v) for v in vectors[p]]
            curve = [jnp.full((SUB, cols), v) for v in curves[p]]

            def march(g, state):
                keep, sums = state
                for u in range(unroll):
                    z = first + step * (g * unroll + u)
                    hinges = [cell_ref[3 + k, z] for k in range(knots - 1)]
                    terms = [curve[0]] + [curve[k + 1] * hinges[k] for k in range(knots - 1)]
                    while len(terms) > 1:
                        terms = [sum(terms[j : j + 2][1:], terms[j]) for j in range(0, len(terms), 2)]
                    opacity = terms[0]
                    facing = cell_ref[0, z] * vector[0] + cell_ref[1, z] * vector[1] + cell_ref[2, z] * vector[2]
                    taken = keep * opacity
                    weight = taken * (AMBIENT + jnp.abs(facing))
                    keep = keep - taken
                    sums = [sums[0] + weight] + [sums[k + 1] + weight * hinges[k] for k in range(knots - 1)]
                return keep, sums

            keep, sums = lax.fori_loop(0, depth // unroll, march, (jnp.ones((SUB, cols), jnp.float32), [zero] * knots))
            for channel in range(3):
                tint = bends(chosen[p], channel, 1.0)
                color = tint[0] * sums[0]
                for k in range(1, knots):
                    color = color + tint[k] * sums[k]
                out_ref[p, channel, at, :] = color
            out_ref[p, 3, at, :] = 1.0 - keep
        return carry

    lax.fori_loop(0, rows // SUB, row_tile, 0)


def swap_along(block, axis, mask):
    return lax.ppermute(block, axis, [(i, i ^ mask) for i in range(lax.axis_size(axis))])


def on_device(field, light_vectors, transfer, light_index, flips):
    parts = lax.axis_size("depth")
    cells, all_rows, cols = field.shape
    rows = all_rows // parts
    passes = light_index.shape[0]
    lights, channels, knots = transfer.shape
    message = cells * rows + 2 * cells + SUB
    scal = jnp.concatenate([lax.axis_index("depth").astype(jnp.int32)[None], flips, light_index])

    packed = pl.pallas_call(
        functools.partial(pack_kernel, parts),
        out_shape=[jax.ShapeDtypeStruct((message, cols), jnp.float32)] * parts,
        in_specs=[pl.BlockSpec(memory_space=SMEM), pl.BlockSpec(memory_space=VMEM)],
        out_specs=[pl.BlockSpec(memory_space=pl.ANY)] * parts,
        scratch_shapes=[VMEM((parts, 2 * cells, cols), jnp.float32), pltpu.SemaphoreType.DMA((2, parts))],
        name="pack",
    )(scal, field)
    bricks = [packed[0]] + [swap_along(packed[m], "depth", m) for m in range(1, parts)]

    edges = pl.pallas_call(
        functools.partial(edge_kernel, parts),
        out_shape=jax.ShapeDtypeStruct((rows, cols), jnp.float32),
        in_specs=[pl.BlockSpec(memory_space=VMEM)],
        out_specs=pl.BlockSpec(memory_space=VMEM),
        name="edges",
    )(field)
    around = lax.all_gather(edges, "tile")
    tile, tiles = lax.axis_index("tile"), lax.axis_size("tile")
    left = jnp.where(tile > 0, lax.dynamic_index_in_dim(around, jnp.maximum(tile - 1, 0), 0, False), 0.0)
    right = jnp.where(tile < tiles - 1, lax.dynamic_index_in_dim(around, jnp.minimum(tile + 1, tiles - 1), 0, False), 0.0)
    sides = jnp.where(jnp.arange(cols) % 2 == 0, left, right)
    lateral = lax.all_gather(sides, "depth")
    return pl.pallas_call(
        functools.partial(shade_kernel, parts, cells, passes, knots, 32),
        out_shape=jax.ShapeDtypeStruct((passes, channels, rows, cols), jnp.float32),
        in_specs=[pl.BlockSpec(memory_space=SMEM)] * 3 + [pl.BlockSpec(memory_space=VMEM)] * (1 + parts),
        out_specs=pl.BlockSpec(memory_space=VMEM),
        scratch_shapes=[
            VMEM((knots + 2, parts * cells, SUB, cols), jnp.float32),
            VMEM((parts + 2, 2, rows, cols), jnp.float32),
        ],
        name="shade",
    )(scal, light_vectors, transfer.reshape(lights, channels * knots), lateral, *bricks)


def solution(mesh):
    in_specs = (P("depth", None, "tile"), P(), P(), P(), P("tile"))
    out_specs = P(None, None, "depth", "tile")
    return jax.shard_map(
        on_device, mesh=mesh, in_specs=in_specs, out_specs=out_specs, check_vma=False
    )
```

```python
import functools

import jax
import jax.numpy as jnp
from jax import lax
from jax.experimental import pallas as pl
from jax.experimental.pallas import tpu as pltpu
from jax.sharding import PartitionSpec as P

AMBIENT = 0.3
OPACITY = 2.0
SUB = 8
VMEM = pltpu.VMEM
SMEM = pltpu.SMEM


def edge_kernel(parts, field_ref, out_ref):
    cells, _, cols = field_ref.shape
    rows = out_ref.shape[0]
    lane_pair = lax.broadcasted_iota(jnp.int32, (SUB, cols), 1) // 2

    def tile(i, carry):
        acc = jnp.zeros((SUB, cols), jnp.float32)
        for part in range(parts):
            for z in range(cells):
                slot = part * cells + z
                start = pl.multiple_of(part * rows + i * SUB, SUB)
                value = field_ref[z, pl.ds(start, SUB), :]
                moved = pltpu.roll(value, (2 * slot + 1) % cols, 1)
                acc = jnp.where(lane_pair == slot, moved, acc)
        out_ref[pl.ds(pl.multiple_of(i * SUB, SUB), SUB), :] = acc
        return carry

    lax.fori_loop(0, rows // SUB, tile, 0)


def pack_kernel(parts, field_ref, *refs):
    outs, (near_ref, extra_ref, sems) = refs[:parts], refs[parts:]
    cells, all_rows, cols = field_ref.shape
    rows = all_rows // parts
    me = lax.axis_index("depth")
    copies, nears = [], []
    for m in range(parts):
        low = pl.multiple_of((me ^ m) * rows, SUB)
        centre = outs[m].at[pl.ds(2 * cells, cells * rows), :].reshape(cells, rows, cols)
        before = pl.multiple_of(jnp.maximum(low - SUB, 0), SUB)
        after = pl.multiple_of(jnp.minimum(low + rows, all_rows - SUB), SUB)
        for side, start in enumerate((before, after)):
            nears.append(
                pltpu.make_async_copy(field_ref.at[:, pl.ds(start, SUB), :], near_ref.at[m, side], sems.at[1 + side, m])
            )
            nears[-1].start()
        copies.append(pltpu.make_async_copy(field_ref.at[:, pl.ds(low, rows), :], centre, sems.at[0, m]))
        copies[-1].start()
    for m in range(parts):
        part = me ^ m
        above = jnp.where(part > 0, 1.0, 0.0)
        below = jnp.where(part < parts - 1, 1.0, 0.0)
        nears[2 * m].wait()
        nears[2 * m + 1].wait()
        for z in range(cells):
            extra_ref[m, z : z + 1, :] = near_ref[m, 0, z, SUB - 1 : SUB, :] * above
            extra_ref[m, cells + z : cells + z + 1, :] = near_ref[m, 1, z, 0:1, :] * below
        copies.append(pltpu.make_async_copy(extra_ref.at[m], outs[m].at[pl.ds(0, 2 * cells), :], sems.at[3, m]))
        copies[-1].start()
    for copy in copies:
        copy.wait()


def shade_kernel(parts, cells, passes, knots, unroll, index_ref, flip_ref, lights_ref, curves_ref, *refs):
    bricks, laterals, (out_ref, cell_ref, ends_ref) = refs[:parts], refs[parts : 2 * parts], refs[2 * parts :]
    cols = bricks[0].shape[1]
    rows = out_ref.shape[2]
    depth = parts * cells
    me = lax.axis_index("depth")
    flip = flip_ref[0]
    step = 1 - 2 * flip
    first = flip * (depth - 1)
    scale = OPACITY / depth
    lane = lax.broadcasted_iota(jnp.int32, (SUB, cols), 1)
    sublane = lax.broadcasted_iota(jnp.int32, (SUB, cols), 0)
    is_first = lane == 0
    is_last = lane == cols - 1

    def bends(index, channel):
        points = [curves_ref[index, channel, k] for k in range(knots)]
        slopes = [points[k + 1] - points[k] for k in range(knots - 1)]
        return [points[0], slopes[0]] + [slopes[k] - slopes[k - 1] for k in range(1, knots - 1)]

    def segments(index, channel, factor):
        points = [curves_ref[index, channel, k] * factor for k in range(knots)]
        offset = jnp.zeros((SUB, cols), jnp.float32)
        slope = jnp.zeros((SUB, cols), jnp.float32)
        for k in range(knots - 1):
            rise = points[k + 1] - points[k]
            slope = jnp.where(lane == k, rise, slope)
            offset = jnp.where(lane == k, points[k] - k * rise, offset)
        return offset, slope

    chosen = [index_ref[p] for p in range(passes)]
    vectors = [[lights_ref[chosen[p], axis] for axis in range(3)] for p in range(passes)]
    tables = [segments(chosen[p], 3, scale) for p in range(passes)]

    ends_ref[0, 1] = jnp.zeros((rows, cols), jnp.float32)
    ends_ref[parts + 1, 0] = jnp.zeros((rows, cols), jnp.float32)
    for m in range(parts):
        ends_ref[(me ^ m) + 1, 0] = bricks[m][2 * cells : 2 * cells + rows, :]
        ends_ref[(me ^ m) + 1, 1] = bricks[m][(cells - 1) * rows + 2 * cells : cells * rows + 2 * cells, :]

    def row_tile(i, carry):
        base = pl.multiple_of(i * SUB, SUB)
        at = pl.ds(base, SUB)
        is_top = jnp.logical_and(sublane == 0, i == 0)
        is_bottom = jnp.logical_and(sublane == SUB - 1, i == rows // SUB - 1)
        for m in range(parts):
            part = me ^ m
            brick = bricks[m]
            sides = pltpu.roll(laterals[m][at, :], (cols - 1 - 2 * cells * me) % cols, 1)
            line = [ends_ref[part, 1, at, :]]
            line += [brick[pl.ds(2 * cells + z * rows + base, SUB), :] for z in range(cells)]
            line += [ends_ref[part + 2, 0, at, :]]
            for z in range(cells):
                here = line[z + 1]
                start = 2 * cells + z * rows + base
                upper = jnp.where(is_top, brick[z : z + 1, :], brick[pl.ds(start - 1, SUB), :])
                lower = jnp.where(is_bottom, brick[cells + z : cells + z + 1, :], brick[pl.ds(start + 1, SUB), :])
                edge = pltpu.roll(sides, (cols - 2 * z) % cols, 1) if z else sides
                grad_x = pltpu.roll(jnp.where(is_first, edge, here), cols - 1, 1) - pltpu.roll(
                    jnp.where(is_last, edge, here), 1, 1
                )
                grad_y = lower - upper
                grad_z = line[z + 2] - line[z]
                inverse = lax.rsqrt(grad_x * grad_x + grad_y * grad_y + grad_z * grad_z + 4.0)
                half = 0.5 * (knots - 1)
                position = half + half * jnp.tanh(0.5 * here)
                spot = part * cells + z
                cell_ref[0, spot] = grad_x * inverse
                cell_ref[1, spot] = grad_y * inverse
                cell_ref[2, spot] = grad_z * inverse
                cell_ref[3, spot] = position
                for k in range(1, knots - 1):
                    cell_ref[3 + k, spot] = jnp.maximum(position - k, 0.0)
                segment = jnp.minimum(position.astype(jnp.int32), knots - 2)
                for p, (offset, slope) in enumerate(tables):
                    found = jnp.take_along_axis(offset, segment, axis=1, mode="promise_in_bounds")
                    rise = jnp.take_along_axis(slope, segment, axis=1, mode="promise_in_bounds")
                    cell_ref[knots + 2 + p, spot] = found + rise * position

        zero = jnp.zeros((SUB, cols), jnp.float32)
        for low in range(0, passes, 2):
            group = range(low, min(low + 2, passes))
            vector = {p: [jnp.full((SUB, cols), v) for v in vectors[p]] for p in group}

            def march(g, state):
                for u in range(unroll):
                    z = first + step * (g * unroll + u)
                    hinges = [cell_ref[3 + k, z] for k in range(knots - 1)]
                    normal = [cell_ref[axis, z] for axis in range(3)]
                    following = []
                    for p, (keep, sums) in zip(group, state):
                        facing = normal[0] * vector[p][0] + normal[1] * vector[p][1] + normal[2] * vector[p][2]
                        taken = keep * cell_ref[knots + 2 + p, z]
                        weight = taken * (AMBIENT + jnp.abs(facing))
                        sums = [sums[0] + weight] + [sums[k + 1] + weight * hinges[k] for k in range(knots - 1)]
                        following.append((keep - taken, sums))
                    state = following
                return state

            initial = [(jnp.ones((SUB, cols), jnp.float32), [zero] * knots) for p in group]
            state = lax.fori_loop(0, depth // unroll, march, initial)
            for p, (keep, sums) in zip(group, state):
                for channel in range(3):
                    tint = bends(chosen[p], channel)
                    color = tint[0] * sums[0]
                    for k in range(1, knots):
                        color = color + tint[k] * sums[k]
                    out_ref[p, channel, at, :] = color
                out_ref[p, 3, at, :] = 1.0 - keep
        return carry

    lax.fori_loop(0, rows // SUB, row_tile, 0)


def shift_along(block, axis, amount):
    count = lax.axis_size(axis)
    route = [(i, i + amount) for i in range(count) if 0 <= i + amount < count]
    return lax.ppermute(block, axis, route)


def swap_along(block, axis, mask):
    return lax.ppermute(block, axis, [(i, i ^ mask) for i in range(lax.axis_size(axis))])


def on_device(field, light_vectors, transfer, light_index, flips):
    parts = lax.axis_size("depth")
    cells, all_rows, cols = field.shape
    rows = all_rows // parts
    passes = light_index.shape[0]
    lights, channels, knots = transfer.shape
    message = cells * rows + 2 * cells + SUB
    packed = pl.pallas_call(
        functools.partial(pack_kernel, parts),
        out_shape=[jax.ShapeDtypeStruct((message, cols), jnp.float32)] * parts,
        in_specs=[pl.BlockSpec(memory_space=pl.ANY)],
        out_specs=[pl.BlockSpec(memory_space=pl.ANY)] * parts,
        scratch_shapes=[
            VMEM((parts, 2, cells, SUB, cols), jnp.float32),
            VMEM((parts, 2 * cells, cols), jnp.float32),
            pltpu.SemaphoreType.DMA((4, parts)),
        ],
        name="pack",
    )(field)
    bricks = [packed[0]] + [swap_along(packed[m], "depth", m) for m in range(1, parts)]

    edges = pl.pallas_call(
        functools.partial(edge_kernel, parts),
        out_shape=jax.ShapeDtypeStruct((rows, cols), jnp.float32),
        in_specs=[pl.BlockSpec(memory_space=VMEM)],
        out_specs=pl.BlockSpec(memory_space=VMEM),
        name="edges",
    )(field)
    left = shift_along(edges, "tile", 1)
    right = shift_along(edges, "tile", -1)
    sides = jnp.where(jnp.arange(cols) % 2 == 0, left, right)
    laterals = [sides] + [swap_along(sides, "depth", m) for m in range(1, parts)]
    return pl.pallas_call(
        functools.partial(shade_kernel, parts, cells, passes, knots, 32),
        out_shape=jax.ShapeDtypeStruct((passes, channels, rows, cols), jnp.float32),
        in_specs=[pl.BlockSpec(memory_space=SMEM)] * 4 + [pl.BlockSpec(memory_space=VMEM)] * (2 * parts),
        out_specs=pl.BlockSpec(memory_space=VMEM),
        scratch_shapes=[
            VMEM((knots + 2 + passes, parts * cells, SUB, cols), jnp.float32),
            VMEM((parts + 2, 2, rows, cols), jnp.float32),
        ],
        name="shade",
    )(light_index, flips, light_vectors, transfer, *bricks, *laterals)


def solution(mesh):
    in_specs = (P("depth", None, "tile"), P(), P(), P(), P("tile"))
    out_specs = P(None, None, "depth", "tile")
    return jax.shard_map(
        on_device, mesh=mesh, in_specs=in_specs, out_specs=out_specs, check_vma=False
    )
```

```python
import functools

import jax
import jax.numpy as jnp
from jax import lax
from jax.experimental import pallas as pl
from jax.experimental.pallas import tpu as pltpu
from jax.sharding import PartitionSpec as P

AMBIENT = 0.3
OPACITY = 2.0
SUB = 8
VMEM = pltpu.VMEM
SMEM = pltpu.SMEM


def edge_kernel(parts, field_ref, _, out_ref):
    cells, _, cols = field_ref.shape
    rows = out_ref.shape[0]
    lane_pair = lax.broadcasted_iota(jnp.int32, (SUB, cols), 1) // 2

    def tile(i, carry):
        acc = jnp.zeros((SUB, cols), jnp.float32)
        for part in range(parts):
            for z in range(cells):
                slot = part * cells + z
                start = pl.multiple_of(part * rows + i * SUB, SUB)
                value = field_ref[z, pl.ds(start, SUB), :]
                moved = pltpu.roll(value, (2 * slot + 1) % cols, 1)
                acc = jnp.where(lane_pair == slot, moved, acc)
        out_ref[pl.ds(pl.multiple_of(i * SUB, SUB), SUB), :] = acc
        return carry

    lax.fori_loop(0, rows // SUB, tile, 0)


def pack_kernel(parts, field_ref, *refs):
    outs, (extra_ref, sems) = refs[:parts], refs[parts:]
    cells, all_rows, cols = field_ref.shape
    rows = all_rows // parts
    me = lax.axis_index("depth")
    copies = []
    for m in range(parts):
        low = pl.multiple_of((me ^ m) * rows, SUB)
        centre = outs[m].at[pl.ds(2 * cells, cells * rows), :].reshape(cells, rows, cols)
        copies.append(pltpu.make_async_copy(field_ref.at[:, pl.ds(low, rows), :], centre, sems.at[0, m]))
        copies[-1].start()
    for m in range(parts):
        part = me ^ m
        low = part * rows
        above = jnp.where(part > 0, 1.0, 0.0)
        below = jnp.where(part < parts - 1, 1.0, 0.0)
        for z in range(cells):
            extra_ref[m, z : z + 1, :] = field_ref[z, pl.ds(jnp.maximum(low - 1, 0), 1), :] * above
            extra_ref[m, cells + z : cells + z + 1, :] = (
                field_ref[z, pl.ds(jnp.minimum(low + rows, all_rows - 1), 1), :] * below
            )
        copies.append(pltpu.make_async_copy(extra_ref.at[m], outs[m].at[pl.ds(0, 2 * cells), :], sems.at[1, m]))
        copies[-1].start()
    for copy in copies:
        copy.wait()


def shade_kernel(parts, cells, passes, knots, unroll, index_ref, flip_ref, lights_ref, curves_ref, *refs):
    bricks, laterals, (out_ref, cell_ref, ends_ref) = refs[:parts], refs[parts : 2 * parts - 1], refs[2 * parts - 1 :]
    cols = bricks[0].shape[1]
    rows = out_ref.shape[2]
    depth = parts * cells
    me = lax.axis_index("depth")
    flip = flip_ref[0]
    step = 1 - 2 * flip
    first = flip * (depth - 1)
    scale = OPACITY / depth
    lane = lax.broadcasted_iota(jnp.int32, (SUB, cols), 1)
    sublane = lax.broadcasted_iota(jnp.int32, (SUB, cols), 0)
    is_first = lane == 0
    is_last = lane == cols - 1

    def bends(index, channel):
        points = [curves_ref[index, channel, k] for k in range(knots)]
        slopes = [points[k + 1] - points[k] for k in range(knots - 1)]
        return [points[0], slopes[0]] + [slopes[k] - slopes[k - 1] for k in range(1, knots - 1)]

    chosen = [index_ref[p] for p in range(passes)]
    vectors = [[lights_ref[chosen[p], axis] for axis in range(3)] for p in range(passes)]
    curves = [[value * scale for value in bends(chosen[p], 3)] for p in range(passes)]

    ends_ref[0, 1] = jnp.zeros((rows, cols), jnp.float32)
    ends_ref[parts + 1, 0] = jnp.zeros((rows, cols), jnp.float32)
    for m in range(parts):
        ends_ref[(me ^ m) + 1, 0] = bricks[m][2 * cells : 2 * cells + rows, :]
        ends_ref[(me ^ m) + 1, 1] = bricks[m][(cells - 1) * rows + 2 * cells : cells * rows + 2 * cells, :]

    def row_tile(i, carry):
        base = pl.multiple_of(i * SUB, SUB)
        at = pl.ds(base, SUB)
        is_top = jnp.logical_and(sublane == 0, i == 0)
        is_bottom = jnp.logical_and(sublane == SUB - 1, i == rows // SUB - 1)
        for m in range(parts):
            part = me ^ m
            brick = bricks[m]
            got = laterals[m][at, :] if m < parts - 1 else brick[pl.ds((2 + rows) * cells + base, SUB), :]
            sides = pltpu.roll(got, (cols - 1 - 2 * cells * me) % cols, 1)
            line = [ends_ref[part, 1, at, :]]
            line += [brick[pl.ds(2 * cells + z * rows + base, SUB), :] for z in range(cells)]
            line += [ends_ref[part + 2, 0, at, :]]
            for z in range(cells):
                here = line[z + 1]
                start = 2 * cells + z * rows + base
                upper = jnp.where(is_top, brick[z : z + 1, :], brick[pl.ds(start - 1, SUB), :])
                lower = jnp.where(is_bottom, brick[cells + z : cells + z + 1, :], brick[pl.ds(start + 1, SUB), :])
                edge = pltpu.roll(sides, (cols - 2 * z) % cols, 1) if z else sides
                grad_x = pltpu.roll(jnp.where(is_first, edge, here), cols - 1, 1) - pltpu.roll(
                    jnp.where(is_last, edge, here), 1, 1
                )
                grad_y = lower - upper
                grad_z = line[z + 2] - line[z]
                inverse = lax.rsqrt(grad_x * grad_x + grad_y * grad_y + grad_z * grad_z + 4.0)
                half = 0.5 * (knots - 1)
                position = half + half * jnp.tanh(0.5 * here)
                spot = part * cells + z
                cell_ref[0, spot] = grad_x * inverse
                cell_ref[1, spot] = grad_y * inverse
                cell_ref[2, spot] = grad_z * inverse
                cell_ref[3, spot] = position
                for k in range(1, knots - 1):
                    cell_ref[3 + k, spot] = jnp.maximum(position - k, 0.0)

        zero = jnp.zeros((SUB, cols), jnp.float32)
        for low in range(0, passes, 2):
            group = range(low, min(low + 2, passes))
            vector = {p: [jnp.full((SUB, cols), v) for v in vectors[p]] for p in group}
            curve = {p: [jnp.full((SUB, cols), v) for v in curves[p]] for p in group}

            def march(g, state):
                for u in range(unroll):
                    z = first + step * (g * unroll + u)
                    hinges = [cell_ref[3 + k, z] for k in range(knots - 1)]
                    normal = [cell_ref[axis, z] for axis in range(3)]
                    following = []
                    for p, (keep, sums) in zip(group, state):
                        facing = normal[0] * vector[p][0] + normal[1] * vector[p][1] + normal[2] * vector[p][2]
                        terms = [curve[p][0]] + [curve[p][k + 1] * hinges[k] for k in range(knots - 1)]
                        while len(terms) > 1:
                            terms = [sum(terms[j : j + 2][1:], terms[j]) for j in range(0, len(terms), 2)]
                        taken = keep * terms[0]
                        weight = taken * (AMBIENT + jnp.abs(facing))
                        sums = [sums[0] + weight] + [sums[k + 1] + weight * hinges[k] for k in range(knots - 1)]
                        following.append((keep - taken, sums))
                    state = following
                return state

            initial = [(jnp.ones((SUB, cols), jnp.float32), [zero] * knots) for p in group]
            state = lax.fori_loop(0, depth // unroll, march, initial)
            for p, (keep, sums) in zip(group, state):
                for channel in range(3):
                    tint = bends(chosen[p], channel)
                    color = tint[0] * sums[0]
                    for k in range(1, knots):
                        color = color + tint[k] * sums[k]
                    out_ref[p, channel, at, :] = color
                out_ref[p, 3, at, :] = 1.0 - keep
        return carry

    lax.fori_loop(0, rows // SUB, row_tile, 0)


def shift_along(block, axis, amount):
    count = lax.axis_size(axis)
    route = [(i, i + amount) for i in range(count) if 0 <= i + amount < count]
    return lax.ppermute(block, axis, route)


def swap_along(block, axis, mask):
    return lax.ppermute(block, axis, [(i, i ^ mask) for i in range(lax.axis_size(axis))])


def on_device(field, light_vectors, transfer, light_index, flips):
    parts = lax.axis_size("depth")
    cells, all_rows, cols = field.shape
    rows = all_rows // parts
    passes = light_index.shape[0]
    lights, channels, knots = transfer.shape
    message = cells * rows + 2 * cells
    tails = [SUB] * (parts - 1) + [rows]

    packed = pl.pallas_call(
        functools.partial(pack_kernel, parts),
        out_shape=[jax.ShapeDtypeStruct((message + tail, cols), jnp.float32) for tail in tails],
        in_specs=[pl.BlockSpec(memory_space=VMEM)],
        out_specs=[pl.BlockSpec(memory_space=pl.ANY)] * parts,
        scratch_shapes=[VMEM((parts, 2 * cells, cols), jnp.float32), pltpu.SemaphoreType.DMA((2, parts))],
        name="pack",
    )(field)
    bricks = [packed[0]] + [swap_along(packed[m], "depth", m) for m in range(1, parts - 1)]

    edges = pl.pallas_call(
        functools.partial(edge_kernel, parts),
        out_shape=jax.ShapeDtypeStruct((rows, cols), jnp.float32),
        in_specs=[pl.BlockSpec(memory_space=VMEM), pl.BlockSpec(memory_space=pl.ANY)],
        out_specs=pl.BlockSpec(memory_space=VMEM),
        name="edges",
    )(field, packed[0])
    left = shift_along(edges, "tile", 1)
    right = shift_along(edges, "tile", -1)
    sides = jnp.where(jnp.arange(cols) % 2 == 0, left, right)
    laterals = [sides] + [swap_along(sides, "depth", m) for m in range(1, parts - 1)]
    far = lax.dynamic_update_slice(packed[-1], sides, (message, 0))
    bricks.append(swap_along(far, "depth", parts - 1))
    return pl.pallas_call(
        functools.partial(shade_kernel, parts, cells, passes, knots, parts * cells),
        out_shape=jax.ShapeDtypeStruct((passes, channels, rows, cols), jnp.float32),
        in_specs=[pl.BlockSpec(memory_space=SMEM)] * 4 + [pl.BlockSpec(memory_space=VMEM)] * (2 * parts - 1),
        out_specs=pl.BlockSpec(memory_space=VMEM),
        scratch_shapes=[
            VMEM((knots + 2, parts * cells, SUB, cols), jnp.float32),
            VMEM((parts + 2, 2, rows, cols), jnp.float32),
        ],
        name="shade",
    )(light_index, flips, light_vectors, transfer, *bricks, *laterals)


def solution(mesh):
    in_specs = (P("depth", None, "tile"), P(), P(), P(), P("tile"))
    out_specs = P(None, None, "depth", "tile")
    return jax.shard_map(
        on_device, mesh=mesh, in_specs=in_specs, out_specs=out_specs, check_vma=False
    )
```

```python
import functools

import jax
import jax.numpy as jnp
from jax import lax
from jax.experimental import pallas as pl
from jax.experimental.pallas import tpu as pltpu
from jax.sharding import PartitionSpec as P

AMBIENT = 0.3
OPACITY = 2.0
SUB = 8
VMEM = pltpu.VMEM
SMEM = pltpu.SMEM
MIB = 1 << 20


def edge_kernel(parts, field_ref, _, out_ref):
    cells, _, cols = field_ref.shape
    rows = out_ref.shape[0]
    lane_pair = lax.broadcasted_iota(jnp.int32, (SUB, cols), 1) // 2

    def tile(i, carry):
        acc = jnp.zeros((SUB, cols), jnp.float32)
        for part in range(parts):
            for z in range(cells):
                slot = part * cells + z
                start = pl.multiple_of(part * rows + i * SUB, SUB)
                value = field_ref[z, pl.ds(start, SUB), :]
                moved = pltpu.roll(value, (2 * slot + 1) % cols, 1)
                acc = jnp.where(lane_pair == slot, moved, acc)
        out_ref[pl.ds(pl.multiple_of(i * SUB, SUB), SUB), :] = acc
        return carry

    lax.fori_loop(0, rows // SUB, tile, 0)


def pack_kernel(parts, field_ref, *outs):
    cells, all_rows, cols = field_ref.shape
    rows = all_rows // parts
    me = lax.axis_index("depth")
    for m in range(parts):
        part = me ^ m
        low = pl.multiple_of(part * rows, SUB)
        above = jnp.where(part > 0, 1.0, 0.0)
        below = jnp.where(part < parts - 1, 1.0, 0.0)
        head = outs[m]
        for z in range(cells):
            head[z : z + 1, :] = field_ref[z, pl.ds(jnp.maximum(low - 1, 0), 1), :] * above
            head[cells + z : cells + z + 1, :] = field_ref[z, pl.ds(jnp.minimum(low + rows, all_rows - 1), 1), :] * below
        for z in range(cells):
            values = field_ref[z, pl.ds(low, rows), :]
            if m < parts - 1:
                head[2 * cells + z * rows : 2 * cells + (z + 1) * rows, :] = values
            elif z == 0:
                head[2 * cells : 2 * cells + rows, :] = values
            elif z == cells - 1:
                head[2 * cells + rows : 2 * cells + 2 * rows, :] = values
            else:
                outs[parts][z * rows : (z + 1) * rows, :] = values


def brick_views(parts, cells, rows, refs):
    views = []
    for m in range(parts - 1):
        head, lateral = refs[2 * m], refs[2 * m + 1]
        views.append((head, [(head, 2 * cells + z * rows) for z in range(cells)], lateral))
    return views


def far_view(cells, rows, head, body):
    places = [(head, 2 * cells)] + [(body, z * rows) for z in range(1, cells - 1)] + [(head, 2 * cells + rows)]
    return head, places, body


def fill_ends(parts, cells, rows, heads, ends_ref):
    me = lax.axis_index("depth")
    ends_ref[0, 1] = jnp.zeros_like(ends_ref[0, 1])
    ends_ref[parts + 1, 0] = jnp.zeros_like(ends_ref[0, 0])
    for m in range(parts):
        last = (cells - 1) * rows if m < parts - 1 else rows
        ends_ref[(me ^ m) + 1, 0] = heads[m][2 * cells : 2 * cells + rows, :]
        ends_ref[(me ^ m) + 1, 1] = heads[m][2 * cells + last : 2 * cells + last + rows, :]


def tables(light_refs, passes, parts, cells):
    index_ref, lights_ref, curves_ref = light_refs
    knots = curves_ref.shape[2]

    def bends(index, channel):
        points = [curves_ref[index, channel, k] for k in range(knots)]
        slopes = [points[k + 1] - points[k] for k in range(knots - 1)]
        return [points[0], slopes[0]] + [slopes[k] - slopes[k - 1] for k in range(1, knots - 1)]

    chosen = [index_ref[p] for p in range(passes)]
    vectors = [[lights_ref[index, axis] for axis in range(3)] for index in chosen]
    scale = OPACITY / (parts * cells)
    curves = [[value * scale for value in bends(index, 3)] for index in chosen]
    tints = [[bends(index, channel) for channel in range(3)] for index in chosen]
    return vectors, curves, tints


def prepare_steps(m, view, base, cells, rows, knots, cols, ends_ref, cell_ref):
    head, places, lateral = view
    me = lax.axis_index("depth")
    part = me ^ m
    at = pl.ds(base, SUB)
    lane = lax.broadcasted_iota(jnp.int32, (SUB, cols), 1)
    sublane = lax.broadcasted_iota(jnp.int32, (SUB, cols), 0)
    is_first = lane == 0
    is_last = lane == cols - 1
    is_top = jnp.logical_and(sublane == 0, base == 0)
    is_bottom = jnp.logical_and(sublane == SUB - 1, base == rows - SUB)
    sides = pltpu.roll(lateral[at, :], (cols - 1 - 2 * cells * me) % cols, 1)

    def layer(z):
        if z < 0:
            return ends_ref[part, 1, at, :]
        if z == cells:
            return ends_ref[part + 2, 0, at, :]
        ref, low = places[z]
        return ref[pl.ds(low + base, SUB), :]

    def step(z):
        ref, low = places[z]
        here = layer(z)
        upper = jnp.where(is_top, head[z : z + 1, :], ref[pl.ds(low + base - 1, SUB), :])
        lower = jnp.where(is_bottom, head[cells + z : cells + z + 1, :], ref[pl.ds(low + base + 1, SUB), :])
        edge = pltpu.roll(sides, (cols - 2 * z) % cols, 1) if z else sides
        grad_x = pltpu.roll(jnp.where(is_first, edge, here), cols - 1, 1) - pltpu.roll(
            jnp.where(is_last, edge, here), 1, 1
        )
        grad_y = lower - upper
        grad_z = layer(z + 1) - layer(z - 1)
        inverse = lax.rsqrt(grad_x * grad_x + grad_y * grad_y + grad_z * grad_z + 4.0)
        half = 0.5 * (knots - 1)
        position = half + half * jnp.tanh(0.5 * here)
        cell_ref[0, z] = grad_x * inverse
        cell_ref[1, z] = grad_y * inverse
        cell_ref[2, z] = grad_z * inverse
        cell_ref[3, z] = position
        for k in range(1, knots - 1):
            cell_ref[3 + k, z] = jnp.maximum(position - k, 0.0)

    return [functools.partial(step, z) for z in range(cells)]


def tree(terms):
    while len(terms) > 1:
        terms = [sum(terms[j + 1 : j + 2], terms[j]) for j in range(0, len(terms), 2)]
    return terms[0]


def march_unit(flip, vectors, curves, cells, knots, cols, cell_ref, beside):
    passes = len(vectors)
    shape = (SUB, cols)
    zero = jnp.zeros(shape, jnp.float32)
    result = []
    beside = list(beside)
    for low in range(0, passes, 2):
        group = range(low, min(low + 2, passes))
        vector = {p: [jnp.full(shape, v) for v in vectors[p]] for p in group}
        curve = {p: [jnp.full(shape, v) for v in curves[p]] for p in group}
        state = {p: (jnp.ones(shape, jnp.float32), [zero] * knots) for p in group}
        share = -(-len(beside) * 2 // max(passes - low, 1))
        mine, beside = beside[:share], beside[share:]
        for u in range(cells):
            for step in mine[u * share // cells : (u + 1) * share // cells]:
                step()
            z = u + flip * (cells - 1 - 2 * u)
            hinges = [cell_ref[3 + k, z] for k in range(knots - 1)]
            normal = [cell_ref[axis, z] for axis in range(3)]
            for p in group:
                keep, sums = state[p]
                opacity = tree([curve[p][0]] + [curve[p][k + 1] * hinges[k] for k in range(knots - 1)])
                facing = normal[0] * vector[p][0] + normal[1] * vector[p][1] + normal[2] * vector[p][2]
                taken = keep * opacity
                weight = taken * (AMBIENT + jnp.abs(facing))
                sums = [sums[0] + weight] + [sums[k + 1] + weight * hinges[k] for k in range(knots - 1)]
                state[p] = (keep - taken, sums)
        result += [[state[p][0]] + state[p][1] for p in group]
    return result


def near_kernel(parts, cells, index_ref, flip_ref, lights_ref, curves_ref, *refs):
    inputs, far_head, out_ref, ends_ref, cell_refs = refs[: 2 * parts - 2], refs[2 * parts - 2], refs[2 * parts - 1], refs[2 * parts], refs[2 * parts + 1 :]
    rows, cols = out_ref.shape[2:]
    knots = curves_ref.shape[2]
    passes = index_ref.shape[0]
    flip = flip_ref[0]
    vectors, curves, _ = tables((index_ref, lights_ref, curves_ref), passes, parts, cells)
    views = brick_views(parts, cells, rows, inputs)
    fill_ends(parts, cells, rows, [view[0] for view in views] + [far_head], ends_ref)
    count = parts - 1
    tiles = rows // SUB

    def prepare(m, base):
        return prepare_steps(m, views[m], base, cells, rows, knots, cols, ends_ref, cell_refs[m])

    for step in prepare(0, 0):
        step()

    def tile(i, carry):
        base = pl.multiple_of(i * SUB, SUB)
        after = pl.multiple_of(jnp.minimum(i + 1, tiles - 1) * SUB, SUB)
        for m in range(count):
            beside = prepare(m + 1, base) if m + 1 < count else prepare(0, after)
            result = march_unit(flip, vectors, curves, cells, knots, cols, cell_refs[m], beside)
            for p in range(passes):
                for j in range(knots + 1):
                    out_ref[m, p * (knots + 1) + j, pl.ds(base, SUB), :] = result[p][j]
        return carry

    lax.fori_loop(0, tiles, tile, 0)


def over_either(first_leads, one, other):
    shape = one[0].shape
    unit = jnp.ones(shape, jnp.float32)
    scale_one = jnp.where(first_leads, unit, other[0])
    scale_other = jnp.where(first_leads, one[0], unit)
    return [one[0] * other[0]] + [scale_one * a + scale_other * b for a, b in zip(one[1:], other[1:])]


def far_kernel(parts, cells, index_ref, flip_ref, lights_ref, curves_ref, *refs):
    heads, body, states, out_ref, ends_ref, cell_refs = refs[:parts], refs[parts], refs[parts + 1], refs[parts + 2], refs[parts + 3], refs[parts + 4 :]
    rows, cols = out_ref.shape[2:]
    knots = curves_ref.shape[2]
    passes = index_ref.shape[0]
    flip = flip_ref[0]
    me = lax.axis_index("depth")
    vectors, curves, tints = tables((index_ref, lights_ref, curves_ref), passes, parts, cells)
    view = far_view(cells, rows, heads[-1], body)
    fill_ends(parts, cells, rows, heads, ends_ref)
    tiles = rows // SUB

    def prepare(base, slot):
        return prepare_steps(parts - 1, view, base, cells, rows, knots, cols, ends_ref, cell_refs[slot])

    def finish(result, base):
        at = pl.ds(base, SUB)
        for p in range(passes):
            images = [[states[m, p * (knots + 1) + j, at, :] for j in range(knots + 1)] for m in range(parts - 1)]
            images.append(result[p])
            bit = 0
            while len(images) > 1:
                leads = ((me >> bit) & 1) == flip
                images = [over_either(leads, images[j], images[j + 1]) for j in range(0, len(images), 2)]
                bit += 1
            keep, sums = images[0][0], images[0][1:]
            for channel in range(3):
                out_ref[p, channel, at, :] = tree([tints[p][channel][k] * sums[k] for k in range(knots)])
            out_ref[p, 3, at, :] = 1.0 - keep

    for step in prepare(0, 0):
        step()

    def pair(i, carry):
        for slot in range(2):
            base = pl.multiple_of((2 * i + slot) * SUB, SUB)
            after = pl.multiple_of(jnp.minimum(2 * i + slot + 1, tiles - 1) * SUB, SUB)
            result = march_unit(flip, vectors, curves, cells, knots, cols, cell_refs[slot], prepare(after, 1 - slot))
            finish(result, base)
        return carry

    lax.fori_loop(0, tiles // 2, pair, 0)


def shift_along(block, axis, amount):
    count = lax.axis_size(axis)
    route = [(i, i + amount) for i in range(count) if 0 <= i + amount < count]
    return lax.ppermute(block, axis, route)


def swap_along(block, axis, mask):
    return lax.ppermute(block, axis, [(i, i ^ mask) for i in range(lax.axis_size(axis))])


def estimate(micros):
    return pl.CostEstimate(flops=0, transcendentals=0, bytes_accessed=int(micros * 3_690_000))


def on_device(field, light_vectors, transfer, light_index, flips):
    parts = lax.axis_size("depth")
    cells, all_rows, cols = field.shape
    rows = all_rows // parts
    passes = light_index.shape[0]
    channels, knots = transfer.shape[1:]
    in_vmem = pl.BlockSpec(memory_space=VMEM)
    in_smem = pl.BlockSpec(memory_space=SMEM)

    near_rows = 2 * cells + cells * rows + SUB
    head_rows = 2 * cells + 2 * rows + SUB
    body_rows = (cells - 1) * rows + SUB
    shapes = [(near_rows, cols)] * (parts - 1) + [(head_rows, cols), (body_rows, cols)]
    *near, far_head, far_body = pl.pallas_call(
        functools.partial(pack_kernel, parts),
        out_shape=[jax.ShapeDtypeStruct(shape, jnp.float32) for shape in shapes],
        in_specs=[in_vmem],
        out_specs=[in_vmem] * (parts + 1),
        compiler_params=pltpu.CompilerParams(vmem_limit_bytes=12 * MIB),
        cost_estimate=estimate(1),
        name="pack",
    )(field)
    far_head = swap_along(far_head, "depth", parts - 1)
    own = near[0]
    near = [own] + [swap_along(near[m], "depth", m) for m in range(1, parts - 1)]

    edges = pl.pallas_call(
        functools.partial(edge_kernel, parts),
        out_shape=jax.ShapeDtypeStruct((rows, cols), jnp.float32),
        in_specs=[in_vmem, pl.BlockSpec(memory_space=pl.ANY)],
        out_specs=in_vmem,
        compiler_params=pltpu.CompilerParams(vmem_limit_bytes=8 * MIB),
        cost_estimate=estimate(1),
        name="edges",
    )(field, own)
    left = shift_along(edges, "tile", 1)
    right = shift_along(edges, "tile", -1)
    sides = jnp.where(jnp.arange(cols) % 2 == 0, left, right)
    laterals = [sides] + [swap_along(sides, "depth", m) for m in range(1, parts - 1)]
    far_body = swap_along(lax.dynamic_update_slice(far_body, sides, (0, 0)), "depth", parts - 1)

    lights = (light_index, flips, light_vectors, transfer)
    cell_shape = VMEM((knots + 2, cells, SUB, cols), jnp.float32)
    ends_shape = VMEM((parts + 2, 2, rows, cols), jnp.float32)
    states = pl.pallas_call(
        functools.partial(near_kernel, parts, cells),
        out_shape=jax.ShapeDtypeStruct((parts - 1, passes * (knots + 1), rows, cols), jnp.float32),
        in_specs=[in_smem] * 4 + [in_vmem] * (2 * parts - 1),
        out_specs=in_vmem,
        scratch_shapes=[ends_shape] + [cell_shape] * (parts - 1),
        compiler_params=pltpu.CompilerParams(vmem_limit_bytes=16 * MIB),
        cost_estimate=estimate(60),
        name="near",
    )(*lights, *[ref for both in zip(near, laterals) for ref in both], far_head)
    return pl.pallas_call(
        functools.partial(far_kernel, parts, cells),
        out_shape=jax.ShapeDtypeStruct((passes, channels, rows, cols), jnp.float32),
        in_specs=[in_smem] * 4 + [in_vmem] * (parts + 2),
        out_specs=in_vmem,
        scratch_shapes=[ends_shape] + [cell_shape] * 2,
        compiler_params=pltpu.CompilerParams(vmem_limit_bytes=16 * MIB),
        cost_estimate=estimate(5),
        name="far",
    )(*lights, *near, far_head, far_body, states)


def solution(mesh):
    in_specs = (P("depth", None, "tile"), P(), P(), P(), P("tile"))
    out_specs = P(None, None, "depth", "tile")
    return jax.shard_map(
        on_device, mesh=mesh, in_specs=in_specs, out_specs=out_specs, check_vma=False
    )
```

```python
import functools

import jax
import jax.numpy as jnp
from jax import lax
from jax.experimental import pallas as pl
from jax.experimental.pallas import tpu as pltpu
from jax.sharding import PartitionSpec as P

AMBIENT = 0.3
OPACITY = 2.0
SUB = 8
VMEM = pltpu.VMEM
SMEM = pltpu.SMEM
MIB = 1 << 20


def edge_kernel(parts, field_ref, _, out_ref):
    cells, _, cols = field_ref.shape
    rows = out_ref.shape[0]
    lane_pair = lax.broadcasted_iota(jnp.int32, (SUB, cols), 1) // 2

    def tile(i, carry):
        acc = jnp.zeros((SUB, cols), jnp.float32)
        for part in range(parts):
            for z in range(cells):
                slot = part * cells + z
                start = pl.multiple_of(part * rows + i * SUB, SUB)
                value = field_ref[z, pl.ds(start, SUB), :]
                moved = pltpu.roll(value, (2 * slot + 1) % cols, 1)
                acc = jnp.where(lane_pair == slot, moved, acc)
        out_ref[pl.ds(pl.multiple_of(i * SUB, SUB), SUB), :] = acc
        return carry

    lax.fori_loop(0, rows // SUB, tile, 0)


def pack_kernel(parts, field_ref, *outs):
    cells, all_rows, cols = field_ref.shape
    rows = all_rows // parts
    me = lax.axis_index("depth")
    for m in range(parts):
        part = me ^ m
        low = pl.multiple_of(part * rows, SUB)
        above = jnp.where(part > 0, 1.0, 0.0)
        below = jnp.where(part < parts - 1, 1.0, 0.0)
        head = outs[m]
        for z in range(cells):
            head[z : z + 1, :] = field_ref[z, pl.ds(jnp.maximum(low - 1, 0), 1), :] * above
            head[cells + z : cells + z + 1, :] = field_ref[z, pl.ds(jnp.minimum(low + rows, all_rows - 1), 1), :] * below
        for z in range(cells):
            values = field_ref[z, pl.ds(low, rows), :]
            if m < parts - 1:
                head[2 * cells + z * rows : 2 * cells + (z + 1) * rows, :] = values
            elif z == 0:
                head[2 * cells : 2 * cells + rows, :] = values
            elif z == cells - 1:
                head[2 * cells + rows : 2 * cells + 2 * rows, :] = values
            else:
                outs[parts][z * rows : (z + 1) * rows, :] = values


def brick_views(parts, cells, rows, refs):
    views = []
    for m in range(parts - 1):
        head, lateral = refs[2 * m], refs[2 * m + 1]
        views.append((head, [(head, 2 * cells + z * rows) for z in range(cells)], lateral))
    return views


def far_view(cells, rows, head, body):
    places = [(head, 2 * cells)] + [(body, z * rows) for z in range(1, cells - 1)] + [(head, 2 * cells + rows)]
    return head, places, body


def fill_ends(parts, cells, rows, heads, ends_ref):
    me = lax.axis_index("depth")
    ends_ref[0, 1] = jnp.zeros_like(ends_ref[0, 1])
    ends_ref[parts + 1, 0] = jnp.zeros_like(ends_ref[0, 0])
    for m in range(parts):
        last = (cells - 1) * rows if m < parts - 1 else rows
        ends_ref[(me ^ m) + 1, 0] = heads[m][2 * cells : 2 * cells + rows, :]
        ends_ref[(me ^ m) + 1, 1] = heads[m][2 * cells + last : 2 * cells + last + rows, :]


def tables(light_refs, passes, parts, cells):
    index_ref, lights_ref, curves_ref = light_refs
    knots = curves_ref.shape[2]

    def bends(index, channel):
        points = [curves_ref[index, channel, k] for k in range(knots)]
        slopes = [points[k + 1] - points[k] for k in range(knots - 1)]
        return [points[0], slopes[0]] + [slopes[k] - slopes[k - 1] for k in range(1, knots - 1)]

    chosen = [index_ref[p] for p in range(passes)]
    vectors = [[lights_ref[index, axis] for axis in range(3)] for index in chosen]
    scale = OPACITY / (parts * cells)
    curves = [[value * scale for value in bends(index, 3)] for index in chosen]
    tints = [[bends(index, channel) for channel in range(3)] for index in chosen]
    return vectors, curves, tints


def prepare_steps(m, view, base, cells, rows, knots, cols, ends_ref, cell_ref):
    head, places, lateral = view
    me = lax.axis_index("depth")
    part = me ^ m
    at = pl.ds(base, SUB)
    lane = lax.broadcasted_iota(jnp.int32, (SUB, cols), 1)
    sublane = lax.broadcasted_iota(jnp.int32, (SUB, cols), 0)
    is_first = lane == 0
    is_last = lane == cols - 1
    is_top = jnp.logical_and(sublane == 0, base == 0)
    is_bottom = jnp.logical_and(sublane == SUB - 1, base == rows - SUB)
    sides = pltpu.roll(lateral[at, :], (cols - 1 - 2 * cells * me) % cols, 1)

    def layer(z):
        if z < 0:
            return ends_ref[part, 1, at, :]
        if z == cells:
            return ends_ref[part + 2, 0, at, :]
        ref, low = places[z]
        return ref[pl.ds(low + base, SUB), :]

    def step(z):
        ref, low = places[z]
        here = layer(z)
        upper = jnp.where(is_top, head[z : z + 1, :], ref[pl.ds(low + base - 1, SUB), :])
        lower = jnp.where(is_bottom, head[cells + z : cells + z + 1, :], ref[pl.ds(low + base + 1, SUB), :])
        edge = pltpu.roll(sides, (cols - 2 * z) % cols, 1) if z else sides
        grad_x = pltpu.roll(jnp.where(is_first, edge, here), cols - 1, 1) - pltpu.roll(
            jnp.where(is_last, edge, here), 1, 1
        )
        grad_y = lower - upper
        grad_z = layer(z + 1) - layer(z - 1)
        inverse = lax.rsqrt(grad_x * grad_x + grad_y * grad_y + grad_z * grad_z + 4.0)
        half = 0.5 * (knots - 1)
        position = half + half * jnp.tanh(0.5 * here)
        cell_ref[0, z] = grad_x * inverse
        cell_ref[1, z] = grad_y * inverse
        cell_ref[2, z] = grad_z * inverse
        cell_ref[3, z] = position
        for k in range(1, knots - 1):
            cell_ref[3 + k, z] = jnp.maximum(position - k, 0.0)

    return [functools.partial(step, z) for z in range(cells)]


def tree(terms):
    while len(terms) > 1:
        terms = [sum(terms[j + 1 : j + 2], terms[j]) for j in range(0, len(terms), 2)]
    return terms[0]


def march_unit(flip, vectors, curves, cells, knots, cols, cell_ref, beside):
    passes = len(vectors)
    shape = (SUB, cols)
    zero = jnp.zeros(shape, jnp.float32)
    result = []
    beside = list(beside)
    for low in range(0, passes, 2):
        group = range(low, min(low + 2, passes))
        vector = {p: [jnp.full(shape, v) for v in vectors[p]] for p in group}
        curve = {p: [jnp.full(shape, v) for v in curves[p]] for p in group}
        state = {p: (jnp.ones(shape, jnp.float32), [zero] * knots) for p in group}
        share = -(-len(beside) * 2 // max(passes - low, 1))
        mine, beside = beside[:share], beside[share:]
        for u in range(cells):
            for step in mine[u * share // cells : (u + 1) * share // cells]:
                step()
            z = u + flip * (cells - 1 - 2 * u)
            hinges = [cell_ref[3 + k, z] for k in range(knots - 1)]
            normal = [cell_ref[axis, z] for axis in range(3)]
            for p in group:
                keep, sums = state[p]
                opacity = tree([curve[p][0]] + [curve[p][k + 1] * hinges[k] for k in range(knots - 1)])
                facing = normal[0] * vector[p][0] + normal[1] * vector[p][1] + normal[2] * vector[p][2]
                taken = keep * opacity
                weight = taken * (AMBIENT + jnp.abs(facing))
                sums = [sums[0] + weight] + [sums[k + 1] + weight * hinges[k] for k in range(knots - 1)]
                state[p] = (keep - taken, sums)
        result += [[state[p][0]] + state[p][1] for p in group]
    return result


def near_kernel(parts, cells, index_ref, flip_ref, lights_ref, curves_ref, *refs):
    inputs, far_head, out_ref, ends_ref, cell_refs = refs[: 2 * parts - 2], refs[2 * parts - 2], refs[2 * parts - 1], refs[2 * parts], refs[2 * parts + 1 :]
    rows, cols = out_ref.shape[2:]
    knots = curves_ref.shape[2]
    passes = index_ref.shape[0]
    flip = flip_ref[0]
    vectors, curves, _ = tables((index_ref, lights_ref, curves_ref), passes, parts, cells)
    views = brick_views(parts, cells, rows, inputs)
    fill_ends(parts, cells, rows, [view[0] for view in views] + [far_head], ends_ref)
    count = parts - 1
    tiles = rows // SUB

    def prepare(m, base):
        return prepare_steps(m, views[m], base, cells, rows, knots, cols, ends_ref, cell_refs[m])

    for step in prepare(0, 0):
        step()

    def tile(i, carry):
        base = pl.multiple_of(i * SUB, SUB)
        after = pl.multiple_of(jnp.minimum(i + 1, tiles - 1) * SUB, SUB)
        for m in range(count):
            beside = prepare(m + 1, base) if m + 1 < count else prepare(0, after)
            result = march_unit(flip, vectors, curves, cells, knots, cols, cell_refs[m], beside)
            for p in range(passes):
                for j in range(knots + 1):
                    out_ref[m, p * (knots + 1) + j, pl.ds(base, SUB), :] = result[p][j]
        return carry

    lax.fori_loop(0, tiles, tile, 0)


def over_either(first_leads, one, other):
    shape = one[0].shape
    unit = jnp.ones(shape, jnp.float32)
    scale_one = jnp.where(first_leads, unit, other[0])
    scale_other = jnp.where(first_leads, one[0], unit)
    return [one[0] * other[0]] + [scale_one * a + scale_other * b for a, b in zip(one[1:], other[1:])]


def far_kernel(parts, cells, index_ref, flip_ref, lights_ref, curves_ref, *refs):
    heads, body, states, out_ref, ends_ref, cell_refs = refs[:parts], refs[parts], refs[parts + 1], refs[parts + 2], refs[parts + 3], refs[parts + 4 :]
    rows, cols = out_ref.shape[2:]
    knots = curves_ref.shape[2]
    passes = index_ref.shape[0]
    flip = flip_ref[0]
    me = lax.axis_index("depth")
    vectors, curves, tints = tables((index_ref, lights_ref, curves_ref), passes, parts, cells)
    view = far_view(cells, rows, heads[-1], body)
    fill_ends(parts, cells, rows, heads, ends_ref)
    tiles = rows // SUB

    def prepare(base, slot):
        return prepare_steps(parts - 1, view, base, cells, rows, knots, cols, ends_ref, cell_refs[slot])

    def finish(result, base):
        at = pl.ds(base, SUB)
        for p in range(passes):
            images = [[states[m, p * (knots + 1) + j, at, :] for j in range(knots + 1)] for m in range(parts - 1)]
            images.append(result[p])
            bit = 0
            while len(images) > 1:
                leads = ((me >> bit) & 1) == flip
                images = [over_either(leads, images[j], images[j + 1]) for j in range(0, len(images), 2)]
                bit += 1
            keep, sums = images[0][0], images[0][1:]
            for channel in range(3):
                out_ref[p, channel, at, :] = tree([tints[p][channel][k] * sums[k] for k in range(knots)])
            out_ref[p, 3, at, :] = 1.0 - keep

    for step in prepare(0, 0):
        step()

    def pair(i, carry):
        for slot in range(2):
            base = pl.multiple_of((2 * i + slot) * SUB, SUB)
            after = pl.multiple_of(jnp.minimum(2 * i + slot + 1, tiles - 1) * SUB, SUB)
            result = march_unit(flip, vectors, curves, cells, knots, cols, cell_refs[slot], prepare(after, 1 - slot))
            finish(result, base)
        return carry

    lax.fori_loop(0, tiles // 2, pair, 0)


def shift_along(block, axis, amount):
    count = lax.axis_size(axis)
    route = [(i, i + amount) for i in range(count) if 0 <= i + amount < count]
    return lax.ppermute(block, axis, route)


def swap_along(block, axis, mask):
    return lax.ppermute(block, axis, [(i, i ^ mask) for i in range(lax.axis_size(axis))])


def estimate(micros):
    return pl.CostEstimate(flops=int(micros * 1_000_000_000), transcendentals=0, bytes_accessed=0)


def on_device(field, light_vectors, transfer, light_index, flips):
    parts = lax.axis_size("depth")
    cells, all_rows, cols = field.shape
    rows = all_rows // parts
    passes = light_index.shape[0]
    channels, knots = transfer.shape[1:]
    in_vmem = pl.BlockSpec(memory_space=VMEM)
    in_smem = pl.BlockSpec(memory_space=SMEM)

    near_rows = 2 * cells + cells * rows + SUB
    head_rows = 2 * cells + 2 * rows + SUB
    body_rows = (cells - 1) * rows + SUB
    shapes = [(near_rows, cols)] * (parts - 1) + [(head_rows, cols), (body_rows, cols)]
    *near, far_head, far_body = pl.pallas_call(
        functools.partial(pack_kernel, parts),
        out_shape=[jax.ShapeDtypeStruct(shape, jnp.float32) for shape in shapes],
        in_specs=[in_vmem],
        out_specs=[in_vmem] * (parts + 1),
        compiler_params=pltpu.CompilerParams(vmem_limit_bytes=12 * MIB),
        cost_estimate=estimate(1),
        name="pack",
    )(field)
    far_head = swap_along(far_head, "depth", parts - 1)
    own = near[0]
    near = [own] + [swap_along(near[m], "depth", m) for m in range(1, parts - 1)]

    edges = pl.pallas_call(
        functools.partial(edge_kernel, parts),
        out_shape=jax.ShapeDtypeStruct((rows, cols), jnp.float32),
        in_specs=[in_vmem, pl.BlockSpec(memory_space=pl.ANY)],
        out_specs=in_vmem,
        compiler_params=pltpu.CompilerParams(vmem_limit_bytes=8 * MIB),
        cost_estimate=estimate(1),
        name="edges",
    )(field, own)
    left = shift_along(edges, "tile", 1)
    right = shift_along(edges, "tile", -1)
    sides = jnp.where(jnp.arange(cols) % 2 == 0, left, right)
    laterals = [sides] + [swap_along(sides, "depth", m) for m in range(1, parts - 1)]
    *laterals, far_body = lax.optimization_barrier((*laterals, lax.dynamic_update_slice(far_body, sides, (0, 0))))
    far_body = swap_along(far_body, "depth", parts - 1)

    lights = (light_index, flips, light_vectors, transfer)
    cell_shape = VMEM((knots + 2, cells, SUB, cols), jnp.float32)
    ends_shape = VMEM((parts + 2, 2, rows, cols), jnp.float32)
    states = pl.pallas_call(
        functools.partial(near_kernel, parts, cells),
        out_shape=jax.ShapeDtypeStruct((parts - 1, passes * (knots + 1), rows, cols), jnp.float32),
        in_specs=[in_smem] * 4 + [in_vmem] * (2 * parts - 1),
        out_specs=in_vmem,
        scratch_shapes=[ends_shape] + [cell_shape] * (parts - 1),
        compiler_params=pltpu.CompilerParams(vmem_limit_bytes=16 * MIB),
        cost_estimate=estimate(60),
        name="near",
    )(*lights, *[ref for both in zip(near, laterals) for ref in both], far_head)
    return pl.pallas_call(
        functools.partial(far_kernel, parts, cells),
        out_shape=jax.ShapeDtypeStruct((passes, channels, rows, cols), jnp.float32),
        in_specs=[in_smem] * 4 + [in_vmem] * (parts + 2),
        out_specs=in_vmem,
        scratch_shapes=[ends_shape] + [cell_shape] * 2,
        compiler_params=pltpu.CompilerParams(vmem_limit_bytes=16 * MIB),
        cost_estimate=estimate(5),
        name="far",
    )(*lights, *near, far_head, far_body, states)


def solution(mesh):
    in_specs = (P("depth", None, "tile"), P(), P(), P(), P("tile"))
    out_specs = P(None, None, "depth", "tile")
    return jax.shard_map(
        on_device, mesh=mesh, in_specs=in_specs, out_specs=out_specs, check_vma=False
    )
```

```python
import functools

import jax
import jax.numpy as jnp
from jax import lax
from jax.experimental import pallas as pl
from jax.experimental.pallas import tpu as pltpu
from jax.sharding import PartitionSpec as P

AMBIENT = 0.3
OPACITY = 2.0
SUB = 8
VMEM = pltpu.VMEM
SMEM = pltpu.SMEM
MIB = 1 << 20


def near_pack_kernel(parts, field_ref, *refs):
    outs, (rim_ref, sems) = refs[: parts - 2], refs[parts - 2 :]
    cells, all_rows, cols = field_ref.shape
    rows = all_rows // parts
    me = lax.axis_index("depth")
    copies, rims = [], []
    for m in range(1, parts - 1):
        low = pl.multiple_of((me ^ m) * rows, SUB)
        before = pl.multiple_of(jnp.maximum(low - SUB, 0), SUB)
        after = pl.multiple_of(jnp.minimum(low + rows, all_rows - SUB), SUB)
        for side, start in enumerate((before, after)):
            source = field_ref.at[:, pl.ds(start, SUB), :]
            rims.append(pltpu.make_async_copy(source, rim_ref.at[m - 1, side], sems.at[side, m - 1]))
        centre = outs[m - 1].at[pl.ds(2 * cells, cells * rows), :].reshape(cells, rows, cols)
        copies.append(pltpu.make_async_copy(field_ref.at[:, pl.ds(low, rows), :], centre, sems.at[2, m - 1]))
    for copy in rims + copies:
        copy.start()
    for copy in rims:
        copy.wait()
    for m in range(1, parts - 1):
        part = me ^ m
        above = jnp.where(part > 0, 1.0, 0.0)
        below = jnp.where(part < parts - 1, 1.0, 0.0)
        for z in range(cells):
            outs[m - 1][z : z + 1, :] = rim_ref[m - 1, 0, z, SUB - 1 : SUB, :] * above
            outs[m - 1][cells + z : cells + z + 1, :] = rim_ref[m - 1, 1, z, 0:1, :] * below
    for copy in copies:
        copy.wait()


def edge_kernel(parts, field_ref, _, edge_ref, own_ref, head_ref, body_ref):
    cells, all_rows, cols = field_ref.shape
    rows = all_rows // parts
    me = lax.axis_index("depth")
    lane_pair = lax.broadcasted_iota(jnp.int32, (SUB, cols), 1) // 2

    def tile(i, carry):
        acc = jnp.zeros((SUB, cols), jnp.float32)
        for part in range(parts):
            for z in range(cells):
                slot = part * cells + z
                start = pl.multiple_of(part * rows + i * SUB, SUB)
                value = field_ref[z, pl.ds(start, SUB), :]
                moved = pltpu.roll(value, (2 * slot + 1) % cols, 1)
                acc = jnp.where(lane_pair == slot, moved, acc)
        edge_ref[pl.ds(pl.multiple_of(i * SUB, SUB), SUB), :] = acc
        return carry

    lax.fori_loop(0, rows // SUB, tile, 0)
    for m, head in ((0, own_ref), (parts - 1, head_ref)):
        part = me ^ m
        low = pl.multiple_of(part * rows, SUB)
        above = jnp.where(part > 0, 1.0, 0.0)
        below = jnp.where(part < parts - 1, 1.0, 0.0)
        for z in range(cells):
            head[z : z + 1, :] = field_ref[z, pl.ds(jnp.maximum(low - 1, 0), 1), :] * above
            head[cells + z : cells + z + 1, :] = field_ref[z, pl.ds(jnp.minimum(low + rows, all_rows - 1), 1), :] * below
        places = near_places(cells, rows, own_ref) if m == 0 else far_places(cells, rows, parts, head_ref, body_ref)
        for z in range(cells):
            ref, start = places[z]
            ref[start : start + rows, :] = field_ref[z, pl.ds(low, rows), :]


def side_kernel(parts, left_ref, right_ref, *outs):
    rows, cols = left_ref.shape
    group = rows // parts
    width = cols // parts
    me = lax.axis_index("depth")
    lane = lax.broadcasted_iota(jnp.int32, (rows, cols), 1)
    sides = jnp.where(lane % 2 == 0, left_ref[...], right_ref[...])
    for m in range(parts):
        acc = jnp.zeros((group, cols), jnp.float32)
        for j in range(parts):
            moved = pltpu.roll(sides[j * group : (j + 1) * group], (j - (me ^ m) + parts) * width % cols, 1)
            acc = jnp.where(lane[:group] // width == j, moved, acc)
        outs[m][...] = acc


def near_places(cells, rows, head):
    return [(head, 2 * cells + z * rows) for z in range(cells)]


def far_places(cells, rows, parts, head, body):
    skip = rows // parts
    middle = [(body, skip + (z - 1) * rows) for z in range(1, cells - 1)]
    return [(head, 2 * cells)] + middle + [(head, 2 * cells + rows)]


def fill_ends(parts, cells, rows, heads, ends_ref):
    me = lax.axis_index("depth")
    ends_ref[0, 1] = jnp.zeros_like(ends_ref[0, 1])
    ends_ref[parts + 1, 0] = jnp.zeros_like(ends_ref[0, 0])
    for m in range(parts):
        last = (cells - 1) * rows if m < parts - 1 else rows
        ends_ref[(me ^ m) + 1, 0] = heads[m][2 * cells : 2 * cells + rows, :]
        ends_ref[(me ^ m) + 1, 1] = heads[m][2 * cells + last : 2 * cells + last + rows, :]


def fill_table(index_ref, lights_ref, curves_ref, scale, table_ref):
    passes = index_ref.shape[0]
    channels, knots = curves_ref.shape[1:]
    shape = table_ref.shape[2:]
    for p in range(passes):
        chosen = index_ref[p]
        for axis in range(3):
            table_ref[p, axis] = jnp.full(shape, lights_ref[chosen, axis])
        for channel in range(channels):
            factor = scale if channel == channels - 1 else 1.0
            points = [curves_ref[chosen, channel, k] * factor for k in range(knots)]
            slopes = [points[k + 1] - points[k] for k in range(knots - 1)]
            bends = [points[0], slopes[0]] + [slopes[k] - slopes[k - 1] for k in range(1, knots - 1)]
            for k in range(knots):
                table_ref[p, 3 + channel * knots + k] = jnp.full(shape, bends[k])


def prepare_steps(m, zs, head, places, lateral, base, cells, rows, parts, knots, cols, ends_ref, cell_ref):
    me = lax.axis_index("depth")
    part = me ^ m
    at = pl.ds(base, SUB)
    lane = lax.broadcasted_iota(jnp.int32, (SUB, cols), 1)
    sublane = lax.broadcasted_iota(jnp.int32, (SUB, cols), 0)
    is_first = lane == 0
    is_last = lane == cols - 1
    is_top = jnp.logical_and(sublane == 0, base == 0)
    is_bottom = jnp.logical_and(sublane == SUB - 1, base == rows - SUB)
    group = rows // parts
    got = lateral[pl.ds(pl.multiple_of(base % group, SUB), SUB), :]
    sides = pltpu.roll(got, (2 * cols - 1 - base // group * (cols // parts)) % cols, 1)

    def layer(z):
        if z < 0:
            return ends_ref[part, 1, at, :]
        if z == cells:
            return ends_ref[part + 2, 0, at, :]
        ref, low = places[z]
        return ref[pl.ds(low + base, SUB), :]

    def step(z):
        ref, low = places[z]
        here = layer(z)
        upper = jnp.where(is_top, head[z : z + 1, :], ref[pl.ds(low + base - 1, SUB), :])
        lower = jnp.where(is_bottom, head[cells + z : cells + z + 1, :], ref[pl.ds(low + base + 1, SUB), :])
        edge = pltpu.roll(sides, (cols - 2 * z) % cols, 1) if z else sides
        grad_x = pltpu.roll(jnp.where(is_first, edge, here), cols - 1, 1) - pltpu.roll(
            jnp.where(is_last, edge, here), 1, 1
        )
        grad_y = lower - upper
        grad_z = layer(z + 1) - layer(z - 1)
        inverse = lax.rsqrt(grad_x * grad_x + grad_y * grad_y + grad_z * grad_z + 4.0)
        half = 0.5 * (knots - 1)
        position = half + half * jnp.tanh(0.5 * here)
        cell_ref[0, z] = grad_x * inverse
        cell_ref[1, z] = grad_y * inverse
        cell_ref[2, z] = grad_z * inverse
        cell_ref[3, z] = position
        for k in range(1, knots - 1):
            cell_ref[3 + k, z] = jnp.maximum(position - k, 0.0)

    return [functools.partial(step, z) for z in zs]


def tree(terms):
    while len(terms) > 1:
        terms = [sum(terms[j + 1 : j + 2], terms[j]) for j in range(0, len(terms), 2)]
    return terms[0]


def march_unit(flip, table_ref, zs, cells, knots, cell_ref, beside, inner=None):
    passes = table_ref.shape[0]
    shape = table_ref.shape[2:]
    zero = jnp.zeros(shape, jnp.float32)
    curve_at = 3 + 3 * knots
    result = []
    beside = list(beside)
    for low in range(0, passes, 2):
        group = range(low, min(low + 2, passes))
        vector = {p: [table_ref[p, axis] for axis in range(3)] for p in group}
        curve = {p: [table_ref[p, curve_at + k] for k in range(knots)] for p in group}
        state = {p: (jnp.ones(shape, jnp.float32), [zero] * knots) for p in group}
        share = -(-len(beside) * 2 // max(passes - low, 1))
        mine, beside = beside[:share], beside[share:]
        for u, spot in enumerate(zs):
            for step in mine[u * share // len(zs) : (u + 1) * share // len(zs)]:
                step()
            z = spot + flip * (cells - 1 - 2 * spot)
            hinges = [cell_ref[3 + k, z] for k in range(knots - 1)]
            normal = [cell_ref[axis, z] for axis in range(3)]
            for p in group:
                keep, sums = state[p]
                opacity = tree([curve[p][0]] + [curve[p][k + 1] * hinges[k] for k in range(knots - 1)])
                facing = normal[0] * vector[p][0] + normal[1] * vector[p][1] + normal[2] * vector[p][2]
                taken = keep * opacity
                weight = taken * (AMBIENT + jnp.abs(facing))
                sums = [sums[0] + weight] + [sums[k + 1] + weight * hinges[k] for k in range(knots - 1)]
                keep = keep - taken
                if inner is not None and u == 0:
                    keep, sums = keep * inner(p, 0), [total + keep * inner(p, j + 1) for j, total in enumerate(sums)]
                state[p] = (keep, sums)
        result += [[state[p][0]] + state[p][1] for p in group]
    return result


def own_kernel(parts, index_ref, flip_ref, lights_ref, curves_ref, own_ref, lateral_ref, out_ref, table_ref, *cell_refs):
    rows, cols = out_ref.shape[1:]
    knots = curves_ref.shape[2]
    passes = index_ref.shape[0]
    cells = cell_refs[0].shape[1]
    flip = flip_ref[0]
    tiles = rows // SUB
    inner = range(1, cells - 1)
    fill_table(index_ref, lights_ref, curves_ref, OPACITY / (parts * cells), table_ref)
    places = near_places(cells, rows, own_ref)

    def prepare(base, slot):
        return prepare_steps(
            0, inner, own_ref, places, lateral_ref, base, cells, rows, parts, knots, cols, None, cell_refs[slot]
        )

    for step in prepare(0, 0):
        step()

    def pair(i, carry):
        for slot in range(2):
            base = pl.multiple_of((2 * i + slot) * SUB, SUB)
            after = pl.multiple_of(jnp.minimum(2 * i + slot + 1, tiles - 1) * SUB, SUB)
            result = march_unit(flip, table_ref, inner, cells, knots, cell_refs[slot], prepare(after, 1 - slot))
            for p in range(passes):
                for j in range(knots + 1):
                    out_ref[p * (knots + 1) + j, pl.ds(base, SUB), :] = result[p][j]
        return carry

    lax.fori_loop(0, tiles // 2, pair, 0)


def near_kernel(parts, flip_ref, table_ref, inner_ref, *refs):
    count = parts - 1
    heads, laterals, out_ref, ends_ref = refs[:parts], refs[parts : 2 * parts - 1], refs[2 * parts - 1], refs[2 * parts]
    cell_refs = refs[2 * parts + 1 :]
    rows, cols = out_ref.shape[2:]
    cells = cell_refs[0].shape[1]
    passes = table_ref.shape[0]
    knots = inner_ref.shape[0] // passes - 1
    flip = flip_ref[0]
    tiles = rows // SUB
    zs = [(0, cells - 1)] + [range(cells)] * (count - 1)
    places = [near_places(cells, rows, head) for head in heads[:count]]
    fill_ends(parts, cells, rows, heads, ends_ref)

    def prepare(m, base):
        return prepare_steps(
            m, zs[m], heads[m], places[m], laterals[m], base, cells, rows, parts, knots, cols, ends_ref, cell_refs[m]
        )

    for step in prepare(0, 0):
        step()

    def tile(i, carry):
        base = pl.multiple_of(i * SUB, SUB)
        after = pl.multiple_of(jnp.minimum(i + 1, tiles - 1) * SUB, SUB)
        at = pl.ds(base, SUB)
        for m in range(count):
            beside = prepare(m + 1, base) if m + 1 < count else prepare(0, after)
            inner = (lambda p, j: inner_ref[p * (knots + 1) + j, at, :]) if m == 0 else None
            result = march_unit(flip, table_ref, zs[m], cells, knots, cell_refs[m], beside, inner)
            for p in range(passes):
                for j in range(knots + 1):
                    out_ref[m, p * (knots + 1) + j, at, :] = result[p][j]
        return carry

    lax.fori_loop(0, tiles, tile, 0)


def over_either(first_leads, one, other):
    shape = one[0].shape
    unit = jnp.ones(shape, jnp.float32)
    scale_one = jnp.where(first_leads, unit, other[0])
    scale_other = jnp.where(first_leads, one[0], unit)
    return [one[0] * other[0]] + [scale_one * a + scale_other * b for a, b in zip(one[1:], other[1:])]


def far_kernel(parts, flip_ref, table_ref, *refs):
    heads, body, states, out_ref, picture_ref, ends_ref, sems = refs[:parts], *refs[parts : parts + 6]
    cell_refs = refs[parts + 6 :]
    rows, cols = out_ref.shape[2:]
    cells = cell_refs[0].shape[1]
    passes = table_ref.shape[0]
    knots = states.shape[1] // passes - 1
    flip = flip_ref[0]
    me = lax.axis_index("depth")
    places = far_places(cells, rows, parts, heads[-1], body)
    fill_ends(parts, cells, rows, heads, ends_ref)
    tiles = rows // SUB

    def prepare(base, slot):
        return prepare_steps(
            parts - 1, range(cells), heads[-1], places, body, base, cells, rows, parts, knots, cols, ends_ref, cell_refs[slot]
        )

    def send(index):
        at = pl.ds(pl.multiple_of(index * SUB, SUB), SUB)
        return pltpu.make_async_copy(picture_ref.at[:, :, at, :], out_ref.at[:, :, at, :], sems.at[index])

    def finish(result, index):
        at = pl.ds(pl.multiple_of(index * SUB, SUB), SUB)
        for p in range(passes):
            images = [[states[m, p * (knots + 1) + j, at, :] for j in range(knots + 1)] for m in range(parts - 1)]
            images.append(result[p])
            bit = 0
            while len(images) > 1:
                leads = ((me >> bit) & 1) == flip
                images = [over_either(leads, images[j], images[j + 1]) for j in range(0, len(images), 2)]
                bit += 1
            keep, sums = images[0][0], images[0][1:]
            for channel in range(3):
                picture_ref[p, channel, at, :] = tree([table_ref[p, 3 + channel * knots + k] * sums[k] for k in range(knots)])
            picture_ref[p, 3, at, :] = 1.0 - keep
        send(index).start()

    for step in prepare(0, 0):
        step()

    def pair(i, carry):
        for slot in range(2):
            index = 2 * i + slot
            after = pl.multiple_of(jnp.minimum(index + 1, tiles - 1) * SUB, SUB)
            result = march_unit(flip, table_ref, range(cells), cells, knots, cell_refs[slot], prepare(after, 1 - slot))
            finish(result, index)
        return carry

    lax.fori_loop(0, tiles // 2, pair, 0)
    for index in range(tiles):
        send(index).wait()


def shift_along(block, axis, amount):
    count = lax.axis_size(axis)
    route = [(i, i + amount) for i in range(count) if 0 <= i + amount < count]
    return lax.ppermute(block, axis, route)


def swap_along(block, axis, mask):
    return lax.ppermute(block, axis, [(i, i ^ mask) for i in range(lax.axis_size(axis))])


def estimate(micros):
    return pl.CostEstimate(flops=int(micros * 1_000_000_000), transcendentals=0, bytes_accessed=0)


def on_device(field, light_vectors, transfer, light_index, flips):
    parts = lax.axis_size("depth")
    cells, all_rows, cols = field.shape
    rows = all_rows // parts
    passes = light_index.shape[0]
    channels, knots = transfer.shape[1:]
    tiles = rows // SUB
    values = passes * (knots + 1)
    in_vmem = pl.BlockSpec(memory_space=VMEM)
    in_smem = pl.BlockSpec(memory_space=SMEM)
    in_any = pl.BlockSpec(memory_space=pl.ANY)

    def array(*shape):
        return jax.ShapeDtypeStruct(shape, jnp.float32)

    def settings(mib, micros):
        return dict(
            compiler_params=pltpu.CompilerParams(vmem_limit_bytes=mib * MIB),
            cost_estimate=pl.CostEstimate(flops=int(micros * 1e9), transcendentals=0, bytes_accessed=0),
        )

    near_rows = 2 * cells + cells * rows + SUB
    head_rows = 2 * cells + 2 * rows + SUB
    skip = rows // parts
    body_rows = skip + (cells - 2) * rows + SUB
    packed = pl.pallas_call(
        functools.partial(near_pack_kernel, parts),
        out_shape=[array(near_rows, cols)] * (parts - 2),
        in_specs=[in_any],
        out_specs=[in_vmem] * (parts - 2),
        scratch_shapes=[VMEM((parts - 2, 2, cells, SUB, cols), jnp.float32), pltpu.SemaphoreType.DMA((3, parts - 2))],
        name="pack",
        **settings(8, 1),
    )(field)
    near = [swap_along(packed[m - 1], "depth", m) for m in range(1, parts - 1)]

    edges, own, far_head, far_body = pl.pallas_call(
        functools.partial(edge_kernel, parts),
        out_shape=[array(rows, cols), array(near_rows, cols), array(head_rows, cols), array(body_rows, cols)],
        in_specs=[in_vmem, in_any],
        out_specs=[in_vmem] * 4,
        name="edges",
        **settings(8, 1),
    )(field, packed[0])
    far_head = swap_along(far_head, "depth", parts - 1)
    sides = pl.pallas_call(
        functools.partial(side_kernel, parts),
        out_shape=[array(skip, cols)] * parts,
        in_specs=[in_vmem] * 2,
        out_specs=[in_vmem] * parts,
        name="sides",
        **settings(4, 0.1),
    )(shift_along(edges, "tile", 1), shift_along(edges, "tile", -1))
    laterals = [swap_along(sides[m], "depth", m) for m in range(1, parts - 1)]
    *laterals, far_body = lax.optimization_barrier((*laterals, lax.dynamic_update_slice(far_body, sides[-1], (0, 0))))
    far_body = swap_along(far_body, "depth", parts - 1)

    cell_shape = VMEM((knots + 2, cells, SUB, cols), jnp.float32)
    ends_shape = VMEM((parts + 2, 2, rows, cols), jnp.float32)
    inner, table = pl.pallas_call(
        functools.partial(own_kernel, parts),
        out_shape=[array(values, rows, cols), array(passes, 3 + channels * knots, SUB, cols)],
        in_specs=[in_smem] * 4 + [in_vmem] * 2,
        out_specs=[in_vmem] * 2,
        scratch_shapes=[cell_shape] * 2,
        name="own",
        **settings(8, 4),
    )(light_index, flips, light_vectors, transfer, own, sides[0])
    states = pl.pallas_call(
        functools.partial(near_kernel, parts),
        out_shape=array(parts - 1, values, rows, cols),
        in_specs=[in_smem] + [in_vmem] * (2 * parts + 1),
        out_specs=in_vmem,
        scratch_shapes=[ends_shape] + [cell_shape] * (parts - 1),
        name="near",
        **settings(16, 60),
    )(flips, table, inner, own, *near, far_head, sides[0], *laterals)
    return pl.pallas_call(
        functools.partial(far_kernel, parts),
        out_shape=array(passes, channels, rows, cols),
        in_specs=[in_smem] + [in_vmem] * (parts + 3),
        out_specs=in_any,
        scratch_shapes=[
            VMEM((passes, channels, rows, cols), jnp.float32),
            ends_shape,
            pltpu.SemaphoreType.DMA((tiles,)),
        ]
        + [cell_shape] * 2,
        name="far",
        **settings(16, 5),
    )(flips, table, own, *near, far_head, far_body, states)


def solution(mesh):
    in_specs = (P("depth", None, "tile"), P(), P(), P(), P("tile"))
    out_specs = P(None, None, "depth", "tile")
    return jax.shard_map(
        on_device, mesh=mesh, in_specs=in_specs, out_specs=out_specs, check_vma=False
    )
```

```python
import functools

import jax
import jax.numpy as jnp
from jax import lax
from jax.experimental import pallas as pl
from jax.experimental.pallas import tpu as pltpu
from jax.sharding import PartitionSpec as P

AMBIENT = 0.3
OPACITY = 2.0
SUB = 8
VMEM = pltpu.VMEM
SMEM = pltpu.SMEM
MIB = 1 << 20


def pack_kernel(parts, field_ref, *refs):
    outs, (rim_ref, sems) = refs[: parts - 1], refs[parts - 1 :]
    cells, all_rows, cols = field_ref.shape
    rows = all_rows // parts
    me = lax.axis_index("depth")
    copies, rims = [], []
    for j, out in enumerate(outs):
        low = pl.multiple_of((me ^ (j + 1)) * rows, SUB)
        before = pl.multiple_of(jnp.maximum(low - SUB, 0), SUB)
        after = pl.multiple_of(jnp.minimum(low + rows, all_rows - SUB), SUB)
        for side, start in enumerate((before, after)):
            source = field_ref.at[:, pl.ds(start, SUB), :]
            rims.append(pltpu.make_async_copy(source, rim_ref.at[j, side], sems.at[side, j]))
        block = field_ref.at[:, pl.ds(low, rows), :]
        if j < parts - 2:
            centre = out.at[pl.ds(2 * cells, cells * rows), :].reshape(cells, rows, cols)
            copies.append(pltpu.make_async_copy(block, centre, sems.at[2, j]))
        else:
            for side in range(2):
                layer = out.at[pl.ds(2 * cells + side * rows, rows), :]
                copies.append(pltpu.make_async_copy(block.at[side * (cells - 1)], layer, sems.at[2 + side, j]))
    for copy in rims + copies:
        copy.start()
    for copy in rims:
        copy.wait()
    for j, out in enumerate(outs):
        part = me ^ (j + 1)
        above = jnp.where(part > 0, 1.0, 0.0)
        below = jnp.where(part < parts - 1, 1.0, 0.0)
        for z in range(cells):
            out[z : z + 1, :] = rim_ref[j, 0, z, SUB - 1 : SUB, :] * above
            out[cells + z : cells + z + 1, :] = rim_ref[j, 1, z, 0:1, :] * below
    for copy in copies:
        copy.wait()


def edge_kernel(parts, field_ref, _, edge_ref, own_ref, body_ref):
    cells, all_rows, cols = field_ref.shape
    rows = all_rows // parts
    me = lax.axis_index("depth")
    lane_pair = lax.broadcasted_iota(jnp.int32, (SUB, cols), 1) // 2

    def tile(i, carry):
        acc = jnp.zeros((SUB, cols), jnp.float32)
        for part in range(parts):
            for z in range(cells):
                slot = part * cells + z
                start = pl.multiple_of(part * rows + i * SUB, SUB)
                value = field_ref[z, pl.ds(start, SUB), :]
                moved = pltpu.roll(value, (2 * slot + 1) % cols, 1)
                acc = jnp.where(lane_pair == slot, moved, acc)
        edge_ref[pl.ds(pl.multiple_of(i * SUB, SUB), SUB), :] = acc
        return carry

    lax.fori_loop(0, rows // SUB, tile, 0)
    low = pl.multiple_of(me * rows, SUB)
    above = jnp.where(me > 0, 1.0, 0.0)
    below = jnp.where(me < parts - 1, 1.0, 0.0)
    for z in range(cells):
        own_ref[z : z + 1, :] = field_ref[z, pl.ds(jnp.maximum(low - 1, 0), 1), :] * above
        own_ref[cells + z : cells + z + 1, :] = field_ref[z, pl.ds(jnp.minimum(low + rows, all_rows - 1), 1), :] * below
    far_low = pl.multiple_of((me ^ (parts - 1)) * rows, SUB)
    own_places = near_places(cells, rows, own_ref)
    body_places = far_places(cells, rows, parts, None, body_ref)
    for z in range(cells):
        ref, start = own_places[z]
        ref[start : start + rows, :] = field_ref[z, pl.ds(low, rows), :]
    for z in range(1, cells - 1):
        ref, start = body_places[z]
        ref[start : start + rows, :] = field_ref[z, pl.ds(far_low, rows), :]


def side_kernel(parts, left_ref, right_ref, _, *outs):
    rows, cols = left_ref.shape
    group = rows // parts
    width = cols // parts
    me = lax.axis_index("depth")
    lane = lax.broadcasted_iota(jnp.int32, (rows, cols), 1)
    sides = jnp.where(lane % 2 == 0, left_ref[...], right_ref[...])
    for m in range(parts):
        acc = jnp.zeros((group, cols), jnp.float32)
        for j in range(parts):
            moved = pltpu.roll(sides[j * group : (j + 1) * group], (j - (me ^ m) + parts) * width % cols, 1)
            acc = jnp.where(lane[:group] // width == j, moved, acc)
        outs[m][...] = acc


def near_places(cells, rows, head):
    return [(head, 2 * cells + z * rows) for z in range(cells)]


def far_places(cells, rows, parts, head, body):
    skip = rows // parts
    middle = [(body, skip + (z - 1) * rows) for z in range(1, cells - 1)]
    return [(head, 2 * cells)] + middle + [(head, 2 * cells + rows)]


def fill_ends(parts, cells, rows, heads, ends_ref):
    me = lax.axis_index("depth")
    ends_ref[0, 1] = jnp.zeros_like(ends_ref[0, 1])
    ends_ref[parts + 1, 0] = jnp.zeros_like(ends_ref[0, 0])
    for m in range(parts):
        last = (cells - 1) * rows if m < parts - 1 else rows
        ends_ref[(me ^ m) + 1, 0] = heads[m][2 * cells : 2 * cells + rows, :]
        ends_ref[(me ^ m) + 1, 1] = heads[m][2 * cells + last : 2 * cells + last + rows, :]


def fill_table(index_ref, lights_ref, curves_ref, scale, table_ref):
    passes = index_ref.shape[0]
    channels, knots = curves_ref.shape[1:]
    shape = table_ref.shape[2:]
    for p in range(passes):
        chosen = index_ref[p]
        for axis in range(3):
            table_ref[p, axis] = jnp.full(shape, lights_ref[chosen, axis])
        for channel in range(channels):
            factor = scale if channel == channels - 1 else 1.0
            points = [curves_ref[chosen, channel, k] * factor for k in range(knots)]
            slopes = [points[k + 1] - points[k] for k in range(knots - 1)]
            bends = [points[0], slopes[0]] + [slopes[k] - slopes[k - 1] for k in range(1, knots - 1)]
            for k in range(knots):
                table_ref[p, 3 + channel * knots + k] = jnp.full(shape, bends[k])


def prepare_steps(m, zs, head, places, lateral, base, cells, rows, parts, knots, cols, ends_ref, cell_ref):
    me = lax.axis_index("depth")
    part = me ^ m
    at = pl.ds(base, SUB)
    lane = lax.broadcasted_iota(jnp.int32, (SUB, cols), 1)
    sublane = lax.broadcasted_iota(jnp.int32, (SUB, cols), 0)
    is_first = lane == 0
    is_last = lane == cols - 1
    is_top = jnp.logical_and(sublane == 0, base == 0)
    is_bottom = jnp.logical_and(sublane == SUB - 1, base == rows - SUB)
    group = rows // parts
    got = lateral[pl.ds(pl.multiple_of(base % group, SUB), SUB), :]
    sides = pltpu.roll(got, (2 * cols - 1 - base // group * (cols // parts)) % cols, 1)

    def layer(z):
        if z < 0:
            return ends_ref[part, 1, at, :]
        if z == cells:
            return ends_ref[part + 2, 0, at, :]
        ref, low = places[z]
        return ref[pl.ds(low + base, SUB), :]

    def step(z):
        ref, low = places[z]
        here = layer(z)
        upper = jnp.where(is_top, head[z : z + 1, :], ref[pl.ds(low + base - 1, SUB), :])
        lower = jnp.where(is_bottom, head[cells + z : cells + z + 1, :], ref[pl.ds(low + base + 1, SUB), :])
        edge = pltpu.roll(sides, (cols - 2 * z) % cols, 1) if z else sides
        grad_x = pltpu.roll(jnp.where(is_first, edge, here), cols - 1, 1) - pltpu.roll(
            jnp.where(is_last, edge, here), 1, 1
        )
        grad_y = lower - upper
        grad_z = layer(z + 1) - layer(z - 1)
        inverse = lax.rsqrt(grad_x * grad_x + grad_y * grad_y + grad_z * grad_z + 4.0)
        half = 0.5 * (knots - 1)
        position = half + half * jnp.tanh(0.5 * here)
        cell_ref[0, z] = grad_x * inverse
        cell_ref[1, z] = grad_y * inverse
        cell_ref[2, z] = grad_z * inverse
        cell_ref[3, z] = position
        for k in range(1, knots - 1):
            cell_ref[3 + k, z] = jnp.maximum(position - k, 0.0)

    return [functools.partial(step, z) for z in zs]


def tree(terms):
    while len(terms) > 1:
        terms = [sum(terms[j + 1 : j + 2], terms[j]) for j in range(0, len(terms), 2)]
    return terms[0]


def march_unit(flip, table_ref, zs, cells, knots, cell_ref, beside, inner=None):
    passes = table_ref.shape[0]
    shape = table_ref.shape[2:]
    zero = jnp.zeros(shape, jnp.float32)
    curve_at = 3 + 3 * knots
    result = []
    beside = list(beside)
    for low in range(0, passes, 2):
        group = range(low, min(low + 2, passes))
        vector = {p: [table_ref[p, axis] for axis in range(3)] for p in group}
        curve = {p: [table_ref[p, curve_at + k] for k in range(knots)] for p in group}
        state = {p: (jnp.ones(shape, jnp.float32), [zero] * knots) for p in group}
        share = -(-len(beside) * 2 // max(passes - low, 1))
        mine, beside = beside[:share], beside[share:]
        for u, spot in enumerate(zs):
            for step in mine[u * share // len(zs) : (u + 1) * share // len(zs)]:
                step()
            z = spot + flip * (cells - 1 - 2 * spot)
            hinges = [cell_ref[3 + k, z] for k in range(knots - 1)]
            normal = [cell_ref[axis, z] for axis in range(3)]
            for p in group:
                keep, sums = state[p]
                opacity = tree([curve[p][0]] + [curve[p][k + 1] * hinges[k] for k in range(knots - 1)])
                facing = normal[0] * vector[p][0] + normal[1] * vector[p][1] + normal[2] * vector[p][2]
                taken = keep * opacity
                weight = taken * (AMBIENT + jnp.abs(facing))
                sums = [sums[0] + weight] + [sums[k + 1] + weight * hinges[k] for k in range(knots - 1)]
                keep = keep - taken
                if inner is not None and u == 0:
                    keep, sums = keep * inner(p, 0), [total + keep * inner(p, j + 1) for j, total in enumerate(sums)]
                state[p] = (keep, sums)
        result += [[state[p][0]] + state[p][1] for p in group]
    return result


def own_kernel(parts, index_ref, flip_ref, lights_ref, curves_ref, own_ref, lateral_ref, out_ref, table_ref, *cell_refs):
    rows, cols = out_ref.shape[1:]
    knots = curves_ref.shape[2]
    passes = index_ref.shape[0]
    cells = cell_refs[0].shape[1]
    flip = flip_ref[0]
    tiles = rows // SUB
    inner = range(1, cells - 1)
    fill_table(index_ref, lights_ref, curves_ref, OPACITY / (parts * cells), table_ref)
    places = near_places(cells, rows, own_ref)

    def prepare(base, slot):
        return prepare_steps(
            0, inner, own_ref, places, lateral_ref, base, cells, rows, parts, knots, cols, None, cell_refs[slot]
        )

    for step in prepare(0, 0):
        step()

    def pair(i, carry):
        for slot in range(2):
            base = pl.multiple_of((2 * i + slot) * SUB, SUB)
            after = pl.multiple_of(jnp.minimum(2 * i + slot + 1, tiles - 1) * SUB, SUB)
            result = march_unit(flip, table_ref, inner, cells, knots, cell_refs[slot], prepare(after, 1 - slot))
            for p in range(passes):
                for j in range(knots + 1):
                    out_ref[p * (knots + 1) + j, pl.ds(base, SUB), :] = result[p][j]
        return carry

    lax.fori_loop(0, tiles // 2, pair, 0)


def near_kernel(parts, flip_ref, table_ref, inner_ref, *refs):
    count = parts - 1
    heads, laterals, out_ref, ends_ref = refs[:parts], refs[parts : 2 * parts - 1], refs[2 * parts - 1], refs[2 * parts]
    cell_refs = refs[2 * parts + 1 :]
    rows, cols = out_ref.shape[2:]
    cells = cell_refs[0].shape[1]
    passes = table_ref.shape[0]
    knots = inner_ref.shape[0] // passes - 1
    flip = flip_ref[0]
    tiles = rows // SUB
    zs = [(0, cells - 1)] + [range(cells)] * (count - 1)
    places = [near_places(cells, rows, head) for head in heads[:count]]
    fill_ends(parts, cells, rows, heads, ends_ref)

    def prepare(m, base):
        return prepare_steps(
            m, zs[m], heads[m], places[m], laterals[m], base, cells, rows, parts, knots, cols, ends_ref, cell_refs[m]
        )

    for step in prepare(0, 0):
        step()

    def tile(i, carry):
        base = pl.multiple_of(i * SUB, SUB)
        after = pl.multiple_of(jnp.minimum(i + 1, tiles - 1) * SUB, SUB)
        at = pl.ds(base, SUB)
        for m in range(count):
            beside = prepare(m + 1, base) if m + 1 < count else prepare(0, after)
            inner = (lambda p, j: inner_ref[p * (knots + 1) + j, at, :]) if m == 0 else None
            result = march_unit(flip, table_ref, zs[m], cells, knots, cell_refs[m], beside, inner)
            for p in range(passes):
                for j in range(knots + 1):
                    out_ref[m, p * (knots + 1) + j, at, :] = result[p][j]
        return carry

    lax.fori_loop(0, tiles, tile, 0)


def over_either(first_leads, one, other):
    shape = one[0].shape
    unit = jnp.ones(shape, jnp.float32)
    scale_one = jnp.where(first_leads, unit, other[0])
    scale_other = jnp.where(first_leads, one[0], unit)
    return [one[0] * other[0]] + [scale_one * a + scale_other * b for a, b in zip(one[1:], other[1:])]


def far_kernel(parts, flip_ref, table_ref, *refs):
    heads, body, states, out_ref, picture_ref, ends_ref, sems = refs[:parts], *refs[parts : parts + 6]
    cell_refs = refs[parts + 6 :]
    rows, cols = out_ref.shape[2:]
    cells = cell_refs[0].shape[1]
    passes = table_ref.shape[0]
    knots = states.shape[1] // passes - 1
    flip = flip_ref[0]
    me = lax.axis_index("depth")
    places = far_places(cells, rows, parts, heads[-1], body)
    fill_ends(parts, cells, rows, heads, ends_ref)
    tiles = rows // SUB

    def prepare(base, slot):
        return prepare_steps(
            parts - 1, range(cells), heads[-1], places, body, base, cells, rows, parts, knots, cols, ends_ref, cell_refs[slot]
        )

    def send(index):
        at = pl.ds(pl.multiple_of(index * SUB, SUB), SUB)
        return pltpu.make_async_copy(picture_ref.at[:, :, at, :], out_ref.at[:, :, at, :], sems.at[index])

    def finish(result, index):
        at = pl.ds(pl.multiple_of(index * SUB, SUB), SUB)
        for p in range(passes):
            images = [[states[m, p * (knots + 1) + j, at, :] for j in range(knots + 1)] for m in range(parts - 1)]
            images.append(result[p])
            bit = 0
            while len(images) > 1:
                leads = ((me >> bit) & 1) == flip
                images = [over_either(leads, images[j], images[j + 1]) for j in range(0, len(images), 2)]
                bit += 1
            keep, sums = images[0][0], images[0][1:]
            for channel in range(3):
                picture_ref[p, channel, at, :] = tree([table_ref[p, 3 + channel * knots + k] * sums[k] for k in range(knots)])
            picture_ref[p, 3, at, :] = 1.0 - keep
        send(index).start()

    for step in prepare(0, 0):
        step()

    def pair(i, carry):
        for slot in range(2):
            index = 2 * i + slot
            after = pl.multiple_of(jnp.minimum(index + 1, tiles - 1) * SUB, SUB)
            result = march_unit(flip, table_ref, range(cells), cells, knots, cell_refs[slot], prepare(after, 1 - slot))
            finish(result, index)
        return carry

    lax.fori_loop(0, tiles // 2, pair, 0)
    for index in range(tiles):
        send(index).wait()


def shift_along(block, axis, amount):
    count = lax.axis_size(axis)
    route = [(i, i + amount) for i in range(count) if 0 <= i + amount < count]
    return lax.ppermute(block, axis, route)


def swap_along(block, axis, mask):
    return lax.ppermute(block, axis, [(i, i ^ mask) for i in range(lax.axis_size(axis))])


def estimate(micros):
    return pl.CostEstimate(flops=int(micros * 1_000_000_000), transcendentals=0, bytes_accessed=0)


def on_device(field, light_vectors, transfer, light_index, flips):
    parts = lax.axis_size("depth")
    cells, all_rows, cols = field.shape
    rows = all_rows // parts
    passes = light_index.shape[0]
    channels, knots = transfer.shape[1:]
    tiles = rows // SUB
    values = passes * (knots + 1)
    in_vmem = pl.BlockSpec(memory_space=VMEM)
    in_smem = pl.BlockSpec(memory_space=SMEM)
    in_any = pl.BlockSpec(memory_space=pl.ANY)
    in_hbm = pl.BlockSpec(memory_space=pltpu.HBM)

    def array(*shape):
        return jax.ShapeDtypeStruct(shape, jnp.float32)

    def settings(mib, micros):
        return dict(
            compiler_params=pltpu.CompilerParams(vmem_limit_bytes=mib * MIB),
            cost_estimate=pl.CostEstimate(flops=int(micros * 1e9), transcendentals=0, bytes_accessed=0),
        )

    near_rows = 2 * cells + cells * rows + SUB
    head_rows = 2 * cells + 2 * rows + SUB
    skip = rows // parts
    body_rows = skip + (cells - 2) * rows + SUB
    *packed, far_head = pl.pallas_call(
        functools.partial(pack_kernel, parts),
        out_shape=[array(near_rows, cols)] * (parts - 2) + [array(head_rows, cols)],
        in_specs=[in_hbm],
        out_specs=[in_vmem] * (parts - 1),
        scratch_shapes=[VMEM((parts - 1, 2, cells, SUB, cols), jnp.float32), pltpu.SemaphoreType.DMA((4, parts - 1))],
        name="pack",
        **settings(8, 1),
    )(field)
    near = [swap_along(packed[m - 1], "depth", m) for m in range(1, parts - 1)]

    far_head = swap_along(far_head, "depth", parts - 1)

    edges, own, far_body = pl.pallas_call(
        functools.partial(edge_kernel, parts),
        out_shape=[array(rows, cols), array(near_rows, cols), array(body_rows, cols)],
        in_specs=[in_vmem, in_any],
        out_specs=[in_vmem] * 3,
        name="edges",
        **settings(8, 1),
    )(field, packed[0])
    sides = pl.pallas_call(
        functools.partial(side_kernel, parts),
        out_shape=[array(skip, cols)] * parts,
        in_specs=[in_vmem] * 2 + [in_any],
        out_specs=[in_vmem] * parts,
        name="sides",
        **settings(4, 0.1),
    )(shift_along(edges, "tile", 1), shift_along(edges, "tile", -1), far_head)
    laterals = [swap_along(sides[m], "depth", m) for m in range(1, parts - 1)]
    far_body = swap_along(lax.dynamic_update_slice(far_body, sides[-1], (0, 0)), "depth", parts - 1)

    cell_shape = VMEM((knots + 2, cells, SUB, cols), jnp.float32)
    ends_shape = VMEM((parts + 2, 2, rows, cols), jnp.float32)
    inner, table = pl.pallas_call(
        functools.partial(own_kernel, parts),
        out_shape=[array(values, rows, cols), array(passes, 3 + channels * knots, SUB, cols)],
        in_specs=[in_smem] * 4 + [in_vmem] * 2,
        out_specs=[in_vmem] * 2,
        scratch_shapes=[cell_shape] * 2,
        name="own",
        **settings(8, 4),
    )(light_index, flips, light_vectors, transfer, own, sides[0])
    states = pl.pallas_call(
        functools.partial(near_kernel, parts),
        out_shape=array(parts - 1, values, rows, cols),
        in_specs=[in_smem] + [in_vmem] * (2 * parts + 1),
        out_specs=in_vmem,
        scratch_shapes=[ends_shape] + [cell_shape] * (parts - 1),
        name="near",
        **settings(16, 60),
    )(flips, table, inner, own, *near, far_head, sides[0], *laterals)
    return pl.pallas_call(
        functools.partial(far_kernel, parts),
        out_shape=array(passes, channels, rows, cols),
        in_specs=[in_smem] + [in_vmem] * (parts + 3),
        out_specs=in_any,
        scratch_shapes=[
            VMEM((passes, channels, rows, cols), jnp.float32),
            ends_shape,
            pltpu.SemaphoreType.DMA((tiles,)),
        ]
        + [cell_shape] * 2,
        name="far",
        **settings(16, 5),
    )(flips, table, own, *near, far_head, far_body, states)


def solution(mesh):
    in_specs = (P("depth", None, "tile"), P(), P(), P(), P("tile"))
    out_specs = P(None, None, "depth", "tile")
    return jax.shard_map(
        on_device, mesh=mesh, in_specs=in_specs, out_specs=out_specs, check_vma=False
    )
```

```python
import functools

import jax
import jax.numpy as jnp
from jax import lax
from jax.experimental import pallas as pl
from jax.experimental.pallas import tpu as pltpu
from jax.sharding import PartitionSpec as P

AMBIENT = 0.3
OPACITY = 2.0
SUB = 8
VMEM = pltpu.VMEM
SMEM = pltpu.SMEM
MIB = 1 << 20
FINE = 49152.0


def pack_kernel(parts, field_ref, *refs):
    outs, (rim_ref, sems) = refs[: parts - 1], refs[parts - 1 :]
    cells, all_rows, cols = field_ref.shape
    rows = all_rows // parts
    me = lax.axis_index("depth")
    copies, rims = [], []
    for j, out in enumerate(outs):
        low = pl.multiple_of((me ^ (j + 1)) * rows, SUB)
        before = pl.multiple_of(jnp.maximum(low - SUB, 0), SUB)
        after = pl.multiple_of(jnp.minimum(low + rows, all_rows - SUB), SUB)
        for side, start in enumerate((before, after)):
            source = field_ref.at[:, pl.ds(start, SUB), :]
            rims.append(pltpu.make_async_copy(source, rim_ref.at[j, side], sems.at[side, j]))
        block = field_ref.at[:, pl.ds(low, rows), :]
        if j < parts - 2:
            centre = out.at[pl.ds(2 * cells, cells * rows), :].reshape(cells, rows, cols)
            copies.append(pltpu.make_async_copy(block, centre, sems.at[2, j]))
        else:
            for side in range(2):
                layer = out.at[pl.ds(2 * cells + side * rows, rows), :]
                copies.append(pltpu.make_async_copy(block.at[side * (cells - 1)], layer, sems.at[2 + side, j]))
    for copy in rims + copies:
        copy.start()
    for copy in rims:
        copy.wait()
    for j, out in enumerate(outs):
        part = me ^ (j + 1)
        above = jnp.where(part > 0, 1.0, 0.0)
        below = jnp.where(part < parts - 1, 1.0, 0.0)
        for z in range(cells):
            out[z : z + 1, :] = rim_ref[j, 0, z, SUB - 1 : SUB, :] * above
            out[cells + z : cells + z + 1, :] = rim_ref[j, 1, z, 0:1, :] * below
    for copy in copies:
        copy.wait()


def edge_kernel(parts, field_ref, _, edge_ref, own_ref, body_ref):
    cells, all_rows, cols = field_ref.shape
    rows = all_rows // parts
    me = lax.axis_index("depth")
    lane_pair = lax.broadcasted_iota(jnp.int32, (SUB, cols), 1) // 2

    def tile(i, carry):
        acc = jnp.zeros((SUB, cols), jnp.float32)
        for part in range(parts):
            for z in range(cells):
                slot = part * cells + z
                start = pl.multiple_of(part * rows + i * SUB, SUB)
                value = field_ref[z, pl.ds(start, SUB), :]
                moved = pltpu.roll(value, (2 * slot + 1) % cols, 1)
                acc = jnp.where(lane_pair == slot, moved, acc)
        edge_ref[pl.ds(pl.multiple_of(i * SUB, SUB), SUB), :] = acc
        return carry

    lax.fori_loop(0, rows // SUB, tile, 0)
    low = pl.multiple_of(me * rows, SUB)
    above = jnp.where(me > 0, 1.0, 0.0)
    below = jnp.where(me < parts - 1, 1.0, 0.0)
    for z in range(cells):
        own_ref[z : z + 1, :] = field_ref[z, pl.ds(jnp.maximum(low - 1, 0), 1), :] * above
        own_ref[cells + z : cells + z + 1, :] = field_ref[z, pl.ds(jnp.minimum(low + rows, all_rows - 1), 1), :] * below
    far_low = pl.multiple_of((me ^ (parts - 1)) * rows, SUB)
    own_places = near_places(cells, rows, own_ref)
    body_places = far_places(cells, rows, parts, None, body_ref)
    for z in range(cells):
        ref, start = own_places[z]
        ref[start : start + rows, :] = field_ref[z, pl.ds(low, rows), :]
    for z in range(1, cells - 1):
        ref, start = body_places[z]
        ref[start : start + rows, :] = field_ref[z, pl.ds(far_low, rows), :]


def side_kernel(parts, left_ref, right_ref, _, *outs):
    rows, cols = left_ref.shape
    group = rows // parts
    width = cols // parts
    me = lax.axis_index("depth")
    lane = lax.broadcasted_iota(jnp.int32, (rows, cols), 1)
    sides = jnp.where(lane % 2 == 0, left_ref[...], right_ref[...])
    for m in range(parts):
        acc = jnp.zeros((group, cols), jnp.float32)
        for j in range(parts):
            moved = pltpu.roll(sides[j * group : (j + 1) * group], (j - (me ^ m) + parts) * width % cols, 1)
            acc = jnp.where(lane[:group] // width == j, moved, acc)
        outs[m][...] = acc


def near_places(cells, rows, head):
    return [(head, 2 * cells + z * rows) for z in range(cells)]


def far_places(cells, rows, parts, head, body):
    skip = rows // parts
    middle = [(body, skip + (z - 1) * rows) for z in range(1, cells - 1)]
    return [(head, 2 * cells)] + middle + [(head, 2 * cells + rows)]


def fill_ends(parts, cells, rows, heads, ends_ref):
    me = lax.axis_index("depth")
    ends_ref[0, 1] = jnp.zeros_like(ends_ref[0, 1])
    ends_ref[parts + 1, 0] = jnp.zeros_like(ends_ref[0, 0])
    for m in range(parts):
        last = (cells - 1) * rows if m < parts - 1 else rows
        ends_ref[(me ^ m) + 1, 0] = heads[m][2 * cells : 2 * cells + rows, :]
        ends_ref[(me ^ m) + 1, 1] = heads[m][2 * cells + last : 2 * cells + last + rows, :]


def fill_weights(index_ref, curves_ref, scale, weight_ref):
    passes = index_ref.shape[0]
    channels, knots = curves_ref.shape[1:]
    shape = (2 * SUB, weight_ref.shape[1])
    row = lax.broadcasted_iota(jnp.int32, shape, 0)
    lane = lax.broadcasted_iota(jnp.int32, shape, 1)
    block = knots * SUB
    knot = lane // SUB
    on_row = lane % SUB == row % SUB
    zero = jnp.zeros(shape, jnp.float32)
    for pair in range(passes * channels // 2):
        halves = []
        for channel in (2 * pair, 2 * pair + 1):
            chosen = index_ref[channel // channels]
            factor = scale if channel % channels == channels - 1 else 1.0
            points = [curves_ref[chosen, channel % channels, k] * factor for k in range(knots)]
            half = zero
            for k in range(knots):
                half = jnp.where(jnp.logical_or(knot == k, knot == k + 2 * knots), points[k], half)
                if k + 1 < knots:
                    half = jnp.where(knot == k + knots, points[k + 1] - points[k], half)
            halves.append(half)
        value = jnp.where(on_row, jnp.where(row < SUB, halves[0], halves[1]), zero)
        coarse = value.astype(jnp.bfloat16).astype(jnp.float32)
        value = jnp.where(lane < 2 * block, value, value - coarse)
        weight_ref[2 * pair * SUB : 2 * (pair + 1) * SUB, :] = value.astype(jnp.bfloat16)


def prepare_steps(m, zs, head, places, lateral, base, cells, rows, parts, cols, ends_ref, weight_ref, cell_ref, mixed_ref):
    me = lax.axis_index("depth")
    part = me ^ m
    at = pl.ds(base, SUB)
    lane = lax.broadcasted_iota(jnp.int32, (SUB, cols), 1)
    sublane = lax.broadcasted_iota(jnp.int32, (SUB, cols), 0)
    is_first = lane == 0
    is_last = lane == cols - 1
    is_top = jnp.logical_and(sublane == 0, base == 0)
    is_bottom = jnp.logical_and(sublane == SUB - 1, base == rows - SUB)
    group = rows // parts
    got = lateral[pl.ds(pl.multiple_of(base % group, SUB), SUB), :]
    sides = pltpu.roll(got, (2 * cols - 1 - base // group * (cols // parts)) % cols, 1)

    def layer(z):
        if z < 0:
            return ends_ref[part, 1, at, :]
        if z == cells:
            return ends_ref[part + 2, 0, at, :]
        ref, low = places[z]
        return ref[pl.ds(low + base, SUB), :]

    def step(z):
        ref, low = places[z]
        here = layer(z)
        upper = jnp.where(is_top, head[z : z + 1, :], ref[pl.ds(low + base - 1, SUB), :])
        lower = jnp.where(is_bottom, head[cells + z : cells + z + 1, :], ref[pl.ds(low + base + 1, SUB), :])
        edge = pltpu.roll(sides, (cols - 2 * z) % cols, 1) if z else sides
        grad_x = pltpu.roll(jnp.where(is_first, edge, here), cols - 1, 1) - pltpu.roll(
            jnp.where(is_last, edge, here), 1, 1
        )
        grad_y = lower - upper
        grad_z = layer(z + 1) - layer(z - 1)
        inverse = lax.rsqrt(grad_x * grad_x + grad_y * grad_y + grad_z * grad_z + 4.0)
        cell_ref[0, z] = grad_x * inverse
        cell_ref[1, z] = grad_y * inverse
        cell_ref[2, z] = grad_z * inverse
        half = 0.5 * (knots - 1)
        position = half + half * jnp.tanh(0.5 * here)
        coarse = (position + FINE) - FINE
        segment = jnp.minimum(jnp.floor(position), knots - 2.0)
        rest = position - coarse
        right = coarse - segment
        left = 1.0 - right
        zero = jnp.zeros_like(here)
        is_at = [segment == k for k in range(knots - 1)]
        tents = [jnp.where(is_at[0], left, zero)]
        tents += [jnp.where(is_at[k], left, jnp.where(is_at[k - 1], right, zero)) for k in range(1, knots - 1)]
        tents += [jnp.where(is_at[knots - 2], right, zero)]
        rests = [jnp.where(is_at[k], rest, zero) for k in range(knots - 1)] + [zero]
        return [jnp.concatenate(part, axis=0).astype(jnp.bfloat16) for part in (tents, rests)]

    def two(first, second):
        tents, rests = [jnp.concatenate(both, axis=1) for both in zip(step(first), step(second))]
        right = jnp.concatenate([tents, rests, tents], axis=0)
        mixed = jnp.dot(weight_ref[...], right, preferred_element_type=jnp.float32)
        mixed_ref[first] = mixed[:, :cols]
        mixed_ref[second] = mixed[:, cols:]

    knots = weight_ref.shape[1] // (3 * SUB)
    zs = list(zs)
    return [functools.partial(two, *zs[i : i + 2]) for i in range(0, len(zs), 2)]


def march_unit(flip, vector_ref, zs, cells, cell_ref, mixed_ref, beside, inner=None):
    passes = vector_ref.shape[0]
    channels = mixed_ref.shape[1] // (passes * SUB)
    shape = vector_ref.shape[2:]
    vectors = [[vector_ref[p, axis] for axis in range(3)] for p in range(passes)]
    state = [(jnp.ones(shape, jnp.float32), [jnp.zeros(shape, jnp.float32)] * 3)] * passes
    count = len(beside)
    for u, spot in enumerate(zs):
        for step in beside[u * count // len(zs) : (u + 1) * count // len(zs)]:
            step()
        z = spot + flip * (cells - 1 - 2 * spot)
        normal = [cell_ref[axis, z] for axis in range(3)]
        for p in range(passes):
            keep, sums = state[p]
            mixed = [mixed_ref[z, (p * channels + c) * SUB : (p * channels + c + 1) * SUB, :] for c in range(channels)]
            facing = normal[0] * vectors[p][0] + normal[1] * vectors[p][1] + normal[2] * vectors[p][2]
            taken = keep * mixed[3]
            weight = taken * (AMBIENT + jnp.abs(facing))
            sums = [total + weight * tint for total, tint in zip(sums, mixed)]
            keep = keep - taken
            if inner is not None and u == 0:
                keep, sums = keep * inner(p, 0), [total + keep * inner(p, j + 1) for j, total in enumerate(sums)]
            state[p] = (keep, sums)
    return [[keep] + sums for keep, sums in state]


def own_kernel(parts, index_ref, flip_ref, lights_ref, curves_ref, own_ref, lateral_ref, out_ref, vector_ref, weight_ref, *refs):
    cell_refs, mixed_refs = refs[:2], refs[2:]
    rows, cols = out_ref.shape[1:]
    channels = curves_ref.shape[1]
    passes = index_ref.shape[0]
    cells = cell_refs[0].shape[1]
    flip = flip_ref[0]
    tiles = rows // SUB
    inner = range(1, cells - 1)
    for p in range(passes):
        for axis in range(3):
            vector_ref[p, axis] = jnp.full((SUB, cols), lights_ref[index_ref[p], axis])
    fill_weights(index_ref, curves_ref, OPACITY / (parts * cells), weight_ref)
    places = near_places(cells, rows, own_ref)

    def prepare(base, slot):
        return prepare_steps(
            0, inner, own_ref, places, lateral_ref, base, cells, rows, parts, cols, None, weight_ref, cell_refs[slot], mixed_refs[slot]
        )

    for step in prepare(0, 0):
        step()

    def pair(i, carry):
        for slot in range(2):
            base = pl.multiple_of((2 * i + slot) * SUB, SUB)
            after = pl.multiple_of(jnp.minimum(2 * i + slot + 1, tiles - 1) * SUB, SUB)
            result = march_unit(flip, vector_ref, inner, cells, cell_refs[slot], mixed_refs[slot], prepare(after, 1 - slot))
            for p in range(passes):
                for j in range(channels):
                    out_ref[p * channels + j, pl.ds(base, SUB), :] = result[p][j]
        return carry

    lax.fori_loop(0, tiles // 2, pair, 0)


def near_kernel(parts, flip_ref, vector_ref, weight_ref, inner_ref, *refs):
    count = parts - 1
    heads, laterals, out_ref, ends_ref = refs[:parts], refs[parts : 2 * parts - 1], refs[2 * parts - 1], refs[2 * parts]
    cell_refs, mixed_refs = refs[2 * parts + 1 : 2 * parts + 1 + count], refs[2 * parts + 1 + count :]
    rows, cols = out_ref.shape[2:]
    cells = cell_refs[0].shape[1]
    passes = vector_ref.shape[0]
    channels = inner_ref.shape[0] // passes
    flip = flip_ref[0]
    tiles = rows // SUB
    zs = [(0, cells - 1)] + [range(cells)] * (count - 1)
    places = [near_places(cells, rows, head) for head in heads[:count]]
    fill_ends(parts, cells, rows, heads, ends_ref)

    def prepare(m, base):
        return prepare_steps(
            m, zs[m], heads[m], places[m], laterals[m], base, cells, rows, parts, cols, ends_ref, weight_ref, cell_refs[m], mixed_refs[m]
        )

    for step in prepare(0, 0):
        step()

    def tile(i, carry):
        base = pl.multiple_of(i * SUB, SUB)
        after = pl.multiple_of(jnp.minimum(i + 1, tiles - 1) * SUB, SUB)
        at = pl.ds(base, SUB)
        for m in range(count):
            beside = prepare(m + 1, base) if m + 1 < count else prepare(0, after)
            inner = (lambda p, j: inner_ref[p * channels + j, at, :]) if m == 0 else None
            result = march_unit(flip, vector_ref, zs[m], cells, cell_refs[m], mixed_refs[m], beside, inner)
            for p in range(passes):
                for j in range(channels):
                    out_ref[m, p * channels + j, at, :] = result[p][j]
        return carry

    lax.fori_loop(0, tiles, tile, 0)


def over_either(first_leads, one, other):
    shape = one[0].shape
    unit = jnp.ones(shape, jnp.float32)
    scale_one = jnp.where(first_leads, unit, other[0])
    scale_other = jnp.where(first_leads, one[0], unit)
    return [one[0] * other[0]] + [scale_one * a + scale_other * b for a, b in zip(one[1:], other[1:])]


def far_kernel(parts, flip_ref, vector_ref, weight_ref, *refs):
    heads, body, states, out_ref, picture_ref, ends_ref, sems = refs[:parts], *refs[parts : parts + 6]
    cell_refs, mixed_refs = refs[parts + 6 : parts + 8], refs[parts + 8 :]
    channels, rows, cols = out_ref.shape[1:]
    cells = cell_refs[0].shape[1]
    passes = vector_ref.shape[0]
    flip = flip_ref[0]
    me = lax.axis_index("depth")
    places = far_places(cells, rows, parts, heads[-1], body)
    fill_ends(parts, cells, rows, heads, ends_ref)
    tiles = rows // SUB

    def prepare(base, slot):
        return prepare_steps(
            parts - 1, range(cells), heads[-1], places, body, base, cells, rows, parts, cols, ends_ref, weight_ref, cell_refs[slot], mixed_refs[slot]
        )

    def send(index):
        at = pl.ds(pl.multiple_of(index * SUB, SUB), SUB)
        return pltpu.make_async_copy(picture_ref.at[:, :, at, :], out_ref.at[:, :, at, :], sems.at[index])

    def finish(result, index):
        at = pl.ds(pl.multiple_of(index * SUB, SUB), SUB)
        for p in range(passes):
            images = [[states[m, p * channels + j, at, :] for j in range(channels)] for m in range(parts - 1)]
            images.append(result[p])
            bit = 0
            while len(images) > 1:
                leads = ((me >> bit) & 1) == flip
                images = [over_either(leads, images[j], images[j + 1]) for j in range(0, len(images), 2)]
                bit += 1
            for channel in range(3):
                picture_ref[p, channel, at, :] = images[0][channel + 1]
            picture_ref[p, 3, at, :] = 1.0 - images[0][0]
        send(index).start()

    for step in prepare(0, 0):
        step()

    def pair(i, carry):
        for slot in range(2):
            index = 2 * i + slot
            after = pl.multiple_of(jnp.minimum(index + 1, tiles - 1) * SUB, SUB)
            result = march_unit(flip, vector_ref, range(cells), cells, cell_refs[slot], mixed_refs[slot], prepare(after, 1 - slot))
            finish(result, index)
        return carry

    lax.fori_loop(0, tiles // 2, pair, 0)
    for index in range(tiles):
        send(index).wait()


def shift_along(block, axis, amount):
    count = lax.axis_size(axis)
    route = [(i, i + amount) for i in range(count) if 0 <= i + amount < count]
    return lax.ppermute(block, axis, route)


def swap_along(block, axis, mask):
    return lax.ppermute(block, axis, [(i, i ^ mask) for i in range(lax.axis_size(axis))])


def estimate(micros):
    return pl.CostEstimate(flops=int(micros * 1_000_000_000), transcendentals=0, bytes_accessed=0)


def on_device(field, light_vectors, transfer, light_index, flips):
    parts = lax.axis_size("depth")
    cells, all_rows, cols = field.shape
    rows = all_rows // parts
    passes = light_index.shape[0]
    channels, knots = transfer.shape[1:]
    tiles = rows // SUB
    values = passes * channels
    in_vmem = pl.BlockSpec(memory_space=VMEM)
    in_smem = pl.BlockSpec(memory_space=SMEM)
    in_any = pl.BlockSpec(memory_space=pl.ANY)
    in_hbm = pl.BlockSpec(memory_space=pltpu.HBM)

    def array(*shape):
        return jax.ShapeDtypeStruct(shape, jnp.float32)

    def settings(mib, micros):
        return dict(
            compiler_params=pltpu.CompilerParams(vmem_limit_bytes=mib * MIB),
            cost_estimate=pl.CostEstimate(flops=int(micros * 1e9), transcendentals=0, bytes_accessed=0),
        )

    near_rows = 2 * cells + cells * rows + SUB
    head_rows = 2 * cells + 2 * rows + SUB
    skip = rows // parts
    body_rows = skip + (cells - 2) * rows + SUB
    *packed, far_head = pl.pallas_call(
        functools.partial(pack_kernel, parts),
        out_shape=[array(near_rows, cols)] * (parts - 2) + [array(head_rows, cols)],
        in_specs=[in_hbm],
        out_specs=[in_vmem] * (parts - 1),
        scratch_shapes=[VMEM((parts - 1, 2, cells, SUB, cols), jnp.float32), pltpu.SemaphoreType.DMA((4, parts - 1))],
        name="pack",
        **settings(8, 1),
    )(field)
    near = [swap_along(packed[m - 1], "depth", m) for m in range(1, parts - 1)]

    far_head = swap_along(far_head, "depth", parts - 1)

    edges, own, far_body = pl.pallas_call(
        functools.partial(edge_kernel, parts),
        out_shape=[array(rows, cols), array(near_rows, cols), array(body_rows, cols)],
        in_specs=[in_vmem, in_any],
        out_specs=[in_vmem] * 3,
        name="edges",
        **settings(8, 1),
    )(field, packed[0])
    sides = pl.pallas_call(
        functools.partial(side_kernel, parts),
        out_shape=[array(skip, cols)] * parts,
        in_specs=[in_vmem] * 2 + [in_any],
        out_specs=[in_vmem] * parts,
        name="sides",
        **settings(4, 0.1),
    )(shift_along(edges, "tile", 1), shift_along(edges, "tile", -1), far_head)
    laterals = [swap_along(sides[m], "depth", m) for m in range(1, parts - 1)]
    far_body = swap_along(lax.dynamic_update_slice(far_body, sides[-1], (0, 0)), "depth", parts - 1)

    cell_shape = VMEM((3, cells, SUB, cols), jnp.float32)
    mixed_shape = VMEM((cells, values * SUB, cols), jnp.float32)
    ends_shape = VMEM((parts + 2, 2, rows, cols), jnp.float32)
    weight_shape = jax.ShapeDtypeStruct((values * SUB, 3 * knots * SUB), jnp.bfloat16)
    inner, vectors, weights = pl.pallas_call(
        functools.partial(own_kernel, parts),
        out_shape=[array(values, rows, cols), array(passes, 3, SUB, cols), weight_shape],
        in_specs=[in_smem] * 4 + [in_vmem] * 2,
        out_specs=[in_vmem] * 3,
        scratch_shapes=[cell_shape] * 2 + [mixed_shape] * 2,
        name="own",
        **settings(12, 4),
    )(light_index, flips, light_vectors, transfer, own, sides[0])
    states = pl.pallas_call(
        functools.partial(near_kernel, parts),
        out_shape=array(parts - 1, values, rows, cols),
        in_specs=[in_smem] + [in_vmem] * (2 * parts + 2),
        out_specs=in_vmem,
        scratch_shapes=[ends_shape] + [cell_shape] * (parts - 1) + [mixed_shape] * (parts - 1),
        name="near",
        **settings(16, 60),
    )(flips, vectors, weights, inner, own, *near, far_head, sides[0], *laterals)
    return pl.pallas_call(
        functools.partial(far_kernel, parts),
        out_shape=array(passes, channels, rows, cols),
        in_specs=[in_smem] + [in_vmem] * (parts + 4),
        out_specs=in_any,
        scratch_shapes=[
            VMEM((passes, channels, rows, cols), jnp.float32),
            ends_shape,
            pltpu.SemaphoreType.DMA((tiles,)),
        ]
        + [cell_shape] * 2
        + [mixed_shape] * 2,
        name="far",
        **settings(16, 5),
    )(flips, vectors, weights, own, *near, far_head, far_body, states)


def solution(mesh):
    in_specs = (P("depth", None, "tile"), P(), P(), P(), P("tile"))
    out_specs = P(None, None, "depth", "tile")
    return jax.shard_map(
        on_device, mesh=mesh, in_specs=in_specs, out_specs=out_specs, check_vma=False
    )
```

```python
import functools

import jax
import jax.numpy as jnp
from jax import lax
from jax.experimental import pallas as pl
from jax.experimental.pallas import tpu as pltpu
from jax.sharding import PartitionSpec as P

AMBIENT = 0.3
OPACITY = 2.0
SUB = 8
VMEM = pltpu.VMEM
SMEM = pltpu.SMEM
MIB = 1 << 20
FINE = 49152.0


def pack_kernel(parts, field_ref, *refs):
    outs, (rim_ref, sems) = refs[: parts - 1], refs[parts - 1 :]
    cells, all_rows, cols = field_ref.shape
    rows = all_rows // parts
    me = lax.axis_index("depth")
    copies, rims = [], []
    for j, out in enumerate(outs):
        low = pl.multiple_of((me ^ (j + 1)) * rows, SUB)
        before = pl.multiple_of(jnp.maximum(low - SUB, 0), SUB)
        after = pl.multiple_of(jnp.minimum(low + rows, all_rows - SUB), SUB)
        for side, start in enumerate((before, after)):
            source = field_ref.at[:, pl.ds(start, SUB), :]
            rims.append(pltpu.make_async_copy(source, rim_ref.at[j, side], sems.at[side, j]))
        block = field_ref.at[:, pl.ds(low, rows), :]
        if j < parts - 2:
            centre = out.at[pl.ds(2 * cells, cells * rows), :].reshape(cells, rows, cols)
            copies.append(pltpu.make_async_copy(block, centre, sems.at[2, j]))
        else:
            for side in range(2):
                layer = out.at[pl.ds(2 * cells + side * rows, rows), :]
                copies.append(pltpu.make_async_copy(block.at[side * (cells - 1)], layer, sems.at[2 + side, j]))
    for copy in rims + copies:
        copy.start()
    for copy in rims:
        copy.wait()
    for j, out in enumerate(outs):
        part = me ^ (j + 1)
        above = jnp.where(part > 0, 1.0, 0.0)
        below = jnp.where(part < parts - 1, 1.0, 0.0)
        for z in range(cells):
            out[z : z + 1, :] = rim_ref[j, 0, z, SUB - 1 : SUB, :] * above
            out[cells + z : cells + z + 1, :] = rim_ref[j, 1, z, 0:1, :] * below
    for copy in copies:
        copy.wait()


def edge_kernel(parts, split, field_ref, _, edge_ref, own_ref, body_ref, rest_ref):
    cells, all_rows, cols = field_ref.shape
    rows = all_rows // parts
    me = lax.axis_index("depth")
    lane_pair = lax.broadcasted_iota(jnp.int32, (SUB, cols), 1) // 2

    def tile(i, carry):
        acc = jnp.zeros((SUB, cols), jnp.float32)
        for part in range(parts):
            for z in range(cells):
                slot = part * cells + z
                start = pl.multiple_of(part * rows + i * SUB, SUB)
                value = field_ref[z, pl.ds(start, SUB), :]
                moved = pltpu.roll(value, (2 * slot + 1) % cols, 1)
                acc = jnp.where(lane_pair == slot, moved, acc)
        edge_ref[pl.ds(pl.multiple_of(i * SUB, SUB), SUB), :] = acc
        return carry

    lax.fori_loop(0, rows // SUB, tile, 0)
    low = pl.multiple_of(me * rows, SUB)
    above = jnp.where(me > 0, 1.0, 0.0)
    below = jnp.where(me < parts - 1, 1.0, 0.0)
    for z in range(cells):
        own_ref[z : z + 1, :] = field_ref[z, pl.ds(jnp.maximum(low - 1, 0), 1), :] * above
        own_ref[cells + z : cells + z + 1, :] = field_ref[z, pl.ds(jnp.minimum(low + rows, all_rows - 1), 1), :] * below
    far_low = pl.multiple_of((me ^ (parts - 1)) * rows, SUB)
    own_places, _, _ = near_places(cells, rows, own_ref)
    for z in range(cells):
        ref, start = own_places[z]
        ref[start : start + rows, :] = field_ref[z, pl.ds(low, rows), :]
    skip, more = rows // parts, rows - split
    for z in range(1, cells - 1):
        at = skip + (z - 1) * split
        body_ref[at : at + split, :] = field_ref[z, pl.ds(far_low, split), :]
        next_row = skip + (cells - 2) * split + z - 1
        body_ref[next_row : next_row + 1, :] = field_ref[z, pl.ds(far_low + split, 1), :]
        at = SUB + (z - 1) * more
        rest_ref[at : at + more, :] = field_ref[z, pl.ds(far_low + split, more), :]


def side_kernel(parts, left_ref, right_ref, _, *outs):
    rows, cols = left_ref.shape
    group = rows // parts
    width = cols // parts
    me = lax.axis_index("depth")
    lane = lax.broadcasted_iota(jnp.int32, (rows, cols), 1)
    sides = jnp.where(lane % 2 == 0, left_ref[...], right_ref[...])
    for m in range(parts):
        acc = jnp.zeros((group, cols), jnp.float32)
        for j in range(parts):
            moved = pltpu.roll(sides[j * group : (j + 1) * group], (j - (me ^ m) + parts) * width % cols, 1)
            acc = jnp.where(lane[:group] // width == j, moved, acc)
        outs[m][...] = acc


def near_places(cells, rows, head):
    places = [(head, 2 * cells + z * rows) for z in range(cells)]
    tops = [(0, head, z) for z in range(cells)]
    bottoms = [(rows - SUB, head, cells + z) for z in range(cells)]
    return places, tops, bottoms


def far_places(cells, rows, parts, split, head, body, rest=None):
    skip, more = rows // parts, rows - split
    places, tops, bottoms = near_places(cells, rows, head)
    places[0], places[-1] = (head, 2 * cells), (head, 2 * cells + rows)
    for z in range(1, cells - 1):
        if rest is None:
            places[z] = (body, skip + (z - 1) * split)
            bottoms[z] = (split - SUB, body, skip + (cells - 2) * split + z - 1)
        else:
            places[z] = (rest, SUB + (z - 1) * more - split)
            tops[z] = (split, body, skip + z * split - 1)
    return places, tops, bottoms


def fill_ends(parts, cells, rows, heads, ends_ref):
    me = lax.axis_index("depth")
    ends_ref[0, 1] = jnp.zeros_like(ends_ref[0, 1])
    ends_ref[parts + 1, 0] = jnp.zeros_like(ends_ref[0, 0])
    for m in range(parts):
        last = (cells - 1) * rows if m < parts - 1 else rows
        ends_ref[(me ^ m) + 1, 0] = heads[m][2 * cells : 2 * cells + rows, :]
        ends_ref[(me ^ m) + 1, 1] = heads[m][2 * cells + last : 2 * cells + last + rows, :]


def fill_weights(index_ref, curves_ref, scale, weight_ref):
    passes = index_ref.shape[0]
    channels, knots = curves_ref.shape[1:]
    shape = (2 * SUB, weight_ref.shape[1])
    row = lax.broadcasted_iota(jnp.int32, shape, 0)
    lane = lax.broadcasted_iota(jnp.int32, shape, 1)
    block = knots * SUB
    knot = lane // SUB
    on_row = lane % SUB == row % SUB
    zero = jnp.zeros(shape, jnp.float32)
    for pair in range(passes * channels // 2):
        halves = []
        for channel in (2 * pair, 2 * pair + 1):
            chosen = index_ref[channel // channels]
            factor = scale if channel % channels == channels - 1 else 1.0
            points = [curves_ref[chosen, channel % channels, k] * factor for k in range(knots)]
            half = zero
            for k in range(knots):
                half = jnp.where(jnp.logical_or(knot == k, knot == k + 2 * knots), points[k], half)
                if k + 1 < knots:
                    half = jnp.where(knot == k + knots, points[k + 1] - points[k], half)
            halves.append(half)
        value = jnp.where(on_row, jnp.where(row < SUB, halves[0], halves[1]), zero)
        coarse = value.astype(jnp.bfloat16).astype(jnp.float32)
        value = jnp.where(lane < 2 * block, value, value - coarse)
        weight_ref[2 * pair * SUB : 2 * (pair + 1) * SUB, :] = value.astype(jnp.bfloat16)


def prepare_steps(m, zs, where, lateral, base, cells, rows, parts, cols, ends_ref, weight_ref, cell_ref, mixed_ref):
    me = lax.axis_index("depth")
    part = me ^ m
    at = pl.ds(base, SUB)
    lane = lax.broadcasted_iota(jnp.int32, (SUB, cols), 1)
    sublane = lax.broadcasted_iota(jnp.int32, (SUB, cols), 0)
    is_first = lane == 0
    is_last = lane == cols - 1
    places, tops, bottoms = where
    group = rows // parts
    got = lateral[pl.ds(pl.multiple_of(base % group, SUB), SUB), :]
    sides = pltpu.roll(got, (2 * cols - 1 - base // group * (cols // parts)) % cols, 1)

    def layer(z):
        if z < 0:
            return ends_ref[part, 1, at, :]
        if z == cells:
            return ends_ref[part + 2, 0, at, :]
        ref, low = places[z]
        return ref[pl.ds(low + base, SUB), :]

    def step(z):
        ref, low = places[z]
        here = layer(z)
        top_at, top_ref, top = tops[z]
        bottom_at, bottom_ref, bottom = bottoms[z]
        is_top = jnp.logical_and(sublane == 0, base == top_at)
        is_bottom = jnp.logical_and(sublane == SUB - 1, base == bottom_at)
        upper = jnp.where(is_top, top_ref[top : top + 1, :], ref[pl.ds(low + base - 1, SUB), :])
        lower = jnp.where(is_bottom, bottom_ref[bottom : bottom + 1, :], ref[pl.ds(low + base + 1, SUB), :])
        edge = pltpu.roll(sides, (cols - 2 * z) % cols, 1) if z else sides
        grad_x = pltpu.roll(jnp.where(is_first, edge, here), cols - 1, 1) - pltpu.roll(
            jnp.where(is_last, edge, here), 1, 1
        )
        grad_y = lower - upper
        grad_z = layer(z + 1) - layer(z - 1)
        inverse = lax.rsqrt(grad_x * grad_x + grad_y * grad_y + grad_z * grad_z + 4.0)
        cell_ref[0, z] = grad_x * inverse
        cell_ref[1, z] = grad_y * inverse
        cell_ref[2, z] = grad_z * inverse
        half = 0.5 * (knots - 1)
        position = half + half * jnp.tanh(0.5 * here)
        coarse = (position + FINE) - FINE
        segment = jnp.minimum(jnp.floor(position), knots - 2.0)
        rest = position - coarse
        right = coarse - segment
        left = 1.0 - right
        zero = jnp.zeros_like(here)
        is_at = [segment == k for k in range(knots - 1)]
        tents = [jnp.where(is_at[0], left, zero)]
        tents += [jnp.where(is_at[k], left, jnp.where(is_at[k - 1], right, zero)) for k in range(1, knots - 1)]
        tents += [jnp.where(is_at[knots - 2], right, zero)]
        rests = [jnp.where(is_at[k], rest, zero) for k in range(knots - 1)] + [zero]
        return [jnp.concatenate(part, axis=0).astype(jnp.bfloat16) for part in (tents, rests)]

    def two(first, second):
        tents, rests = [jnp.concatenate(both, axis=1) for both in zip(step(first), step(second))]
        right = jnp.concatenate([tents, rests, tents], axis=0)
        mixed = jnp.dot(weight_ref[...], right, preferred_element_type=jnp.float32)
        mixed_ref[first] = mixed[:, :cols]
        mixed_ref[second] = mixed[:, cols:]

    knots = weight_ref.shape[1] // (3 * SUB)
    zs = list(zs)
    return [functools.partial(two, *zs[i : i + 2]) for i in range(0, len(zs), 2)]


def march_unit(flip, vector_ref, zs, cells, cell_ref, mixed_ref, beside, inner=None):
    passes = vector_ref.shape[0]
    channels = mixed_ref.shape[1] // (passes * SUB)
    shape = vector_ref.shape[2:]
    vectors = [[vector_ref[p, axis] for axis in range(3)] for p in range(passes)]
    state = [(jnp.ones(shape, jnp.float32), [jnp.zeros(shape, jnp.float32)] * 3)] * passes
    count = len(beside)
    for u, spot in enumerate(zs):
        for step in beside[u * count // len(zs) : (u + 1) * count // len(zs)]:
            step()
        z = spot + flip * (cells - 1 - 2 * spot)
        normal = [cell_ref[axis, z] for axis in range(3)]
        for p in range(passes):
            keep, sums = state[p]
            mixed = [mixed_ref[z, (p * channels + c) * SUB : (p * channels + c + 1) * SUB, :] for c in range(channels)]
            facing = normal[0] * vectors[p][0] + normal[1] * vectors[p][1] + normal[2] * vectors[p][2]
            taken = keep * mixed[3]
            weight = taken * (AMBIENT + jnp.abs(facing))
            sums = [total + weight * tint for total, tint in zip(sums, mixed)]
            keep = keep - taken
            if inner is not None and u == 0:
                keep, sums = keep * inner(p, 0), [total + keep * inner(p, j + 1) for j, total in enumerate(sums)]
            state[p] = (keep, sums)
    return [[keep] + sums for keep, sums in state]


def own_kernel(parts, index_ref, flip_ref, lights_ref, curves_ref, own_ref, lateral_ref, out_ref, vector_ref, weight_ref, *refs):
    cell_refs, mixed_refs = refs[:2], refs[2:]
    rows, cols = out_ref.shape[1:]
    channels = curves_ref.shape[1]
    passes = index_ref.shape[0]
    cells = cell_refs[0].shape[1]
    flip = flip_ref[0]
    tiles = rows // SUB
    inner = range(1, cells - 1)
    for p in range(passes):
        for axis in range(3):
            vector_ref[p, axis] = jnp.full((SUB, cols), lights_ref[index_ref[p], axis])
    fill_weights(index_ref, curves_ref, OPACITY / (parts * cells), weight_ref)
    places = near_places(cells, rows, own_ref)

    def prepare(base, slot):
        return prepare_steps(
            0, inner, places, lateral_ref, base, cells, rows, parts, cols, None, weight_ref, cell_refs[slot], mixed_refs[slot]
        )

    for step in prepare(0, 0):
        step()

    def pair(i, carry):
        for slot in range(2):
            base = pl.multiple_of((2 * i + slot) * SUB, SUB)
            after = pl.multiple_of(jnp.minimum(2 * i + slot + 1, tiles - 1) * SUB, SUB)
            result = march_unit(flip, vector_ref, inner, cells, cell_refs[slot], mixed_refs[slot], prepare(after, 1 - slot))
            for p in range(passes):
                for j in range(channels):
                    out_ref[p * channels + j, pl.ds(base, SUB), :] = result[p][j]
        return carry

    lax.fori_loop(0, tiles // 2, pair, 0)


def near_kernel(parts, flip_ref, vector_ref, weight_ref, inner_ref, *refs):
    count = parts - 1
    heads, laterals, out_ref, ends_ref = refs[:parts], refs[parts : 2 * parts - 1], refs[2 * parts - 1], refs[2 * parts]
    cell_refs, mixed_refs = refs[2 * parts + 1 : 2 * parts + 1 + count], refs[2 * parts + 1 + count :]
    rows, cols = out_ref.shape[2:]
    cells = cell_refs[0].shape[1]
    passes = vector_ref.shape[0]
    channels = inner_ref.shape[0] // passes
    flip = flip_ref[0]
    tiles = rows // SUB
    zs = [(0, cells - 1)] + [range(cells)] * (count - 1)
    places = [near_places(cells, rows, head) for head in heads[:count]]
    fill_ends(parts, cells, rows, heads, ends_ref)

    def prepare(m, base):
        return prepare_steps(
            m, zs[m], places[m], laterals[m], base, cells, rows, parts, cols, ends_ref, weight_ref, cell_refs[m], mixed_refs[m]
        )

    for step in prepare(0, 0):
        step()

    def tile(i, carry):
        base = pl.multiple_of(i * SUB, SUB)
        after = pl.multiple_of(jnp.minimum(i + 1, tiles - 1) * SUB, SUB)
        at = pl.ds(base, SUB)
        for m in range(count):
            beside = prepare(m + 1, base) if m + 1 < count else prepare(0, after)
            inner = (lambda p, j: inner_ref[p * channels + j, at, :]) if m == 0 else None
            result = march_unit(flip, vector_ref, zs[m], cells, cell_refs[m], mixed_refs[m], beside, inner)
            for p in range(passes):
                for j in range(channels):
                    out_ref[m, p * channels + j, at, :] = result[p][j]
        return carry

    lax.fori_loop(0, tiles, tile, 0)


def over_either(first_leads, one, other):
    shape = one[0].shape
    unit = jnp.ones(shape, jnp.float32)
    scale_one = jnp.where(first_leads, unit, other[0])
    scale_other = jnp.where(first_leads, one[0], unit)
    return [one[0] * other[0]] + [scale_one * a + scale_other * b for a, b in zip(one[1:], other[1:])]


def far_kernel(parts, split, low, high, flip_ref, vector_ref, weight_ref, *refs):
    heads, body, refs = refs[:parts], refs[parts], refs[parts + 1 :]
    rest, refs = (refs[0], refs[2:]) if low else (None, refs)
    states, out_ref, picture_ref, ends_ref, sems = refs[:5]
    cell_refs, mixed_refs = refs[5:7], refs[7:]
    channels, rows, cols = out_ref.shape[1:]
    cells = cell_refs[0].shape[1]
    passes = vector_ref.shape[0]
    flip = flip_ref[0]
    me = lax.axis_index("depth")
    places = far_places(cells, rows, parts, split, heads[-1], body, rest)
    fill_ends(parts, cells, rows, heads, ends_ref)
    tiles = range(low // SUB, high // SUB)

    def prepare(base, slot):
        return prepare_steps(
            parts - 1, range(cells), places, body, base, cells, rows, parts, cols, ends_ref, weight_ref, cell_refs[slot], mixed_refs[slot]
        )

    def send(index):
        at = pl.ds(pl.multiple_of(index * SUB, SUB), SUB)
        return pltpu.make_async_copy(picture_ref.at[:, :, at, :], out_ref.at[:, :, at, :], sems.at[index])

    def finish(result, index):
        at = pl.ds(pl.multiple_of(index * SUB, SUB), SUB)
        for p in range(passes):
            images = [[states[m, p * channels + j, at, :] for j in range(channels)] for m in range(parts - 1)]
            images.append(result[p])
            bit = 0
            while len(images) > 1:
                leads = ((me >> bit) & 1) == flip
                images = [over_either(leads, images[j], images[j + 1]) for j in range(0, len(images), 2)]
                bit += 1
            for channel in range(3):
                picture_ref[p, channel, at, :] = images[0][channel + 1]
            picture_ref[p, 3, at, :] = 1.0 - images[0][0]
        send(index).start()

    for step in prepare(low, 0):
        step()

    def pair(i, carry):
        for slot in range(2):
            index = tiles[0] + 2 * i + slot
            after = pl.multiple_of(jnp.minimum(index + 1, tiles[-1]) * SUB, SUB)
            result = march_unit(flip, vector_ref, range(cells), cells, cell_refs[slot], mixed_refs[slot], prepare(after, 1 - slot))
            finish(result, index)
        return carry

    lax.fori_loop(0, len(tiles) // 2, pair, 0)
    for index in tiles:
        send(index).wait()


def shift_along(block, axis, amount):
    count = lax.axis_size(axis)
    route = [(i, i + amount) for i in range(count) if 0 <= i + amount < count]
    return lax.ppermute(block, axis, route)


def swap_along(block, axis, mask):
    return lax.ppermute(block, axis, [(i, i ^ mask) for i in range(lax.axis_size(axis))])


def estimate(micros):
    return pl.CostEstimate(flops=int(micros * 1_000_000_000), transcendentals=0, bytes_accessed=0)


def on_device(field, light_vectors, transfer, light_index, flips):
    parts = lax.axis_size("depth")
    cells, all_rows, cols = field.shape
    rows = all_rows // parts
    passes = light_index.shape[0]
    channels, knots = transfer.shape[1:]
    tiles = rows // SUB
    values = passes * channels
    in_vmem = pl.BlockSpec(memory_space=VMEM)
    in_smem = pl.BlockSpec(memory_space=SMEM)
    in_any = pl.BlockSpec(memory_space=pl.ANY)
    in_hbm = pl.BlockSpec(memory_space=pltpu.HBM)

    def array(*shape):
        return jax.ShapeDtypeStruct(shape, jnp.float32)

    def settings(mib, micros):
        return dict(
            compiler_params=pltpu.CompilerParams(vmem_limit_bytes=mib * MIB),
            cost_estimate=pl.CostEstimate(flops=int(micros * 1e9), transcendentals=0, bytes_accessed=0),
        )

    near_rows = 2 * cells + cells * rows + SUB
    head_rows = 2 * cells + 2 * rows + SUB
    skip = rows // parts
    split = rows - rows // parts
    body_rows = skip + (cells - 2) * split + cells
    rest_rows = (cells - 2) * (rows - split) + 2 * SUB
    *packed, far_head = pl.pallas_call(
        functools.partial(pack_kernel, parts),
        out_shape=[array(near_rows, cols)] * (parts - 2) + [array(head_rows, cols)],
        in_specs=[in_hbm],
        out_specs=[in_vmem] * (parts - 1),
        scratch_shapes=[VMEM((parts - 1, 2, cells, SUB, cols), jnp.float32), pltpu.SemaphoreType.DMA((4, parts - 1))],
        name="pack",
        **settings(8, 1),
    )(pltpu.with_memory_space_constraint(field, pltpu.HBM))
    near = [swap_along(packed[m - 1], "depth", m) for m in range(1, parts - 1)]

    far_head = swap_along(far_head, "depth", parts - 1)

    edges, own, far_body, far_rest = pl.pallas_call(
        functools.partial(edge_kernel, parts, split),
        out_shape=[array(rows, cols), array(near_rows, cols), array(body_rows, cols), array(rest_rows, cols)],
        in_specs=[in_vmem, in_any],
        out_specs=[in_vmem] * 4,
        name="edges",
        **settings(8, 1),
    )(field, packed[0])
    sides = pl.pallas_call(
        functools.partial(side_kernel, parts),
        out_shape=[array(skip, cols)] * parts,
        in_specs=[in_vmem] * 2 + [in_any],
        out_specs=[in_vmem] * parts,
        name="sides",
        **settings(4, 0.1),
    )(shift_along(edges, "tile", 1), shift_along(edges, "tile", -1), far_head)
    laterals = [swap_along(sides[m], "depth", m) for m in range(1, parts - 1)]
    far_body = swap_along(lax.dynamic_update_slice(far_body, sides[-1], (0, 0)), "depth", parts - 1)
    *laterals, far_rest = lax.optimization_barrier((*laterals, far_rest))
    far_rest = swap_along(far_rest, "depth", parts - 1)

    cell_shape = VMEM((3, cells, SUB, cols), jnp.float32)
    mixed_shape = VMEM((cells, values * SUB, cols), jnp.float32)
    ends_shape = VMEM((parts + 2, 2, rows, cols), jnp.float32)
    weight_shape = jax.ShapeDtypeStruct((values * SUB, 3 * knots * SUB), jnp.bfloat16)
    inner, vectors, weights = pl.pallas_call(
        functools.partial(own_kernel, parts),
        out_shape=[array(values, rows, cols), array(passes, 3, SUB, cols), weight_shape],
        in_specs=[in_smem] * 4 + [in_vmem] * 2,
        out_specs=[in_vmem] * 3,
        scratch_shapes=[cell_shape] * 2 + [mixed_shape] * 2,
        name="own",
        **settings(12, 4),
    )(light_index, flips, light_vectors, transfer, own, sides[0])
    states = pl.pallas_call(
        functools.partial(near_kernel, parts),
        out_shape=array(parts - 1, values, rows, cols),
        in_specs=[in_smem] + [in_vmem] * (2 * parts + 2),
        out_specs=in_vmem,
        scratch_shapes=[ends_shape] + [cell_shape] * (parts - 1) + [mixed_shape] * (parts - 1),
        name="near",
        **settings(16, 60),
    )(flips, vectors, weights, inner, own, *near, far_head, sides[0], *laterals)
    picture = None
    for low, high in ((0, split), (split, rows)):
        late = [far_rest, picture] if low else []
        picture = pl.pallas_call(
            functools.partial(far_kernel, parts, split, low, high),
            out_shape=array(passes, channels, rows, cols),
            in_specs=[in_smem] + [in_vmem] * (parts + 3) + [in_vmem, in_any][: len(late)] + [in_vmem],
            out_specs=in_any,
            scratch_shapes=[
                VMEM((passes, channels, rows, cols), jnp.float32),
                ends_shape,
                pltpu.SemaphoreType.DMA((tiles,)),
            ]
            + [cell_shape] * 2
            + [mixed_shape] * 2,
            input_output_aliases={parts + 5: 0} if low else {},
            name="late" if low else "far",
            **settings(16, 2),
        )(flips, vectors, weights, own, *near, far_head, far_body, *late, states)
    return picture


def solution(mesh):
    in_specs = (P("depth", None, "tile"), P(), P(), P(), P("tile"))
    out_specs = P(None, None, "depth", "tile")
    return jax.shard_map(
        on_device, mesh=mesh, in_specs=in_specs, out_specs=out_specs, check_vma=False
    )
```

```python
import functools

import jax
import jax.numpy as jnp
from jax import lax
from jax.experimental import pallas as pl
from jax.experimental.pallas import tpu as pltpu
from jax.sharding import PartitionSpec as P

AMBIENT = 0.3
OPACITY = 2.0
SUB = 8
VMEM = pltpu.VMEM
SMEM = pltpu.SMEM
MIB = 1 << 20
FINE = 49152.0


def pack_kernel(parts, field_ref, *refs):
    outs, (rim_ref, sems) = refs[: parts - 1], refs[parts - 1 :]
    cells, all_rows, cols = field_ref.shape
    rows = all_rows // parts
    me = lax.axis_index("depth")
    copies, rims = [], []
    for j, out in enumerate(outs):
        low = pl.multiple_of((me ^ (j + 1)) * rows, SUB)
        before = pl.multiple_of(jnp.maximum(low - SUB, 0), SUB)
        after = pl.multiple_of(jnp.minimum(low + rows, all_rows - SUB), SUB)
        for side, start in enumerate((before, after)):
            source = field_ref.at[:, pl.ds(start, SUB), :]
            rims.append(pltpu.make_async_copy(source, rim_ref.at[j, side], sems.at[side, j]))
        block = field_ref.at[:, pl.ds(low, rows), :]
        if j < parts - 2:
            centre = out.at[pl.ds(2 * cells, cells * rows), :].reshape(cells, rows, cols)
            copies.append(pltpu.make_async_copy(block, centre, sems.at[2, j]))
        else:
            for side in range(2):
                layer = out.at[pl.ds(2 * cells + side * rows, rows), :]
                copies.append(pltpu.make_async_copy(block.at[side * (cells - 1)], layer, sems.at[2 + side, j]))
    for copy in rims + copies:
        copy.start()
    for copy in rims:
        copy.wait()
    for j, out in enumerate(outs):
        part = me ^ (j + 1)
        above = jnp.where(part > 0, 1.0, 0.0)
        below = jnp.where(part < parts - 1, 1.0, 0.0)
        for z in range(cells):
            out[z : z + 1, :] = rim_ref[j, 0, z, SUB - 1 : SUB, :] * above
            out[cells + z : cells + z + 1, :] = rim_ref[j, 1, z, 0:1, :] * below
    for copy in copies:
        copy.wait()


def edge_kernel(parts, split, field_ref, _, edge_ref, own_ref, body_ref, rest_ref):
    cells, all_rows, cols = field_ref.shape
    rows = all_rows // parts
    me = lax.axis_index("depth")
    lane_pair = lax.broadcasted_iota(jnp.int32, (SUB, cols), 1) // 2

    def tile(i, carry):
        acc = jnp.zeros((SUB, cols), jnp.float32)
        for part in range(parts):
            for z in range(cells):
                slot = part * cells + z
                start = pl.multiple_of(part * rows + i * SUB, SUB)
                value = field_ref[z, pl.ds(start, SUB), :]
                moved = pltpu.roll(value, (2 * slot + 1) % cols, 1)
                acc = jnp.where(lane_pair == slot, moved, acc)
        edge_ref[pl.ds(pl.multiple_of(i * SUB, SUB), SUB), :] = acc
        return carry

    lax.fori_loop(0, rows // SUB, tile, 0)
    low = pl.multiple_of(me * rows, SUB)
    above = jnp.where(me > 0, 1.0, 0.0)
    below = jnp.where(me < parts - 1, 1.0, 0.0)
    for z in range(cells):
        own_ref[z : z + 1, :] = field_ref[z, pl.ds(jnp.maximum(low - 1, 0), 1), :] * above
        own_ref[cells + z : cells + z + 1, :] = field_ref[z, pl.ds(jnp.minimum(low + rows, all_rows - 1), 1), :] * below
    far_low = pl.multiple_of((me ^ (parts - 1)) * rows, SUB)
    own_places, _, _ = near_places(cells, rows, own_ref)
    for z in range(cells):
        ref, start = own_places[z]
        ref[start : start + rows, :] = field_ref[z, pl.ds(low, rows), :]
    skip, more = rows // parts, rows - split
    for z in range(1, cells - 1):
        at = skip + (z - 1) * split
        body_ref[at : at + split, :] = field_ref[z, pl.ds(far_low, split), :]
        next_row = skip + (cells - 2) * split + z - 1
        body_ref[next_row : next_row + 1, :] = field_ref[z, pl.ds(far_low + split, 1), :]
        at = SUB + (z - 1) * more
        rest_ref[at : at + more, :] = field_ref[z, pl.ds(far_low + split, more), :]


def side_kernel(parts, even_ref, odd_ref, _, *outs):
    rows, cols = even_ref.shape
    group = rows // parts
    width = cols // parts
    me = lax.axis_index("depth")
    lane = lax.broadcasted_iota(jnp.int32, (rows, cols), 1)
    tile = lax.axis_index("tile")
    sides = jnp.where((lane + tile) % 2 == 1, even_ref[...], odd_ref[...])
    for m in range(parts):
        acc = jnp.zeros((group, cols), jnp.float32)
        for j in range(parts):
            moved = pltpu.roll(sides[j * group : (j + 1) * group], (j - (me ^ m) + parts) * width % cols, 1)
            acc = jnp.where(lane[:group] // width == j, moved, acc)
        outs[m][...] = acc


def near_places(cells, rows, head):
    places = [(head, 2 * cells + z * rows) for z in range(cells)]
    tops = [(0, head, z) for z in range(cells)]
    bottoms = [(rows - SUB, head, cells + z) for z in range(cells)]
    return places, tops, bottoms


def far_places(cells, rows, parts, split, head, body, rest=None):
    skip, more = rows // parts, rows - split
    places, tops, bottoms = near_places(cells, rows, head)
    places[0], places[-1] = (head, 2 * cells), (head, 2 * cells + rows)
    for z in range(1, cells - 1):
        if rest is None:
            places[z] = (body, skip + (z - 1) * split)
            bottoms[z] = (split - SUB, body, skip + (cells - 2) * split + z - 1)
        else:
            places[z] = (rest, SUB + (z - 1) * more - split)
            tops[z] = (split, body, skip + z * split - 1)
    return places, tops, bottoms


def fill_ends(parts, cells, rows, heads, ends_ref):
    me = lax.axis_index("depth")
    ends_ref[0, 1] = jnp.zeros_like(ends_ref[0, 1])
    ends_ref[parts + 1, 0] = jnp.zeros_like(ends_ref[0, 0])
    for m in range(parts):
        last = (cells - 1) * rows if m < parts - 1 else rows
        ends_ref[(me ^ m) + 1, 0] = heads[m][2 * cells : 2 * cells + rows, :]
        ends_ref[(me ^ m) + 1, 1] = heads[m][2 * cells + last : 2 * cells + last + rows, :]


def fill_weights(index_ref, curves_ref, scale, weight_ref):
    passes = index_ref.shape[0]
    channels, knots = curves_ref.shape[1:]
    width = weight_ref.shape[1]
    block = knots * SUB
    points = jnp.concatenate([curves_ref[index_ref[p]] for p in range(passes)], axis=0)
    channel = lax.broadcasted_iota(jnp.int32, points.shape, 0) % channels
    points = jnp.where(channel == channels - 1, points * scale, points)
    knot = lax.broadcasted_iota(jnp.int32, (knots, width), 0)
    lane = lax.broadcasted_iota(jnp.int32, (knots, width), 1)
    target = lane // SUB % knots
    here = jnp.where(knot == target, 1.0, 0.0)
    after = jnp.where(knot == target + 1, 1.0, 0.0)
    is_slope = jnp.logical_and(lane >= block, lane < 2 * block)
    spread = jnp.where(is_slope, after - here, here)
    values = jnp.dot(points, spread, precision=lax.Precision.HIGHEST, preferred_element_type=jnp.float32)
    shape = (2 * SUB, width)
    row = lax.broadcasted_iota(jnp.int32, shape, 0)
    lane = lax.broadcasted_iota(jnp.int32, shape, 1)
    on_row = lane % SUB == row % SUB
    for pair in range(passes * channels // 2):
        upper, lower = [jnp.broadcast_to(values[2 * pair + j : 2 * pair + j + 1], shape) for j in range(2)]
        value = jnp.where(on_row, jnp.where(row < SUB, upper, lower), 0.0)
        coarse = value.astype(jnp.bfloat16).astype(jnp.float32)
        value = jnp.where(lane < 2 * block, value, value - coarse)
        weight_ref[2 * pair * SUB : 2 * (pair + 1) * SUB, :] = value.astype(jnp.bfloat16)


def prepare_steps(m, zs, where, lateral, base, cells, rows, parts, cols, ends_ref, weight_ref, cell_ref, mixed_ref):
    me = lax.axis_index("depth")
    part = me ^ m
    at = pl.ds(base, SUB)
    lane = lax.broadcasted_iota(jnp.int32, (SUB, cols), 1)
    sublane = lax.broadcasted_iota(jnp.int32, (SUB, cols), 0)
    is_first = lane == 0
    is_last = lane == cols - 1
    places, tops, bottoms = where
    group = rows // parts
    got = lateral[pl.ds(pl.multiple_of(base % group, SUB), SUB), :]
    sides = pltpu.roll(got, (2 * cols - 1 - base // group * (cols // parts)) % cols, 1)

    def layer(z):
        if z < 0:
            return ends_ref[part, 1, at, :]
        if z == cells:
            return ends_ref[part + 2, 0, at, :]
        ref, low = places[z]
        return ref[pl.ds(low + base, SUB), :]

    def step(z):
        ref, low = places[z]
        here = layer(z)
        top_at, top_ref, top = tops[z]
        bottom_at, bottom_ref, bottom = bottoms[z]
        is_top = jnp.logical_and(sublane == 0, base == top_at)
        is_bottom = jnp.logical_and(sublane == SUB - 1, base == bottom_at)
        upper = jnp.where(is_top, top_ref[top : top + 1, :], ref[pl.ds(low + base - 1, SUB), :])
        lower = jnp.where(is_bottom, bottom_ref[bottom : bottom + 1, :], ref[pl.ds(low + base + 1, SUB), :])
        edge = pltpu.roll(sides, (cols - 2 * z) % cols, 1) if z else sides
        grad_x = pltpu.roll(jnp.where(is_first, edge, here), cols - 1, 1) - pltpu.roll(
            jnp.where(is_last, edge, here), 1, 1
        )
        grad_y = lower - upper
        grad_z = layer(z + 1) - layer(z - 1)
        inverse = lax.rsqrt(grad_x * grad_x + grad_y * grad_y + grad_z * grad_z + 4.0)
        cell_ref[0, z] = grad_x * inverse
        cell_ref[1, z] = grad_y * inverse
        cell_ref[2, z] = grad_z * inverse
        half = 0.5 * (knots - 1)
        position = half + half * jnp.tanh(0.5 * here)
        coarse = (position + FINE) - FINE
        segment = jnp.minimum(jnp.floor(position), knots - 2.0)
        rest = position - coarse
        right = coarse - segment
        left = 1.0 - right
        zero = jnp.zeros_like(here)
        is_at = [segment == k for k in range(knots - 1)]
        tents = [jnp.where(is_at[0], left, zero)]
        tents += [jnp.where(is_at[k], left, jnp.where(is_at[k - 1], right, zero)) for k in range(1, knots - 1)]
        tents += [jnp.where(is_at[knots - 2], right, zero)]
        rests = [jnp.where(is_at[k], rest, zero) for k in range(knots - 1)] + [zero]
        return [jnp.concatenate(part, axis=0).astype(jnp.bfloat16) for part in (tents, rests)]

    def two(first, second):
        tents, rests = [jnp.concatenate(both, axis=1) for both in zip(step(first), step(second))]
        right = jnp.concatenate([tents, rests, tents], axis=0)
        mixed = jnp.dot(weight_ref[...], right, preferred_element_type=jnp.float32)
        mixed_ref[first] = mixed[:, :cols]
        mixed_ref[second] = mixed[:, cols:]

    knots = weight_ref.shape[1] // (3 * SUB)
    zs = list(zs)
    return [functools.partial(two, *zs[i : i + 2]) for i in range(0, len(zs), 2)]


def march_unit(flip, vector_ref, zs, cells, cell_ref, mixed_ref, beside, inner=None):
    passes = vector_ref.shape[0]
    channels = mixed_ref.shape[1] // (passes * SUB)
    shape = vector_ref.shape[2:]
    vectors = [[vector_ref[p, axis] for axis in range(3)] for p in range(passes)]
    state = [(jnp.ones(shape, jnp.float32), [jnp.zeros(shape, jnp.float32)] * 3)] * passes
    count = len(beside)
    for u, spot in enumerate(zs):
        for step in beside[u * count // len(zs) : (u + 1) * count // len(zs)]:
            step()
        z = spot + flip * (cells - 1 - 2 * spot)
        normal = [cell_ref[axis, z] for axis in range(3)]
        for p in range(passes):
            keep, sums = state[p]
            mixed = [mixed_ref[z, (p * channels + c) * SUB : (p * channels + c + 1) * SUB, :] for c in range(channels)]
            facing = normal[0] * vectors[p][0] + normal[1] * vectors[p][1] + normal[2] * vectors[p][2]
            taken = keep * mixed[3]
            weight = taken * (AMBIENT + jnp.abs(facing))
            sums = [total + weight * tint for total, tint in zip(sums, mixed)]
            keep = keep - taken
            if inner is not None and u == 0:
                keep, sums = keep * inner(p, 0), [total + keep * inner(p, j + 1) for j, total in enumerate(sums)]
            state[p] = (keep, sums)
    return [[keep] + sums for keep, sums in state]


def own_kernel(parts, index_ref, flip_ref, lights_ref, curves_ref, own_ref, lateral_ref, out_ref, vector_ref, weight_ref, *refs):
    cell_refs, mixed_refs = refs[:2], refs[2:]
    rows, cols = out_ref.shape[1:]
    channels = curves_ref.shape[1]
    passes = index_ref.shape[0]
    cells = cell_refs[0].shape[1]
    flip = flip_ref[0]
    tiles = rows // SUB
    inner = range(1, cells - 1)
    for p in range(passes):
        for axis in range(3):
            vector_ref[p, axis] = jnp.full((SUB, cols), lights_ref[index_ref[p], axis])
    fill_weights(index_ref, curves_ref, OPACITY / (parts * cells), weight_ref)
    places = near_places(cells, rows, own_ref)

    def prepare(base, slot):
        return prepare_steps(
            0, inner, places, lateral_ref, base, cells, rows, parts, cols, None, weight_ref, cell_refs[slot], mixed_refs[slot]
        )

    for step in prepare(0, 0):
        step()

    def pair(i, carry):
        for slot in range(2):
            base = pl.multiple_of((2 * i + slot) * SUB, SUB)
            after = pl.multiple_of(jnp.minimum(2 * i + slot + 1, tiles - 1) * SUB, SUB)
            result = march_unit(flip, vector_ref, inner, cells, cell_refs[slot], mixed_refs[slot], prepare(after, 1 - slot))
            for p in range(passes):
                for j in range(channels):
                    out_ref[p * channels + j, pl.ds(base, SUB), :] = result[p][j]
        return carry

    lax.fori_loop(0, tiles // 2, pair, 0)


def near_kernel(parts, flip_ref, vector_ref, weight_ref, inner_ref, *refs):
    count = parts - 1
    heads, laterals, out_ref, ends_ref = refs[:parts], refs[parts : 2 * parts - 1], refs[2 * parts - 1], refs[2 * parts]
    cell_refs, mixed_refs = refs[2 * parts + 1 : 2 * parts + 1 + count], refs[2 * parts + 1 + count :]
    rows, cols = out_ref.shape[2:]
    cells = cell_refs[0].shape[1]
    passes = vector_ref.shape[0]
    channels = inner_ref.shape[0] // passes
    flip = flip_ref[0]
    tiles = rows // SUB
    zs = [(0, cells - 1)] + [range(cells)] * (count - 1)
    places = [near_places(cells, rows, head) for head in heads[:count]]
    fill_ends(parts, cells, rows, heads, ends_ref)

    def prepare(m, base):
        return prepare_steps(
            m, zs[m], places[m], laterals[m], base, cells, rows, parts, cols, ends_ref, weight_ref, cell_refs[m], mixed_refs[m]
        )

    for step in prepare(0, 0):
        step()

    def tile(i, carry):
        base = pl.multiple_of(i * SUB, SUB)
        after = pl.multiple_of(jnp.minimum(i + 1, tiles - 1) * SUB, SUB)
        at = pl.ds(base, SUB)
        for m in range(count):
            beside = prepare(m + 1, base) if m + 1 < count else prepare(0, after)
            inner = (lambda p, j: inner_ref[p * channels + j, at, :]) if m == 0 else None
            result = march_unit(flip, vector_ref, zs[m], cells, cell_refs[m], mixed_refs[m], beside, inner)
            for p in range(passes):
                for j in range(channels):
                    out_ref[m, p * channels + j, at, :] = result[p][j]
        return carry

    lax.fori_loop(0, tiles, tile, 0)


def over_either(first_leads, one, other):
    shape = one[0].shape
    unit = jnp.ones(shape, jnp.float32)
    scale_one = jnp.where(first_leads, unit, other[0])
    scale_other = jnp.where(first_leads, one[0], unit)
    return [one[0] * other[0]] + [scale_one * a + scale_other * b for a, b in zip(one[1:], other[1:])]


def far_kernel(parts, split, low, high, flip_ref, vector_ref, weight_ref, *refs):
    heads, body, refs = refs[:parts], refs[parts], refs[parts + 1 :]
    rest, refs = (refs[0], refs[2:]) if low else (None, refs)
    states, out_ref, picture_ref, ends_ref, sems = refs[:5]
    cell_refs, mixed_refs = refs[5:7], refs[7:]
    channels, rows, cols = out_ref.shape[1:]
    cells = cell_refs[0].shape[1]
    passes = vector_ref.shape[0]
    flip = flip_ref[0]
    me = lax.axis_index("depth")
    places = far_places(cells, rows, parts, split, heads[-1], body, rest)
    fill_ends(parts, cells, rows, heads, ends_ref)
    tiles = range(low // SUB, high // SUB)

    def prepare(base, slot):
        return prepare_steps(
            parts - 1, range(cells), places, body, base, cells, rows, parts, cols, ends_ref, weight_ref, cell_refs[slot], mixed_refs[slot]
        )

    def send(index):
        at = pl.ds(pl.multiple_of(index * SUB, SUB), SUB)
        return pltpu.make_async_copy(picture_ref.at[:, :, at, :], out_ref.at[:, :, at, :], sems.at[index])

    def finish(result, index):
        at = pl.ds(pl.multiple_of(index * SUB, SUB), SUB)
        for p in range(passes):
            images = [[states[m, p * channels + j, at, :] for j in range(channels)] for m in range(parts - 1)]
            images.append(result[p])
            bit = 0
            while len(images) > 1:
                leads = ((me >> bit) & 1) == flip
                images = [over_either(leads, images[j], images[j + 1]) for j in range(0, len(images), 2)]
                bit += 1
            for channel in range(3):
                picture_ref[p, channel, at, :] = images[0][channel + 1]
            picture_ref[p, 3, at, :] = 1.0 - images[0][0]
        send(index).start()

    for step in prepare(low, 0):
        step()

    def pair(i, carry):
        for slot in range(2):
            index = tiles[0] + 2 * i + slot
            after = pl.multiple_of(jnp.minimum(index + 1, tiles[-1]) * SUB, SUB)
            result = march_unit(flip, vector_ref, range(cells), cells, cell_refs[slot], mixed_refs[slot], prepare(after, 1 - slot))
            finish(result, index)
        return carry

    lax.fori_loop(0, len(tiles) // 2, pair, 0)
    for index in tiles:
        send(index).wait()


def swap_pairs(block, axis, start):
    pairs = [(i, i + 1) for i in range(start, lax.axis_size(axis) - 1, 2)]
    return lax.ppermute(block, axis, pairs + [(j, i) for i, j in pairs])


def swap_along(block, axis, mask):
    return lax.ppermute(block, axis, [(i, i ^ mask) for i in range(lax.axis_size(axis))])


def estimate(micros):
    return pl.CostEstimate(flops=int(micros * 1_000_000_000), transcendentals=0, bytes_accessed=0)


def on_device(field, light_vectors, transfer, light_index, flips):
    parts = lax.axis_size("depth")
    cells, all_rows, cols = field.shape
    rows = all_rows // parts
    passes = light_index.shape[0]
    channels, knots = transfer.shape[1:]
    tiles = rows // SUB
    values = passes * channels
    in_vmem = pl.BlockSpec(memory_space=VMEM)
    in_smem = pl.BlockSpec(memory_space=SMEM)
    in_any = pl.BlockSpec(memory_space=pl.ANY)
    in_hbm = pl.BlockSpec(memory_space=pltpu.HBM)

    def array(*shape):
        return jax.ShapeDtypeStruct(shape, jnp.float32)

    def settings(mib, micros):
        return dict(
            compiler_params=pltpu.CompilerParams(vmem_limit_bytes=mib * MIB),
            cost_estimate=pl.CostEstimate(flops=int(micros * 1e9), transcendentals=0, bytes_accessed=0),
        )

    near_rows = 2 * cells + cells * rows + SUB
    head_rows = 2 * cells + 2 * rows + SUB
    skip = rows // parts
    split = rows - rows // parts
    body_rows = skip + (cells - 2) * split + cells
    rest_rows = (cells - 2) * (rows - split) + 2 * SUB
    *packed, far_head = pl.pallas_call(
        functools.partial(pack_kernel, parts),
        out_shape=[array(near_rows, cols)] * (parts - 2) + [array(head_rows, cols)],
        in_specs=[in_hbm],
        out_specs=[in_vmem] * (parts - 1),
        scratch_shapes=[VMEM((parts - 1, 2, cells, SUB, cols), jnp.float32), pltpu.SemaphoreType.DMA((4, parts - 1))],
        name="pack",
        **settings(8, 1),
    )(pltpu.with_memory_space_constraint(field, pltpu.HBM))
    near = [swap_along(packed[m - 1], "depth", m) for m in range(1, parts - 1)]

    far_head = swap_along(far_head, "depth", parts - 1)

    edges, own, far_body, far_rest = pl.pallas_call(
        functools.partial(edge_kernel, parts, split),
        out_shape=[array(rows, cols), array(near_rows, cols), array(body_rows, cols), array(rest_rows, cols)],
        in_specs=[in_vmem, in_any],
        out_specs=[in_vmem] * 4,
        name="edges",
        **settings(8, 1),
    )(field, packed[0])
    sides = pl.pallas_call(
        functools.partial(side_kernel, parts),
        out_shape=[array(skip, cols)] * parts,
        in_specs=[in_vmem] * 2 + [in_any],
        out_specs=[in_vmem] * parts,
        name="sides",
        **settings(4, 0.1),
    )(swap_pairs(edges, "tile", 0), swap_pairs(edges, "tile", 1), far_head)
    laterals = [swap_along(sides[m], "depth", m) for m in range(1, parts - 1)]
    far_body = swap_along(lax.dynamic_update_slice(far_body, sides[-1], (0, 0)), "depth", parts - 1)
    *laterals, far_rest = lax.optimization_barrier((*laterals, far_rest))
    far_rest = swap_along(far_rest, "depth", parts - 1)

    cell_shape = VMEM((3, cells, SUB, cols), jnp.float32)
    mixed_shape = VMEM((cells, values * SUB, cols), jnp.float32)
    ends_shape = VMEM((parts + 2, 2, rows, cols), jnp.float32)
    weight_shape = jax.ShapeDtypeStruct((values * SUB, 3 * knots * SUB), jnp.bfloat16)
    inner, vectors, weights = pl.pallas_call(
        functools.partial(own_kernel, parts),
        out_shape=[array(values, rows, cols), array(passes, 3, SUB, cols), weight_shape],
        in_specs=[in_smem] * 3 + [in_vmem] * 3,
        out_specs=[in_vmem] * 3,
        scratch_shapes=[cell_shape] * 2 + [mixed_shape] * 2,
        name="own",
        **settings(12, 4),
    )(light_index, flips, light_vectors, transfer, own, sides[0])
    states = pl.pallas_call(
        functools.partial(near_kernel, parts),
        out_shape=array(parts - 1, values, rows, cols),
        in_specs=[in_smem] + [in_vmem] * (2 * parts + 2),
        out_specs=in_vmem,
        scratch_shapes=[ends_shape] + [cell_shape] * (parts - 1) + [mixed_shape] * (parts - 1),
        name="near",
        **settings(16, 60),
    )(flips, vectors, weights, inner, own, *near, far_head, sides[0], *laterals)
    picture = None
    for low, high in ((0, split), (split, rows)):
        late = [far_rest, picture] if low else []
        picture = pl.pallas_call(
            functools.partial(far_kernel, parts, split, low, high),
            out_shape=array(passes, channels, rows, cols),
            in_specs=[in_smem] + [in_vmem] * (parts + 3) + [in_vmem, in_any][: len(late)] + [in_vmem],
            out_specs=in_any,
            scratch_shapes=[
                VMEM((passes, channels, rows, cols), jnp.float32),
                ends_shape,
                pltpu.SemaphoreType.DMA((tiles,)),
            ]
            + [cell_shape] * 2
            + [mixed_shape] * 2,
            input_output_aliases={parts + 5: 0} if low else {},
            name="late" if low else "far",
            **settings(16, 2),
        )(flips, vectors, weights, own, *near, far_head, far_body, *late, states)
    return picture


def solution(mesh):
    in_specs = (P("depth", None, "tile"), P(), P(), P(), P("tile"))
    out_specs = P(None, None, "depth", "tile")
    return jax.shard_map(
        on_device, mesh=mesh, in_specs=in_specs, out_specs=out_specs, check_vma=False
    )
```

```python
import functools

import jax
import jax.numpy as jnp
from jax import lax
from jax.experimental import pallas as pl
from jax.experimental.pallas import tpu as pltpu
from jax.sharding import PartitionSpec as P

AMBIENT = 0.3
OPACITY = 2.0
SUB = 8
VMEM = pltpu.VMEM
SMEM = pltpu.SMEM
MIB = 1 << 20
FINE = 49152.0


def pack_kernel(parts, field_ref, *refs):
    outs, (rim_ref, sems) = refs[: parts - 1], refs[parts - 1 :]
    cells, all_rows, cols = field_ref.shape
    rows = all_rows // parts
    me = lax.axis_index("depth")
    copies, rims = [], []
    for j, out in enumerate(outs):
        low = pl.multiple_of((me ^ (j + 1)) * rows, SUB)
        before = pl.multiple_of(jnp.maximum(low - SUB, 0), SUB)
        after = pl.multiple_of(jnp.minimum(low + rows, all_rows - SUB), SUB)
        for side, start in enumerate((before, after)):
            source = field_ref.at[:, pl.ds(start, SUB), :]
            rims.append(pltpu.make_async_copy(source, rim_ref.at[j, side], sems.at[side, j]))
        block = field_ref.at[:, pl.ds(low, rows), :]
        if j < parts - 2:
            centre = out.at[pl.ds(cells, cells * rows), :].reshape(cells, rows, cols)
            quarter = cells // 4
            for q in range(4):
                layers = pl.ds(q * quarter, quarter)
                copies.append(pltpu.make_async_copy(block.at[layers], centre.at[layers], sems.at[2 + q, j]))
        else:
            for side in range(2):
                layer = out.at[pl.ds(cells + side * rows, rows), :]
                copies.append(pltpu.make_async_copy(block.at[side * (cells - 1)], layer, sems.at[2 + side, j]))
    for copy in rims + copies:
        copy.start()
    for copy in rims:
        copy.wait()
    for j, out in enumerate(outs):
        part = me ^ (j + 1)
        above = jnp.where(part > 0, 1.0, 0.0)
        below = jnp.where(part < parts - 1, 1.0, 0.0)
        for z in range(cells):
            out[z : z + 1, :] = rim_ref[j, 0, z, SUB - 1 : SUB, :] * above
            below_at = out.shape[0] - cells + z
            out[below_at : below_at + 1, :] = rim_ref[j, 1, z, 0:1, :] * below
    for copy in copies:
        copy.wait()


def edge_kernel(parts, split, field_ref, _, edge_ref, own_ref, body_ref, rest_ref):
    cells, all_rows, cols = field_ref.shape
    rows = all_rows // parts
    me = lax.axis_index("depth")
    lane_pair = lax.broadcasted_iota(jnp.int32, (SUB, cols), 1) // 2

    def tile(i, carry):
        acc = jnp.zeros((SUB, cols), jnp.float32)
        for part in range(parts):
            for z in range(cells):
                slot = part * cells + z
                start = pl.multiple_of(part * rows + i * SUB, SUB)
                value = field_ref[z, pl.ds(start, SUB), :]
                moved = pltpu.roll(value, (2 * slot + 1) % cols, 1)
                acc = jnp.where(lane_pair == slot, moved, acc)
        edge_ref[pl.ds(pl.multiple_of(i * SUB, SUB), SUB), :] = acc
        return carry

    lax.fori_loop(0, rows // SUB, tile, 0)
    low = pl.multiple_of(me * rows, SUB)
    above = jnp.where(me > 0, 1.0, 0.0)
    below = jnp.where(me < parts - 1, 1.0, 0.0)
    for z in range(cells):
        own_ref[z : z + 1, :] = field_ref[z, pl.ds(jnp.maximum(low - 1, 0), 1), :] * above
        below_at = cells + cells * rows + z
        own_ref[below_at : below_at + 1, :] = field_ref[z, pl.ds(jnp.minimum(low + rows, all_rows - 1), 1), :] * below
    far_low = pl.multiple_of((me ^ (parts - 1)) * rows, SUB)
    own_places, _, _ = near_places(cells, rows, own_ref)
    for z in range(cells):
        ref, start = own_places[z]
        ref[start : start + rows, :] = field_ref[z, pl.ds(low, rows), :]
    skip, more = rows // parts, rows - split
    for z in range(1, cells - 1):
        at = skip + (z - 1) * split
        body_ref[at : at + split, :] = field_ref[z, pl.ds(far_low, split), :]
        next_row = skip + (cells - 2) * split + z - 1
        body_ref[next_row : next_row + 1, :] = field_ref[z, pl.ds(far_low + split, 1), :]
        at = SUB + (z - 1) * more
        rest_ref[at : at + more, :] = field_ref[z, pl.ds(far_low + split, more), :]


def side_kernel(parts, even_ref, odd_ref, _, *outs):
    rows, cols = even_ref.shape
    group = rows // parts
    width = cols // parts
    me = lax.axis_index("depth")
    lane = lax.broadcasted_iota(jnp.int32, (rows, cols), 1)
    tile = lax.axis_index("tile")
    sides = jnp.where((lane + tile) % 2 == 1, even_ref[...], odd_ref[...])
    for m in range(parts):
        acc = jnp.zeros((group, cols), jnp.float32)
        for j in range(parts):
            moved = pltpu.roll(sides[j * group : (j + 1) * group], (j - (me ^ m) + parts) * width % cols, 1)
            acc = jnp.where(lane[:group] // width == j, moved, acc)
        outs[m][...] = acc


def near_places(cells, rows, head):
    count = head.shape[0]
    places = [(head, cells + z * rows) for z in range(cells)]
    tops = [(0, head, z) for z in range(cells)]
    bottoms = [(rows - SUB, head, count - cells + z) for z in range(cells)]
    return places, tops, bottoms


def far_places(cells, rows, parts, split, head, body, rest=None):
    skip, more = rows // parts, rows - split
    places, tops, bottoms = near_places(cells, rows, head)
    places[0], places[-1] = (head, cells), (head, cells + rows)
    for z in range(1, cells - 1):
        if rest is None:
            places[z] = (body, skip + (z - 1) * split)
            bottoms[z] = (split - SUB, body, skip + (cells - 2) * split + z - 1)
        else:
            places[z] = (rest, SUB + (z - 1) * more - split)
            tops[z] = (split, body, skip + z * split - 1)
    return places, tops, bottoms


def fill_ends(parts, cells, rows, heads, ends_ref):
    me = lax.axis_index("depth")
    ends_ref[0, 1] = jnp.zeros_like(ends_ref[0, 1])
    ends_ref[parts + 1, 0] = jnp.zeros_like(ends_ref[0, 0])
    for m in range(parts):
        last = (cells - 1) * rows if m < parts - 1 else rows
        ends_ref[(me ^ m) + 1, 0] = heads[m][cells : cells + rows, :]
        ends_ref[(me ^ m) + 1, 1] = heads[m][cells + last : cells + last + rows, :]


def fill_weights(index_ref, curves_ref, scale, weight_ref):
    passes = index_ref.shape[0]
    channels, knots = curves_ref.shape[1:]
    width = weight_ref.shape[1]
    block = knots * SUB
    points = jnp.concatenate([curves_ref[index_ref[p]] for p in range(passes)], axis=0)
    channel = lax.broadcasted_iota(jnp.int32, points.shape, 0) % channels
    points = jnp.where(channel == channels - 1, points * scale, points)
    knot = lax.broadcasted_iota(jnp.int32, (knots, width), 0)
    lane = lax.broadcasted_iota(jnp.int32, (knots, width), 1)
    target = lane // SUB % knots
    here = jnp.where(knot == target, 1.0, 0.0)
    after = jnp.where(knot == target + 1, 1.0, 0.0)
    is_slope = jnp.logical_and(lane >= block, lane < 2 * block)
    spread = jnp.where(is_slope, after - here, here)
    values = jnp.dot(points, spread, precision=lax.Precision.HIGHEST, preferred_element_type=jnp.float32)
    shape = (2 * SUB, width)
    row = lax.broadcasted_iota(jnp.int32, shape, 0)
    lane = lax.broadcasted_iota(jnp.int32, shape, 1)
    on_row = lane % SUB == row % SUB
    for pair in range(passes * channels // 2):
        upper, lower = [jnp.broadcast_to(values[2 * pair + j : 2 * pair + j + 1], shape) for j in range(2)]
        value = jnp.where(on_row, jnp.where(row < SUB, upper, lower), 0.0)
        coarse = value.astype(jnp.bfloat16).astype(jnp.float32)
        value = jnp.where(lane < 2 * block, value, value - coarse)
        weight_ref[2 * pair * SUB : 2 * (pair + 1) * SUB, :] = value.astype(jnp.bfloat16)


def prepare_steps(m, zs, where, lateral, base, cells, rows, parts, cols, ends_ref, weight_ref, cell_ref, mixed_ref):
    me = lax.axis_index("depth")
    part = me ^ m
    at = pl.ds(base, SUB)
    lane = lax.broadcasted_iota(jnp.int32, (SUB, cols), 1)
    sublane = lax.broadcasted_iota(jnp.int32, (SUB, cols), 0)
    is_first = lane == 0
    is_last = lane == cols - 1
    places, tops, bottoms = where
    group = rows // parts
    got = lateral[pl.ds(pl.multiple_of(base % group, SUB), SUB), :]
    sides = pltpu.roll(got, (2 * cols - 1 - base // group * (cols // parts)) % cols, 1)

    def layer(z):
        if z < 0:
            return ends_ref[part, 1, at, :]
        if z == cells:
            return ends_ref[part + 2, 0, at, :]
        ref, low = places[z]
        return ref[pl.ds(low + base, SUB), :]

    def step(z):
        ref, low = places[z]
        here = layer(z)
        top_at, top_ref, top = tops[z]
        bottom_at, bottom_ref, bottom = bottoms[z]
        is_top = jnp.logical_and(sublane == 0, base == top_at)
        is_bottom = jnp.logical_and(sublane == SUB - 1, base == bottom_at)
        upper = jnp.where(is_top, top_ref[top : top + 1, :], ref[pl.ds(low + base - 1, SUB), :])
        lower = jnp.where(is_bottom, bottom_ref[bottom : bottom + 1, :], ref[pl.ds(low + base + 1, SUB), :])
        edge = pltpu.roll(sides, (cols - 2 * z) % cols, 1) if z else sides
        grad_x = pltpu.roll(jnp.where(is_first, edge, here), cols - 1, 1) - pltpu.roll(
            jnp.where(is_last, edge, here), 1, 1
        )
        grad_y = lower - upper
        grad_z = layer(z + 1) - layer(z - 1)
        inverse = lax.rsqrt(grad_x * grad_x + grad_y * grad_y + grad_z * grad_z + 4.0)
        cell_ref[0, z] = grad_x * inverse
        cell_ref[1, z] = grad_y * inverse
        cell_ref[2, z] = grad_z * inverse
        half = 0.5 * (knots - 1)
        position = half + half * jnp.tanh(0.5 * here)
        coarse = (position + FINE) - FINE
        segment = jnp.minimum(jnp.floor(position), knots - 2.0)
        rest = position - coarse
        right = coarse - segment
        left = 1.0 - right
        twice = lambda value: jnp.concatenate([value, value], axis=0).astype(jnp.bfloat16)
        left, right, rest, segment = twice(left), twice(right), twice(rest), twice(segment)
        zero = jnp.zeros_like(left)
        tents, rests = [], []
        for k in range(0, knots, 2):
            is_here = segment == pair_at + k
            is_before = segment == pair_at + (k - 1)
            tents.append(jnp.where(is_here, left, jnp.where(is_before, right, zero)))
            rests.append(jnp.where(is_here, rest, zero))
        return [jnp.concatenate(part, axis=0) for part in (tents, rests)]

    def two(first, second):
        tents, rests = [jnp.concatenate(both, axis=1) for both in zip(step(first), step(second))]
        right = jnp.concatenate([tents, rests, tents], axis=0)
        mixed = jnp.dot(weight_ref[...], right, preferred_element_type=jnp.float32)
        mixed_ref[first] = mixed[:, :cols]
        mixed_ref[second] = mixed[:, cols:]

    knots = weight_ref.shape[1] // (3 * SUB)
    pair_at = jnp.where(lax.broadcasted_iota(jnp.int32, (2 * SUB, cols), 0) < SUB, 0.0, 1.0).astype(jnp.bfloat16)
    zs = list(zs)
    return [functools.partial(two, *zs[i : i + 2]) for i in range(0, len(zs), 2)]


def march_unit(flip, vector_ref, zs, cells, cell_ref, mixed_ref, beside, inner=None):
    passes = vector_ref.shape[0]
    channels = mixed_ref.shape[1] // (passes * SUB)
    shape = vector_ref.shape[2:]
    vectors = [[vector_ref[p, axis] for axis in range(3)] for p in range(passes)]
    state = [(jnp.ones(shape, jnp.float32), [jnp.zeros(shape, jnp.float32)] * 3)] * passes
    count = len(beside)
    for u, spot in enumerate(zs):
        for step in beside[u * count // len(zs) : (u + 1) * count // len(zs)]:
            step()
        z = spot + flip * (cells - 1 - 2 * spot)
        normal = [cell_ref[axis, z] for axis in range(3)]
        for p in range(passes):
            keep, sums = state[p]
            mixed = [mixed_ref[z, (p * channels + c) * SUB : (p * channels + c + 1) * SUB, :] for c in range(channels)]
            facing = normal[0] * vectors[p][0] + normal[1] * vectors[p][1] + normal[2] * vectors[p][2]
            taken = keep * mixed[3]
            weight = taken * (AMBIENT + jnp.abs(facing))
            sums = [total + weight * tint for total, tint in zip(sums, mixed)]
            keep = keep - taken
            if inner is not None and u == 0:
                keep, sums = keep * inner(p, 0), [total + keep * inner(p, j + 1) for j, total in enumerate(sums)]
            state[p] = (keep, sums)
    return [[keep] + sums for keep, sums in state]


def march_tiles(count, start, prepare, unit):
    def ahead(index, slot):
        return prepare(pl.multiple_of((index + 1) * SUB, SUB), 1 - slot)

    for step in prepare(start * SUB, 0):
        step()

    def pair(i, carry):
        for slot in range(2):
            index = start + 2 * i + slot
            unit(index, slot, ahead(index, slot))
        return carry

    lax.fori_loop(0, count // 2 - 1, pair, 0)
    unit(start + count - 2, 0, ahead(start + count - 2, 0))
    unit(start + count - 1, 1, [])


def own_kernel(parts, index_ref, flip_ref, lights_ref, curves_ref, own_ref, lateral_ref, out_ref, vector_ref, weight_ref, *refs):
    cell_refs, mixed_refs = refs[:2], refs[2:]
    rows, cols = out_ref.shape[1:]
    channels = curves_ref.shape[1]
    passes = index_ref.shape[0]
    cells = cell_refs[0].shape[1]
    flip = flip_ref[0]
    tiles = rows // SUB
    inner = range(1, cells - 1)
    for p in range(passes):
        for axis in range(3):
            vector_ref[p, axis] = jnp.full((SUB, cols), lights_ref[index_ref[p], axis])
    fill_weights(index_ref, curves_ref, OPACITY / (parts * cells), weight_ref)
    places = near_places(cells, rows, own_ref)

    def prepare(base, slot):
        return prepare_steps(
            0, inner, places, lateral_ref, base, cells, rows, parts, cols, None, weight_ref, cell_refs[slot], mixed_refs[slot]
        )

    def unit(index, slot, beside):
        base = pl.multiple_of(index * SUB, SUB)
        result = march_unit(flip, vector_ref, inner, cells, cell_refs[slot], mixed_refs[slot], beside)
        for p in range(passes):
            for j in range(channels):
                out_ref[p * channels + j, pl.ds(base, SUB), :] = result[p][j]

    march_tiles(tiles, 0, prepare, unit)


def near_kernel(parts, flip_ref, vector_ref, weight_ref, inner_ref, *refs):
    count = parts - 1
    heads, laterals, out_ref, ends_ref = refs[:parts], refs[parts : 2 * parts - 1], refs[2 * parts - 1], refs[2 * parts]
    cell_refs, mixed_refs = refs[2 * parts + 1 : 2 * parts + 1 + count], refs[2 * parts + 1 + count :]
    rows, cols = out_ref.shape[2:]
    cells = cell_refs[0].shape[1]
    passes = vector_ref.shape[0]
    channels = inner_ref.shape[0] // passes
    flip = flip_ref[0]
    tiles = rows // SUB
    zs = [(0, cells - 1)] + [range(cells)] * (count - 1)
    places = [near_places(cells, rows, head) for head in heads[:count]]
    fill_ends(parts, cells, rows, heads, ends_ref)

    def prepare(m, base):
        return prepare_steps(
            m, zs[m], places[m], laterals[m], base, cells, rows, parts, cols, ends_ref, weight_ref, cell_refs[m], mixed_refs[m]
        )

    for step in prepare(0, 0):
        step()

    def tile(i, carry):
        base = pl.multiple_of(i * SUB, SUB)
        after = pl.multiple_of(jnp.minimum(i + 1, tiles - 1) * SUB, SUB)
        at = pl.ds(base, SUB)
        for m in range(count):
            beside = prepare(m + 1, base) if m + 1 < count else prepare(0, after)
            inner = (lambda p, j: inner_ref[p * channels + j, at, :]) if m == 0 else None
            result = march_unit(flip, vector_ref, zs[m], cells, cell_refs[m], mixed_refs[m], beside, inner)
            for p in range(passes):
                for j in range(channels):
                    out_ref[m, p * channels + j, at, :] = result[p][j]
        return carry

    lax.fori_loop(0, tiles, tile, 0)


def over_either(first_leads, one, other):
    shape = one[0].shape
    unit = jnp.ones(shape, jnp.float32)
    scale_one = jnp.where(first_leads, unit, other[0])
    scale_other = jnp.where(first_leads, one[0], unit)
    return [one[0] * other[0]] + [scale_one * a + scale_other * b for a, b in zip(one[1:], other[1:])]


def far_kernel(parts, split, low, high, flip_ref, vector_ref, weight_ref, *refs):
    heads, body, refs = refs[:parts], refs[parts], refs[parts + 1 :]
    rest, refs = (refs[0], refs[2:]) if low else (None, refs)
    states, out_ref, picture_ref, ends_ref, sems = refs[:5]
    cell_refs, mixed_refs = refs[5:7], refs[7:]
    channels, rows, cols = out_ref.shape[1:]
    cells = cell_refs[0].shape[1]
    passes = vector_ref.shape[0]
    flip = flip_ref[0]
    me = lax.axis_index("depth")
    places = far_places(cells, rows, parts, split, heads[-1], body, rest)
    fill_ends(parts, cells, rows, heads, ends_ref)
    tiles = range(low // SUB, high // SUB)

    def prepare(base, slot):
        return prepare_steps(
            parts - 1, range(cells), places, body, base, cells, rows, parts, cols, ends_ref, weight_ref, cell_refs[slot], mixed_refs[slot]
        )

    def send(index):
        at = pl.ds(pl.multiple_of(index * SUB, SUB), SUB)
        return pltpu.make_async_copy(picture_ref.at[:, :, at, :], out_ref.at[:, :, at, :], sems.at[index])

    def finish(result, index):
        at = pl.ds(pl.multiple_of(index * SUB, SUB), SUB)
        for p in range(passes):
            images = [[states[m, p * channels + j, at, :] for j in range(channels)] for m in range(parts - 1)]
            images.append(result[p])
            bit = 0
            while len(images) > 1:
                leads = ((me >> bit) & 1) == flip
                images = [over_either(leads, images[j], images[j + 1]) for j in range(0, len(images), 2)]
                bit += 1
            for channel in range(3):
                picture_ref[p, channel, at, :] = images[0][channel + 1]
            picture_ref[p, 3, at, :] = 1.0 - images[0][0]
        send(index).start()

    def unit(index, slot, beside):
        finish(march_unit(flip, vector_ref, range(cells), cells, cell_refs[slot], mixed_refs[slot], beside), index)

    march_tiles(len(tiles), tiles[0], prepare, unit)
    for index in tiles:
        send(index).wait()


def swap_pairs(block, axis, start):
    pairs = [(i, i + 1) for i in range(start, lax.axis_size(axis) - 1, 2)]
    return lax.ppermute(block, axis, pairs + [(j, i) for i, j in pairs])


def swap_along(block, axis, mask):
    return lax.ppermute(block, axis, [(i, i ^ mask) for i in range(lax.axis_size(axis))])


def estimate(micros):
    return pl.CostEstimate(flops=int(micros * 1_000_000_000), transcendentals=0, bytes_accessed=0)


def on_device(field, light_vectors, transfer, light_index, flips):
    parts = lax.axis_size("depth")
    cells, all_rows, cols = field.shape
    rows = all_rows // parts
    passes = light_index.shape[0]
    channels, knots = transfer.shape[1:]
    tiles = rows // SUB
    values = passes * channels
    in_vmem = pl.BlockSpec(memory_space=VMEM)
    in_smem = pl.BlockSpec(memory_space=SMEM)
    in_any = pl.BlockSpec(memory_space=pl.ANY)
    in_hbm = pl.BlockSpec(memory_space=pltpu.HBM)

    def array(*shape):
        return jax.ShapeDtypeStruct(shape, jnp.float32)

    def settings(mib, micros):
        return dict(
            compiler_params=pltpu.CompilerParams(vmem_limit_bytes=mib * MIB),
            cost_estimate=pl.CostEstimate(flops=int(micros * 1e9), transcendentals=0, bytes_accessed=0),
        )

    near_rows = 2 * cells + cells * rows
    head_rows = 2 * cells + 2 * rows
    skip = rows // parts
    split = rows - rows // parts
    body_rows = skip + (cells - 2) * split + cells
    rest_rows = (cells - 2) * (rows - split) + 2 * SUB
    *packed, far_head = pl.pallas_call(
        functools.partial(pack_kernel, parts),
        out_shape=[array(near_rows, cols)] * (parts - 2) + [array(head_rows, cols)],
        in_specs=[in_hbm],
        out_specs=[in_vmem] * (parts - 1),
        scratch_shapes=[VMEM((parts - 1, 2, cells, SUB, cols), jnp.float32), pltpu.SemaphoreType.DMA((6, parts - 1))],
        name="pack",
        **settings(8, 1),
    )(pltpu.with_memory_space_constraint(field, pltpu.HBM))
    near = [swap_along(packed[m - 1], "depth", m) for m in range(1, parts - 1)]

    far_head = swap_along(far_head, "depth", parts - 1)

    edges, own, far_body, far_rest = pl.pallas_call(
        functools.partial(edge_kernel, parts, split),
        out_shape=[array(rows, cols), array(near_rows, cols), array(body_rows, cols), array(rest_rows, cols)],
        in_specs=[in_vmem, in_any],
        out_specs=[in_vmem] * 4,
        name="edges",
        **settings(8, 1),
    )(field, packed[0])
    sides = pl.pallas_call(
        functools.partial(side_kernel, parts),
        out_shape=[array(skip, cols)] * parts,
        in_specs=[in_vmem] * 2 + [in_any],
        out_specs=[in_vmem] * parts,
        name="sides",
        **settings(4, 0.1),
    )(swap_pairs(edges, "tile", 0), swap_pairs(edges, "tile", 1), far_head)
    laterals = [swap_along(sides[m], "depth", m) for m in range(1, parts - 1)]
    far_body = swap_along(lax.dynamic_update_slice(far_body, sides[-1], (0, 0)), "depth", parts - 1)
    *laterals, far_rest = lax.optimization_barrier((*laterals, far_rest))
    far_rest = swap_along(far_rest, "depth", parts - 1)

    cell_shape = VMEM((3, cells, SUB, cols), jnp.float32)
    mixed_shape = VMEM((cells, values * SUB, cols), jnp.float32)
    ends_shape = VMEM((parts + 2, 2, rows, cols), jnp.float32)
    weight_shape = jax.ShapeDtypeStruct((values * SUB, 3 * knots * SUB), jnp.bfloat16)
    inner, vectors, weights = pl.pallas_call(
        functools.partial(own_kernel, parts),
        out_shape=[array(values, rows, cols), array(passes, 3, SUB, cols), weight_shape],
        in_specs=[in_smem] * 3 + [in_vmem] * 3,
        out_specs=[in_vmem] * 3,
        scratch_shapes=[cell_shape] * 2 + [mixed_shape] * 2,
        name="own",
        **settings(12, 4),
    )(light_index, flips, light_vectors, transfer, own, sides[0])
    states = pl.pallas_call(
        functools.partial(near_kernel, parts),
        out_shape=array(parts - 1, values, rows, cols),
        in_specs=[in_smem] + [in_vmem] * (2 * parts + 2),
        out_specs=in_vmem,
        scratch_shapes=[ends_shape] + [cell_shape] * (parts - 1) + [mixed_shape] * (parts - 1),
        name="near",
        **settings(16, 60),
    )(flips, vectors, weights, inner, own, *near, far_head, sides[0], *laterals)
    picture = None
    for low, high in ((0, split), (split, rows)):
        late = [far_rest, picture] if low else []
        picture = pl.pallas_call(
            functools.partial(far_kernel, parts, split, low, high),
            out_shape=array(passes, channels, rows, cols),
            in_specs=[in_smem] + [in_vmem] * (parts + 3) + [in_vmem, in_any][: len(late)] + [in_vmem],
            out_specs=in_any,
            scratch_shapes=[
                VMEM((passes, channels, rows, cols), jnp.float32),
                ends_shape,
                pltpu.SemaphoreType.DMA((tiles,)),
            ]
            + [cell_shape] * 2
            + [mixed_shape] * 2,
            input_output_aliases={parts + 5: 0} if low else {},
            name="late" if low else "far",
            **settings(16, 2),
        )(flips, vectors, weights, own, *near, far_head, far_body, *late, states)
    return picture


def solution(mesh):
    in_specs = (P("depth", None, "tile"), P(), P(), P(), P("tile"))
    out_specs = P(None, None, "depth", "tile")
    return jax.shard_map(
        on_device, mesh=mesh, in_specs=in_specs, out_specs=out_specs, check_vma=False
    )
```

```python
import functools

import jax
import jax.numpy as jnp
from jax import lax
from jax.experimental import pallas as pl
from jax.experimental.pallas import tpu as pltpu
from jax.sharding import PartitionSpec as P

AMBIENT = 0.3
OPACITY = 2.0
SUB = 8
VMEM = pltpu.VMEM
SMEM = pltpu.SMEM
MIB = 1 << 20
FINE = 49152.0
WHOLE = 12582912.0


def pack_kernel(parts, field_ref, *refs):
    outs, (rim_ref, sems) = refs[: parts - 1], refs[parts - 1 :]
    cells, all_rows, cols = field_ref.shape
    rows = all_rows // parts
    me = lax.axis_index("depth")
    copies, rims = [], []
    for j, out in enumerate(outs):
        low = pl.multiple_of((me ^ (j + 1)) * rows, SUB)
        before = pl.multiple_of(jnp.maximum(low - SUB, 0), SUB)
        after = pl.multiple_of(jnp.minimum(low + rows, all_rows - SUB), SUB)
        for side, start in enumerate((before, after)):
            source = field_ref.at[:, pl.ds(start, SUB), :]
            rims.append(pltpu.make_async_copy(source, rim_ref.at[j, side], sems.at[side, j]))
        block = field_ref.at[:, pl.ds(low, rows), :]
        if j < parts - 2:
            centre = out.at[pl.ds(cells, cells * rows), :].reshape(cells, rows, cols)
            quarter = cells // 4
            for q in range(4):
                layers = pl.ds(q * quarter, quarter)
                copies.append(pltpu.make_async_copy(block.at[layers], centre.at[layers], sems.at[2 + q, j]))
        else:
            for side in range(2):
                layer = out.at[pl.ds(cells + side * rows, rows), :]
                copies.append(pltpu.make_async_copy(block.at[side * (cells - 1)], layer, sems.at[2 + side, j]))
    for copy in rims + copies:
        copy.start()
    for copy in rims:
        copy.wait()
    for j, out in enumerate(outs):
        part = me ^ (j + 1)
        above = jnp.where(part > 0, 1.0, 0.0)
        below = jnp.where(part < parts - 1, 1.0, 0.0)
        for z in range(cells):
            out[z : z + 1, :] = rim_ref[j, 0, z, SUB - 1 : SUB, :] * above
            below_at = out.shape[0] - cells + z
            out[below_at : below_at + 1, :] = rim_ref[j, 1, z, 0:1, :] * below
    for copy in copies:
        copy.wait()


def edge_kernel(parts, split, field_ref, _, edge_ref, own_ref, body_ref, rest_ref):
    cells, all_rows, cols = field_ref.shape
    rows = all_rows // parts
    me = lax.axis_index("depth")
    lane_pair = lax.broadcasted_iota(jnp.int32, (SUB, cols), 1) // 2

    def tile(i, carry):
        acc = jnp.zeros((SUB, cols), jnp.float32)
        for part in range(parts):
            for z in range(cells):
                slot = part * cells + z
                start = pl.multiple_of(part * rows + i * SUB, SUB)
                value = field_ref[z, pl.ds(start, SUB), :]
                moved = pltpu.roll(value, (2 * slot + 1) % cols, 1)
                acc = jnp.where(lane_pair == slot, moved, acc)
        edge_ref[pl.ds(pl.multiple_of(i * SUB, SUB), SUB), :] = acc
        return carry

    lax.fori_loop(0, rows // SUB, tile, 0)
    low = pl.multiple_of(me * rows, SUB)
    above = jnp.where(me > 0, 1.0, 0.0)
    below = jnp.where(me < parts - 1, 1.0, 0.0)
    for z in range(cells):
        own_ref[z : z + 1, :] = field_ref[z, pl.ds(jnp.maximum(low - 1, 0), 1), :] * above
        below_at = cells + cells * rows + z
        own_ref[below_at : below_at + 1, :] = field_ref[z, pl.ds(jnp.minimum(low + rows, all_rows - 1), 1), :] * below
    far_low = pl.multiple_of((me ^ (parts - 1)) * rows, SUB)
    own_places, _, _ = near_places(cells, rows, own_ref)
    for z in range(cells):
        ref, start = own_places[z]
        ref[start : start + rows, :] = field_ref[z, pl.ds(low, rows), :]
    skip, more = rows // parts, rows - split
    for z in range(1, cells - 1):
        at = skip + (z - 1) * split
        body_ref[at : at + split, :] = field_ref[z, pl.ds(far_low, split), :]
        next_row = skip + (cells - 2) * split + z - 1
        body_ref[next_row : next_row + 1, :] = field_ref[z, pl.ds(far_low + split, 1), :]
        at = SUB + (z - 1) * more
        rest_ref[at : at + more, :] = field_ref[z, pl.ds(far_low + split, more), :]


def side_kernel(parts, even_ref, odd_ref, _, *outs):
    rows, cols = even_ref.shape
    group = rows // parts
    width = cols // parts
    me = lax.axis_index("depth")
    lane = lax.broadcasted_iota(jnp.int32, (rows, cols), 1)
    tile = lax.axis_index("tile")
    sides = jnp.where((lane + tile) % 2 == 1, even_ref[...], odd_ref[...])
    for m in range(parts):
        acc = jnp.zeros((group, cols), jnp.float32)
        for j in range(parts):
            moved = pltpu.roll(sides[j * group : (j + 1) * group], (j - (me ^ m) + parts) * width % cols, 1)
            acc = jnp.where(lane[:group] // width == j, moved, acc)
        outs[m][...] = acc


def near_places(cells, rows, head):
    count = head.shape[0]
    places = [(head, cells + z * rows) for z in range(cells)]
    tops = [(0, head, z) for z in range(cells)]
    bottoms = [(rows - SUB, head, count - cells + z) for z in range(cells)]
    return places, tops, bottoms


def far_places(cells, rows, parts, split, head, body, rest=None):
    skip, more = rows // parts, rows - split
    places, tops, bottoms = near_places(cells, rows, head)
    places[0], places[-1] = (head, cells), (head, cells + rows)
    for z in range(1, cells - 1):
        if rest is None:
            places[z] = (body, skip + (z - 1) * split)
            bottoms[z] = (split - SUB, body, skip + (cells - 2) * split + z - 1)
        else:
            places[z] = (rest, SUB + (z - 1) * more - split)
            tops[z] = (split, body, skip + z * split - 1)
    return places, tops, bottoms


def fill_ends(parts, cells, rows, heads, ends_ref):
    me = lax.axis_index("depth")
    ends_ref[0, 1] = jnp.zeros_like(ends_ref[0, 1])
    ends_ref[parts + 1, 0] = jnp.zeros_like(ends_ref[0, 0])
    for m in range(parts):
        last = (cells - 1) * rows if m < parts - 1 else rows
        ends_ref[(me ^ m) + 1, 0] = heads[m][cells : cells + rows, :]
        ends_ref[(me ^ m) + 1, 1] = heads[m][cells + last : cells + last + rows, :]


def fill_weights(index_ref, curves_ref, scale, weight_ref):
    passes = index_ref.shape[0]
    channels, knots = curves_ref.shape[1:]
    width = weight_ref.shape[1]
    block = knots * SUB
    points = jnp.concatenate([curves_ref[index_ref[p]] for p in range(passes)], axis=0)
    channel = lax.broadcasted_iota(jnp.int32, points.shape, 0) % channels
    points = jnp.where(channel == channels - 1, points * scale, points)
    knot = lax.broadcasted_iota(jnp.int32, (knots, width), 0)
    lane = lax.broadcasted_iota(jnp.int32, (knots, width), 1)
    target = lane // SUB % knots
    here = jnp.where(knot == target, 1.0, 0.0)
    after = jnp.where(knot == target + 1, 1.0, 0.0)
    is_slope = jnp.logical_and(lane >= block, lane < 2 * block)
    spread = jnp.where(is_slope, after - here, here)
    values = jnp.dot(points, spread, precision=lax.Precision.HIGHEST, preferred_element_type=jnp.float32)
    shape = (2 * SUB, width)
    row = lax.broadcasted_iota(jnp.int32, shape, 0)
    lane = lax.broadcasted_iota(jnp.int32, shape, 1)
    on_row = lane % SUB == row % SUB
    for pair in range(passes * channels // 2):
        upper, lower = [jnp.broadcast_to(values[2 * pair + j : 2 * pair + j + 1], shape) for j in range(2)]
        value = jnp.where(on_row, jnp.where(row < SUB, upper, lower), 0.0)
        coarse = value.astype(jnp.bfloat16).astype(jnp.float32)
        value = jnp.where(lane < 2 * block, value, value - coarse)
        weight_ref[2 * pair * SUB : 2 * (pair + 1) * SUB, :] = value.astype(jnp.bfloat16)


def mix_steps(zs, places, base, cols, weight_ref, mixed_ref):
    knots = weight_ref.shape[1] // (3 * SUB)
    half = 0.5 * (knots - 1)
    row = lax.broadcasted_iota(jnp.int32, (2 * SUB, cols), 0)
    knot_at = [jnp.where(row < SUB, 0.0 + k, 1.0 + k).astype(jnp.bfloat16) for k in range(0, knots, 2)]
    zero = jnp.zeros((2 * SUB, cols), jnp.bfloat16)

    def twice(value):
        return jnp.concatenate([value, value], axis=0).astype(jnp.bfloat16)

    def basis(z):
        ref, low = places[z]
        scaled = half * jnp.tanh(0.5 * ref[pl.ds(low + base, SUB), :])
        position = scaled + half
        segment = ((scaled + (half - 0.5)) + WHOLE) - WHOLE
        coarse = (position + FINE) - FINE
        right = coarse - segment
        left, right, rest = twice(1.0 - right), twice(right), twice(position - coarse)
        here = twice(segment)
        after = twice(segment + 1.0)
        tents, rests = [], []
        for at in knot_at:
            is_here = here == at
            tents.append(jnp.where(is_here, left, jnp.where(after == at, right, zero)))
            rests.append(jnp.where(is_here, rest, zero))
        return [jnp.concatenate(part, axis=0) for part in (tents, rests)]

    def two(first, second):
        tents, rests = [jnp.concatenate(both, axis=1) for both in zip(basis(first), basis(second))]
        right = jnp.concatenate([tents, rests, tents], axis=0)
        mixed = jnp.dot(weight_ref[...], right, preferred_element_type=jnp.float32)
        mixed_ref[first] = mixed[:, :cols]
        mixed_ref[second] = mixed[:, cols:]

    zs = list(zs)
    return [functools.partial(two, *zs[i : i + 2]) for i in range(0, len(zs), 2)]


def slope_steps(m, zs, where, lateral, base, cells, rows, parts, cols, ends_ref, cell_ref):
    places, tops, bottoms = where
    me = lax.axis_index("depth")
    part = me ^ m
    at = pl.ds(base, SUB)
    lane = lax.broadcasted_iota(jnp.int32, (SUB, cols), 1)
    sublane = lax.broadcasted_iota(jnp.int32, (SUB, cols), 0)
    is_first = lane == 0
    is_last = lane == cols - 1
    is_top = {low: jnp.logical_and(sublane == 0, base == low) for low in sorted({top[0] for top in tops})}
    is_bottom = {
        low: jnp.logical_and(sublane == SUB - 1, base == low) for low in sorted({bottom[0] for bottom in bottoms})
    }
    group = rows // parts
    got = lateral[pl.ds(pl.multiple_of(base % group, SUB), SUB), :]
    sides = pltpu.roll(got, (2 * cols - 1 - base // group * (cols // parts)) % cols, 1)

    def layer(z):
        if z < 0:
            return ends_ref[part, 1, at, :]
        if z == cells:
            return ends_ref[part + 2, 0, at, :]
        ref, low = places[z]
        return ref[pl.ds(low + base, SUB), :]

    def step(z):
        ref, low = places[z]
        here = layer(z)
        top_at, top_ref, top = tops[z]
        bottom_at, bottom_ref, bottom = bottoms[z]
        upper = jnp.where(is_top[top_at], top_ref[top : top + 1, :], ref[pl.ds(low + base - 1, SUB), :])
        lower = jnp.where(is_bottom[bottom_at], bottom_ref[bottom : bottom + 1, :], ref[pl.ds(low + base + 1, SUB), :])
        edge = pltpu.roll(sides, (cols - 2 * z) % cols, 1) if z else sides
        grad_x = pltpu.roll(jnp.where(is_first, edge, here), cols - 1, 1) - pltpu.roll(
            jnp.where(is_last, edge, here), 1, 1
        )
        grad_y = lower - upper
        grad_z = layer(z + 1) - layer(z - 1)
        inverse = lax.rsqrt(grad_x * grad_x + grad_y * grad_y + grad_z * grad_z + 4.0)
        cell_ref[0, z] = grad_x * inverse
        cell_ref[1, z] = grad_y * inverse
        cell_ref[2, z] = grad_z * inverse

    return [functools.partial(step, z) for z in zs]


def prepare_steps(m, zs, where, lateral, base, cells, rows, parts, cols, ends_ref, weight_ref, cell_ref, mixed_ref):
    slopes = slope_steps(m, zs, where, lateral, base, cells, rows, parts, cols, ends_ref, cell_ref)
    mixes = mix_steps(zs, where[0], base, cols, weight_ref, mixed_ref)

    def both(i):
        mixes[i]()
        for step in slopes[2 * i : 2 * i + 2]:
            step()

    return [functools.partial(both, i) for i in range(len(mixes))]


def march_unit(flip, vector_ref, zs, cells, cell_ref, mixed_ref, beside, inner=None):
    passes = vector_ref.shape[0]
    channels = mixed_ref.shape[1] // (passes * SUB)
    shape = vector_ref.shape[2:]
    vectors = [[vector_ref[p, axis] for axis in range(3)] for p in range(passes)]
    state = [(jnp.ones(shape, jnp.float32), [jnp.zeros(shape, jnp.float32)] * 3)] * passes
    count = len(beside)
    for u, spot in enumerate(zs):
        for step in beside[u * count // len(zs) : (u + 1) * count // len(zs)]:
            step()
        z = spot + flip * (cells - 1 - 2 * spot)
        normal = [cell_ref[axis, z] for axis in range(3)]
        for p in range(passes):
            keep, sums = state[p]
            mixed = [mixed_ref[z, (p * channels + c) * SUB : (p * channels + c + 1) * SUB, :] for c in range(channels)]
            facing = normal[0] * vectors[p][0] + normal[1] * vectors[p][1] + normal[2] * vectors[p][2]
            taken = keep * mixed[3]
            weight = taken * (AMBIENT + jnp.abs(facing))
            sums = [total + weight * tint for total, tint in zip(sums, mixed)]
            keep = keep - taken
            if inner is not None and u == 0:
                keep, sums = keep * inner(p, 0), [total + keep * inner(p, j + 1) for j, total in enumerate(sums)]
            state[p] = (keep, sums)
    return [[keep] + sums for keep, sums in state]


def march_tiles(count, start, prepare, unit):
    def ahead(index, slot):
        return prepare(pl.multiple_of((index + 1) * SUB, SUB), 1 - slot)

    for step in prepare(start * SUB, 0):
        step()

    def pair(i, carry):
        for slot in range(2):
            index = start + 2 * i + slot
            unit(index, slot, ahead(index, slot))
        return carry

    lax.fori_loop(0, count // 2 - 1, pair, 0)
    unit(start + count - 2, 0, ahead(start + count - 2, 0))
    unit(start + count - 1, 1, [])


def mix_kernel(parts, index_ref, lights_ref, curves_ref, own_ref, vector_ref, weight_ref, mixed_ref):
    tiles, cells, _, cols = mixed_ref.shape
    passes = index_ref.shape[0]
    for p in range(passes):
        for axis in range(3):
            vector_ref[p, axis] = jnp.full((SUB, cols), lights_ref[index_ref[p], axis])
    fill_weights(index_ref, curves_ref, OPACITY / (parts * cells), weight_ref)
    places, _, _ = near_places(cells, tiles * SUB, own_ref)

    def tile(i, carry):
        base = pl.multiple_of(i * SUB, SUB)
        for step in mix_steps(range(1, cells - 1), places, base, cols, weight_ref, mixed_ref.at[i]):
            step()
        return carry

    lax.fori_loop(0, tiles, tile, 0)


def own_kernel(parts, flip_ref, vector_ref, own_ref, mixed_ref, lateral_ref, out_ref, *cell_refs):
    rows, cols = out_ref.shape[1:]
    passes = vector_ref.shape[0]
    channels = out_ref.shape[0] // passes
    cells = cell_refs[0].shape[1]
    flip = flip_ref[0]
    inner = range(1, cells - 1)
    where = near_places(cells, rows, own_ref)

    def prepare(base, slot):
        return slope_steps(0, inner, where, lateral_ref, base, cells, rows, parts, cols, None, cell_refs[slot])

    def unit(index, slot, beside):
        base = pl.multiple_of(index * SUB, SUB)
        result = march_unit(flip, vector_ref, inner, cells, cell_refs[slot], mixed_ref.at[index], beside)
        for p in range(passes):
            for j in range(channels):
                out_ref[p * channels + j, pl.ds(base, SUB), :] = result[p][j]

    march_tiles(rows // SUB, 0, prepare, unit)


def near_kernel(parts, flip_ref, vector_ref, weight_ref, inner_ref, *refs):
    count = parts - 1
    heads, laterals, out_ref, ends_ref = refs[:parts], refs[parts : 2 * parts - 1], refs[2 * parts - 1], refs[2 * parts]
    cell_refs, mixed_refs = refs[2 * parts + 1 : 2 * parts + 1 + count], refs[2 * parts + 1 + count :]
    rows, cols = out_ref.shape[2:]
    cells = cell_refs[0].shape[1]
    passes = vector_ref.shape[0]
    channels = inner_ref.shape[0] // passes
    flip = flip_ref[0]
    tiles = rows // SUB
    zs = [(0, cells - 1)] + [range(cells)] * (count - 1)
    places = [near_places(cells, rows, head) for head in heads[:count]]
    fill_ends(parts, cells, rows, heads, ends_ref)

    def prepare(m, base):
        return prepare_steps(
            m, zs[m], places[m], laterals[m], base, cells, rows, parts, cols, ends_ref, weight_ref, cell_refs[m], mixed_refs[m]
        )

    for step in prepare(0, 0):
        step()

    def tile(i, carry):
        base = pl.multiple_of(i * SUB, SUB)
        after = pl.multiple_of(jnp.minimum(i + 1, tiles - 1) * SUB, SUB)
        at = pl.ds(base, SUB)
        for m in range(count):
            beside = prepare(m + 1, base) if m + 1 < count else prepare(0, after)
            inner = (lambda p, j: inner_ref[p * channels + j, at, :]) if m == 0 else None
            result = march_unit(flip, vector_ref, zs[m], cells, cell_refs[m], mixed_refs[m], beside, inner)
            for p in range(passes):
                for j in range(channels):
                    out_ref[m, p * channels + j, at, :] = result[p][j]
        return carry

    lax.fori_loop(0, tiles, tile, 0)


def over_either(first_leads, one, other):
    shape = one[0].shape
    unit = jnp.ones(shape, jnp.float32)
    scale_one = jnp.where(first_leads, unit, other[0])
    scale_other = jnp.where(first_leads, one[0], unit)
    return [one[0] * other[0]] + [scale_one * a + scale_other * b for a, b in zip(one[1:], other[1:])]


def far_kernel(parts, split, low, high, flip_ref, vector_ref, weight_ref, *refs):
    heads, body, refs = refs[:parts], refs[parts], refs[parts + 1 :]
    rest, refs = (refs[0], refs[2:]) if low else (None, refs)
    states, out_ref, picture_ref, ends_ref, sems = refs[:5]
    cell_refs, mixed_refs = refs[5:7], refs[7:]
    channels, rows, cols = out_ref.shape[1:]
    cells = cell_refs[0].shape[1]
    passes = vector_ref.shape[0]
    flip = flip_ref[0]
    me = lax.axis_index("depth")
    places = far_places(cells, rows, parts, split, heads[-1], body, rest)
    fill_ends(parts, cells, rows, heads, ends_ref)
    tiles = range(low // SUB, high // SUB)

    def prepare(base, slot):
        return prepare_steps(
            parts - 1, range(cells), places, body, base, cells, rows, parts, cols, ends_ref, weight_ref, cell_refs[slot], mixed_refs[slot]
        )

    def send(index):
        at = pl.ds(pl.multiple_of(index * SUB, SUB), SUB)
        return pltpu.make_async_copy(picture_ref.at[:, :, at, :], out_ref.at[:, :, at, :], sems.at[index])

    def finish(result, index):
        at = pl.ds(pl.multiple_of(index * SUB, SUB), SUB)
        for p in range(passes):
            images = [[states[m, p * channels + j, at, :] for j in range(channels)] for m in range(parts - 1)]
            images.append(result[p])
            bit = 0
            while len(images) > 1:
                leads = ((me >> bit) & 1) == flip
                images = [over_either(leads, images[j], images[j + 1]) for j in range(0, len(images), 2)]
                bit += 1
            for channel in range(3):
                picture_ref[p, channel, at, :] = images[0][channel + 1]
            picture_ref[p, 3, at, :] = 1.0 - images[0][0]
        send(index).start()

    def unit(index, slot, beside):
        finish(march_unit(flip, vector_ref, range(cells), cells, cell_refs[slot], mixed_refs[slot], beside), index)

    march_tiles(len(tiles), tiles[0], prepare, unit)
    for index in tiles:
        send(index).wait()


def swap_pairs(block, axis, start):
    pairs = [(i, i + 1) for i in range(start, lax.axis_size(axis) - 1, 2)]
    return lax.ppermute(block, axis, pairs + [(j, i) for i, j in pairs])


def swap_along(block, axis, mask):
    return lax.ppermute(block, axis, [(i, i ^ mask) for i in range(lax.axis_size(axis))])


def estimate(micros):
    return pl.CostEstimate(flops=int(micros * 1_000_000_000), transcendentals=0, bytes_accessed=0)


def on_device(field, light_vectors, transfer, light_index, flips):
    parts = lax.axis_size("depth")
    cells, all_rows, cols = field.shape
    rows = all_rows // parts
    passes = light_index.shape[0]
    channels, knots = transfer.shape[1:]
    tiles = rows // SUB
    values = passes * channels
    in_vmem = pl.BlockSpec(memory_space=VMEM)
    in_smem = pl.BlockSpec(memory_space=SMEM)
    in_any = pl.BlockSpec(memory_space=pl.ANY)
    in_hbm = pl.BlockSpec(memory_space=pltpu.HBM)

    def array(*shape):
        return jax.ShapeDtypeStruct(shape, jnp.float32)

    def settings(mib, micros):
        return dict(
            compiler_params=pltpu.CompilerParams(vmem_limit_bytes=mib * MIB),
            cost_estimate=pl.CostEstimate(flops=int(micros * 1e9), transcendentals=0, bytes_accessed=0),
        )

    near_rows = 2 * cells + cells * rows
    head_rows = 2 * cells + 2 * rows
    skip = rows // parts
    split = rows - rows // parts
    body_rows = skip + (cells - 2) * split + cells
    rest_rows = (cells - 2) * (rows - split) + 2 * SUB
    *packed, far_head = pl.pallas_call(
        functools.partial(pack_kernel, parts),
        out_shape=[array(near_rows, cols)] * (parts - 2) + [array(head_rows, cols)],
        in_specs=[in_hbm],
        out_specs=[in_vmem] * (parts - 1),
        scratch_shapes=[VMEM((parts - 1, 2, cells, SUB, cols), jnp.float32), pltpu.SemaphoreType.DMA((6, parts - 1))],
        name="pack",
        **settings(8, 1),
    )(pltpu.with_memory_space_constraint(field, pltpu.HBM))
    near = [swap_along(packed[m - 1], "depth", m) for m in range(1, parts - 1)]

    far_head = swap_along(far_head, "depth", parts - 1)

    edges, own, far_body, far_rest = pl.pallas_call(
        functools.partial(edge_kernel, parts, split),
        out_shape=[array(rows, cols), array(near_rows, cols), array(body_rows, cols), array(rest_rows, cols)],
        in_specs=[in_vmem, in_any],
        out_specs=[in_vmem] * 4,
        name="edges",
        **settings(8, 1),
    )(field, packed[0])
    sides = pl.pallas_call(
        functools.partial(side_kernel, parts),
        out_shape=[array(skip, cols)] * parts,
        in_specs=[in_vmem] * 2 + [in_any],
        out_specs=[in_vmem] * parts,
        name="sides",
        **settings(4, 0.1),
    )(swap_pairs(edges, "tile", 0), swap_pairs(edges, "tile", 1), far_head)
    laterals = [swap_along(sides[m], "depth", m) for m in range(1, parts - 1)]
    far_body = swap_along(lax.dynamic_update_slice(far_body, sides[-1], (0, 0)), "depth", parts - 1)
    *laterals, far_rest = lax.optimization_barrier((*laterals, far_rest))
    far_rest = swap_along(far_rest, "depth", parts - 1)

    cell_shape = VMEM((3, cells, SUB, cols), jnp.float32)
    mixed_shape = VMEM((cells, values * SUB, cols), jnp.float32)
    ends_shape = VMEM((parts + 2, 2, rows, cols), jnp.float32)
    weight_shape = jax.ShapeDtypeStruct((values * SUB, 3 * knots * SUB), jnp.bfloat16)
    vectors, weights, mixed = pl.pallas_call(
        functools.partial(mix_kernel, parts),
        out_shape=[array(passes, 3, SUB, cols), weight_shape, array(tiles, cells, values * SUB, cols)],
        in_specs=[in_smem] * 2 + [in_vmem] * 2,
        out_specs=[in_vmem] * 3,
        name="mix",
        **settings(8, 0.5),
    )(light_index, light_vectors, transfer, own)
    inner = pl.pallas_call(
        functools.partial(own_kernel, parts),
        out_shape=array(values, rows, cols),
        in_specs=[in_smem] + [in_vmem] * 4,
        out_specs=in_vmem,
        scratch_shapes=[cell_shape] * 2,
        name="own",
        **settings(8, 2),
    )(flips, vectors, own, mixed, sides[0])
    states = pl.pallas_call(
        functools.partial(near_kernel, parts),
        out_shape=array(parts - 1, values, rows, cols),
        in_specs=[in_smem] + [in_vmem] * (2 * parts + 2),
        out_specs=in_vmem,
        scratch_shapes=[ends_shape] + [cell_shape] * (parts - 1) + [mixed_shape] * (parts - 1),
        name="near",
        **settings(16, 60),
    )(flips, vectors, weights, inner, own, *near, far_head, sides[0], *laterals)
    picture = None
    for low, high in ((0, split), (split, rows)):
        late = [far_rest, picture] if low else []
        picture = pl.pallas_call(
            functools.partial(far_kernel, parts, split, low, high),
            out_shape=array(passes, channels, rows, cols),
            in_specs=[in_smem] + [in_vmem] * (parts + 3) + [in_vmem, in_any][: len(late)] + [in_vmem],
            out_specs=in_any,
            scratch_shapes=[
                VMEM((passes, channels, rows, cols), jnp.float32),
                ends_shape,
                pltpu.SemaphoreType.DMA((tiles,)),
            ]
            + [cell_shape] * 2
            + [mixed_shape] * 2,
            input_output_aliases={parts + 5: 0} if low else {},
            name="late" if low else "far",
            **settings(16, 2),
        )(flips, vectors, weights, own, *near, far_head, far_body, *late, states)
    return picture


def solution(mesh):
    in_specs = (P("depth", None, "tile"), P(), P(), P(), P("tile"))
    out_specs = P(None, None, "depth", "tile")
    return jax.shard_map(
        on_device, mesh=mesh, in_specs=in_specs, out_specs=out_specs, check_vma=False
    )
```

```python
import functools

import jax
import jax.numpy as jnp
from jax import lax
from jax.experimental import pallas as pl
from jax.experimental.pallas import tpu as pltpu
from jax.sharding import PartitionSpec as P

AMBIENT = 0.3
OPACITY = 2.0
SUB = 8
GROUP = 4
VMEM = pltpu.VMEM
SMEM = pltpu.SMEM
MIB = 1 << 20
FINE = 49152.0
WHOLE = 12582912.0


def pack_kernel(parts, field_ref, *refs):
    outs, (rim_ref, sems) = refs[: parts - 1], refs[parts - 1 :]
    cells, all_rows, cols = field_ref.shape
    rows = all_rows // parts
    me = lax.axis_index("depth")
    copies, rims = [], []
    for j, out in enumerate(outs):
        low = pl.multiple_of((me ^ (j + 1)) * rows, SUB)
        before = pl.multiple_of(jnp.maximum(low - SUB, 0), SUB)
        after = pl.multiple_of(jnp.minimum(low + rows, all_rows - SUB), SUB)
        for side, start in enumerate((before, after)):
            source = field_ref.at[:, pl.ds(start, SUB), :]
            rims.append(pltpu.make_async_copy(source, rim_ref.at[j, side], sems.at[side, j]))
        block = field_ref.at[:, pl.ds(low, rows), :]
        if j < parts - 2:
            centre = out.at[pl.ds(cells, cells * rows), :].reshape(cells, rows, cols)
            quarter = cells // 4
            for q in range(4):
                layers = pl.ds(q * quarter, quarter)
                copies.append(pltpu.make_async_copy(block.at[layers], centre.at[layers], sems.at[2 + q, j]))
        else:
            for side in range(2):
                layer = out.at[pl.ds(cells + side * rows, rows), :]
                copies.append(pltpu.make_async_copy(block.at[side * (cells - 1)], layer, sems.at[2 + side, j]))
    for copy in rims + copies:
        copy.start()
    for copy in rims:
        copy.wait()
    for j, out in enumerate(outs):
        part = me ^ (j + 1)
        above = jnp.where(part > 0, 1.0, 0.0)
        below = jnp.where(part < parts - 1, 1.0, 0.0)
        for z in range(cells):
            out[z : z + 1, :] = rim_ref[j, 0, z, SUB - 1 : SUB, :] * above
            below_at = out.shape[0] - cells + z
            out[below_at : below_at + 1, :] = rim_ref[j, 1, z, 0:1, :] * below
    for copy in copies:
        copy.wait()


def edge_kernel(parts, split, field_ref, _, edge_ref, own_ref, body_ref, rest_ref):
    cells, all_rows, cols = field_ref.shape
    rows = all_rows // parts
    me = lax.axis_index("depth")
    lane_pair = lax.broadcasted_iota(jnp.int32, (SUB, cols), 1) // 2

    def tile(i, carry):
        acc = jnp.zeros((SUB, cols), jnp.float32)
        for part in range(parts):
            for z in range(cells):
                slot = part * cells + z
                start = pl.multiple_of(part * rows + i * SUB, SUB)
                value = field_ref[z, pl.ds(start, SUB), :]
                moved = pltpu.roll(value, (2 * slot + 1) % cols, 1)
                acc = jnp.where(lane_pair == slot, moved, acc)
        edge_ref[pl.ds(pl.multiple_of(i * SUB, SUB), SUB), :] = acc
        return carry

    lax.fori_loop(0, rows // SUB, tile, 0)
    low = pl.multiple_of(me * rows, SUB)
    above = jnp.where(me > 0, 1.0, 0.0)
    below = jnp.where(me < parts - 1, 1.0, 0.0)
    for z in range(cells):
        own_ref[z : z + 1, :] = field_ref[z, pl.ds(jnp.maximum(low - 1, 0), 1), :] * above
        below_at = cells + cells * rows + z
        own_ref[below_at : below_at + 1, :] = field_ref[z, pl.ds(jnp.minimum(low + rows, all_rows - 1), 1), :] * below
    far_low = pl.multiple_of((me ^ (parts - 1)) * rows, SUB)
    own_places, _, _ = near_places(cells, rows, own_ref)
    for z in range(cells):
        ref, start = own_places[z]
        ref[start : start + rows, :] = field_ref[z, pl.ds(low, rows), :]
    skip, more = rows // parts, rows - split
    for z in range(1, cells - 1):
        at = skip + (z - 1) * split
        body_ref[at : at + split, :] = field_ref[z, pl.ds(far_low, split), :]
        next_row = skip + (cells - 2) * split + z - 1
        body_ref[next_row : next_row + 1, :] = field_ref[z, pl.ds(far_low + split, 1), :]
        at = SUB + (z - 1) * more
        rest_ref[at : at + more, :] = field_ref[z, pl.ds(far_low + split, more), :]


def side_kernel(parts, even_ref, odd_ref, _, *outs):
    rows, cols = even_ref.shape
    group = rows // parts
    width = cols // parts
    me = lax.axis_index("depth")
    lane = lax.broadcasted_iota(jnp.int32, (rows, cols), 1)
    tile = lax.axis_index("tile")
    sides = jnp.where((lane + tile) % 2 == 1, even_ref[...], odd_ref[...])
    for m in range(parts):
        acc = jnp.zeros((group, cols), jnp.float32)
        for j in range(parts):
            moved = pltpu.roll(sides[j * group : (j + 1) * group], (j - (me ^ m) + parts) * width % cols, 1)
            acc = jnp.where(lane[:group] // width == j, moved, acc)
        outs[m][...] = acc


def near_places(cells, rows, head):
    count = head.shape[0]
    places = [(head, cells + z * rows) for z in range(cells)]
    tops = [(0, head, z) for z in range(cells)]
    bottoms = [(rows - SUB, head, count - cells + z) for z in range(cells)]
    return places, tops, bottoms


def far_places(cells, rows, parts, split, head, body, rest=None):
    skip, more = rows // parts, rows - split
    places, tops, bottoms = near_places(cells, rows, head)
    places[0], places[-1] = (head, cells), (head, cells + rows)
    for z in range(1, cells - 1):
        if rest is None:
            places[z] = (body, skip + (z - 1) * split)
            bottoms[z] = (split - SUB, body, skip + (cells - 2) * split + z - 1)
        else:
            places[z] = (rest, SUB + (z - 1) * more - split)
            tops[z] = (split, body, skip + z * split - 1)
    return places, tops, bottoms


def fill_ends(parts, cells, rows, heads, ends_ref):
    me = lax.axis_index("depth")
    ends_ref[0, 1] = jnp.zeros_like(ends_ref[0, 1])
    ends_ref[parts + 1, 0] = jnp.zeros_like(ends_ref[0, 0])
    for m in range(parts):
        last = (cells - 1) * rows if m < parts - 1 else rows
        ends_ref[(me ^ m) + 1, 0] = heads[m][cells : cells + rows, :]
        ends_ref[(me ^ m) + 1, 1] = heads[m][cells + last : cells + last + rows, :]


def fill_weights(index_ref, curves_ref, scale, weight_ref):
    passes = index_ref.shape[0]
    channels, knots = curves_ref.shape[1:]
    width = weight_ref.shape[1]
    block = knots * SUB
    points = jnp.concatenate([curves_ref[index_ref[p]] for p in range(passes)], axis=0)
    channel = lax.broadcasted_iota(jnp.int32, points.shape, 0) % channels
    points = jnp.where(channel == channels - 1, points * scale, points)
    knot = lax.broadcasted_iota(jnp.int32, (knots, width), 0)
    lane = lax.broadcasted_iota(jnp.int32, (knots, width), 1)
    target = lane // SUB % knots
    here = jnp.where(knot == target, 1.0, 0.0)
    after = jnp.where(knot == target + 1, 1.0, 0.0)
    is_slope = jnp.logical_and(lane >= block, lane < 2 * block)
    spread = jnp.where(is_slope, after - here, here)
    values = jnp.dot(points, spread, precision=lax.Precision.HIGHEST, preferred_element_type=jnp.float32)
    shape = (2 * SUB, width)
    row = lax.broadcasted_iota(jnp.int32, shape, 0)
    lane = lax.broadcasted_iota(jnp.int32, shape, 1)
    on_row = lane % SUB == row % SUB
    for pair in range(passes * channels // 2):
        upper, lower = [jnp.broadcast_to(values[2 * pair + j : 2 * pair + j + 1], shape) for j in range(2)]
        value = jnp.where(on_row, jnp.where(row < SUB, upper, lower), 0.0)
        coarse = value.astype(jnp.bfloat16).astype(jnp.float32)
        value = jnp.where(lane < 2 * block, value, value - coarse)
        weight_ref[2 * pair * SUB : 2 * (pair + 1) * SUB, :] = value.astype(jnp.bfloat16)


def mix_steps(zs, places, base, cols, weight_ref, mixed_ref):
    knots = weight_ref.shape[1] // (3 * SUB)
    half = 0.5 * (knots - 1)
    row = lax.broadcasted_iota(jnp.int32, (2 * SUB, cols), 0)
    knot_at = [jnp.where(row < SUB, 0.0 + k, 1.0 + k).astype(jnp.bfloat16) for k in range(0, knots, 2)]
    zero = jnp.zeros((2 * SUB, cols), jnp.bfloat16)

    def twice(value):
        return jnp.concatenate([value, value], axis=0).astype(jnp.bfloat16)

    def basis(z):
        ref, low = places[z]
        scaled = half * jnp.tanh(0.5 * ref[pl.ds(low + base, SUB), :])
        position = scaled + half
        segment = ((scaled + (half - 0.5)) + WHOLE) - WHOLE
        coarse = (position + FINE) - FINE
        right = coarse - segment
        left, right, rest = twice(1.0 - right), twice(right), twice(position - coarse)
        here = twice(segment)
        after = twice(segment + 1.0)
        tents, rests = [], []
        for at in knot_at:
            is_here = here == at
            tents.append(jnp.where(is_here, left, jnp.where(after == at, right, zero)))
            rests.append(jnp.where(is_here, rest, zero))
        return [jnp.concatenate(part, axis=0) for part in (tents, rests)]

    def several(group):
        tents, rests = [jnp.concatenate(parts, axis=1) for parts in zip(*[basis(z) for z in group])]
        right = jnp.concatenate([tents, rests, tents], axis=0)
        mixed = jnp.dot(weight_ref[...], right, preferred_element_type=jnp.float32)
        for j, z in enumerate(group):
            mixed_ref[z] = mixed[:, j * cols : (j + 1) * cols]

    zs = list(zs)
    return [functools.partial(several, zs[i : i + GROUP]) for i in range(0, len(zs), GROUP)]


def slope_steps(m, zs, where, lateral, base, cells, rows, parts, cols, ends_ref, cell_ref):
    places, tops, bottoms = where
    me = lax.axis_index("depth")
    part = me ^ m
    at = pl.ds(base, SUB)
    lane = lax.broadcasted_iota(jnp.int32, (SUB, cols), 1)
    sublane = lax.broadcasted_iota(jnp.int32, (SUB, cols), 0)
    is_first = lane == 0
    is_last = lane == cols - 1
    is_top = {low: jnp.logical_and(sublane == 0, base == low) for low in sorted({top[0] for top in tops})}
    is_bottom = {
        low: jnp.logical_and(sublane == SUB - 1, base == low) for low in sorted({bottom[0] for bottom in bottoms})
    }
    group = rows // parts
    got = lateral[pl.ds(pl.multiple_of(base % group, SUB), SUB), :]
    sides = pltpu.roll(got, (2 * cols - 1 - base // group * (cols // parts)) % cols, 1)

    def layer(z):
        if z < 0:
            return ends_ref[part, 1, at, :]
        if z == cells:
            return ends_ref[part + 2, 0, at, :]
        ref, low = places[z]
        return ref[pl.ds(low + base, SUB), :]

    def step(z):
        ref, low = places[z]
        here = layer(z)
        top_at, top_ref, top = tops[z]
        bottom_at, bottom_ref, bottom = bottoms[z]
        upper = jnp.where(is_top[top_at], top_ref[top : top + 1, :], ref[pl.ds(low + base - 1, SUB), :])
        lower = jnp.where(is_bottom[bottom_at], bottom_ref[bottom : bottom + 1, :], ref[pl.ds(low + base + 1, SUB), :])
        edge = pltpu.roll(sides, (cols - 2 * z) % cols, 1) if z else sides
        grad_x = pltpu.roll(jnp.where(is_first, edge, here), cols - 1, 1) - pltpu.roll(
            jnp.where(is_last, edge, here), 1, 1
        )
        grad_y = lower - upper
        grad_z = layer(z + 1) - layer(z - 1)
        inverse = lax.rsqrt(grad_x * grad_x + grad_y * grad_y + grad_z * grad_z + 4.0)
        cell_ref[0, z] = grad_x * inverse
        cell_ref[1, z] = grad_y * inverse
        cell_ref[2, z] = grad_z * inverse

    return [functools.partial(step, z) for z in zs]


def prepare_steps(m, zs, where, lateral, base, cells, rows, parts, cols, ends_ref, weight_ref, cell_ref, mixed_ref):
    slopes = slope_steps(m, zs, where, lateral, base, cells, rows, parts, cols, ends_ref, cell_ref)
    mixes = mix_steps(zs, where[0], base, cols, weight_ref, mixed_ref)

    def both(i):
        mixes[i]()
        for step in slopes[GROUP * i : GROUP * (i + 1)]:
            step()

    return [functools.partial(both, i) for i in range(len(mixes))]


def march_unit(flip, vector_ref, zs, cells, cell_ref, mixed_ref, beside, inner=None):
    passes = vector_ref.shape[0]
    channels = mixed_ref.shape[1] // (passes * SUB)
    shape = vector_ref.shape[2:]
    vectors = [[vector_ref[p, axis] for axis in range(3)] for p in range(passes)]
    state = [(jnp.ones(shape, jnp.float32), [jnp.zeros(shape, jnp.float32)] * 3)] * passes
    count = len(beside)
    for u, spot in enumerate(zs):
        for step in beside[u * count // len(zs) : (u + 1) * count // len(zs)]:
            step()
        z = spot + flip * (cells - 1 - 2 * spot)
        normal = [cell_ref[axis, z] for axis in range(3)]
        for p in range(passes):
            keep, sums = state[p]
            mixed = [mixed_ref[z, (p * channels + c) * SUB : (p * channels + c + 1) * SUB, :] for c in range(channels)]
            facing = normal[0] * vectors[p][0] + normal[1] * vectors[p][1] + normal[2] * vectors[p][2]
            taken = keep * mixed[3]
            weight = taken * (AMBIENT + jnp.abs(facing))
            sums = [total + weight * tint for total, tint in zip(sums, mixed)]
            keep = keep - taken
            if inner is not None and u == 0:
                keep, sums = keep * inner(p, 0), [total + keep * inner(p, j + 1) for j, total in enumerate(sums)]
            state[p] = (keep, sums)
    return [[keep] + sums for keep, sums in state]


def march_tiles(count, start, prepare, unit):
    def ahead(index, slot):
        return prepare(pl.multiple_of((index + 1) * SUB, SUB), 1 - slot)

    for step in prepare(start * SUB, 0):
        step()

    def pair(i, carry):
        for slot in range(2):
            index = start + 2 * i + slot
            unit(index, slot, ahead(index, slot))
        return carry

    lax.fori_loop(0, count // 2 - 1, pair, 0)
    unit(start + count - 2, 0, ahead(start + count - 2, 0))
    unit(start + count - 1, 1, [])


def mix_kernel(parts, index_ref, lights_ref, curves_ref, own_ref, vector_ref, weight_ref, mixed_ref):
    tiles, cells, _, cols = mixed_ref.shape
    passes = index_ref.shape[0]
    for p in range(passes):
        for axis in range(3):
            vector_ref[p, axis] = jnp.full((SUB, cols), lights_ref[index_ref[p], axis])
    fill_weights(index_ref, curves_ref, OPACITY / (parts * cells), weight_ref)
    places, _, _ = near_places(cells, tiles * SUB, own_ref)

    def tile(i, carry):
        base = pl.multiple_of(i * SUB, SUB)
        for step in mix_steps(range(1, cells - 1), places, base, cols, weight_ref, mixed_ref.at[i]):
            step()
        return carry

    lax.fori_loop(0, tiles, tile, 0)


def own_kernel(parts, flip_ref, vector_ref, own_ref, mixed_ref, lateral_ref, out_ref, *cell_refs):
    rows, cols = out_ref.shape[1:]
    passes = vector_ref.shape[0]
    channels = out_ref.shape[0] // passes
    cells = cell_refs[0].shape[1]
    flip = flip_ref[0]
    inner = range(1, cells - 1)
    where = near_places(cells, rows, own_ref)

    def prepare(base, slot):
        return slope_steps(0, inner, where, lateral_ref, base, cells, rows, parts, cols, None, cell_refs[slot])

    def unit(index, slot, beside):
        base = pl.multiple_of(index * SUB, SUB)
        result = march_unit(flip, vector_ref, inner, cells, cell_refs[slot], mixed_ref.at[index], beside)
        for p in range(passes):
            for j in range(channels):
                out_ref[p * channels + j, pl.ds(base, SUB), :] = result[p][j]

    march_tiles(rows // SUB, 0, prepare, unit)


def near_kernel(parts, flip_ref, vector_ref, weight_ref, inner_ref, *refs):
    count = parts - 1
    heads, laterals, out_ref, ends_ref = refs[:parts], refs[parts : 2 * parts - 1], refs[2 * parts - 1], refs[2 * parts]
    cell_refs, mixed_refs = refs[2 * parts + 1 : 2 * parts + 1 + count], refs[2 * parts + 1 + count :]
    rows, cols = out_ref.shape[2:]
    cells = cell_refs[0].shape[1]
    passes = vector_ref.shape[0]
    channels = inner_ref.shape[0] // passes
    flip = flip_ref[0]
    tiles = rows // SUB
    zs = [(0, cells - 1)] + [range(cells)] * (count - 1)
    places = [near_places(cells, rows, head) for head in heads[:count]]
    fill_ends(parts, cells, rows, heads, ends_ref)

    def prepare(m, base):
        return prepare_steps(
            m, zs[m], places[m], laterals[m], base, cells, rows, parts, cols, ends_ref, weight_ref, cell_refs[m], mixed_refs[m]
        )

    for step in prepare(0, 0):
        step()

    def tile(i, carry):
        base = pl.multiple_of(i * SUB, SUB)
        after = pl.multiple_of(jnp.minimum(i + 1, tiles - 1) * SUB, SUB)
        at = pl.ds(base, SUB)
        for m in range(count):
            beside = prepare(m + 1, base) if m + 1 < count else prepare(0, after)
            inner = (lambda p, j: inner_ref[p * channels + j, at, :]) if m == 0 else None
            result = march_unit(flip, vector_ref, zs[m], cells, cell_refs[m], mixed_refs[m], beside, inner)
            for p in range(passes):
                for j in range(channels):
                    out_ref[m, p * channels + j, at, :] = result[p][j]
        return carry

    lax.fori_loop(0, tiles, tile, 0)


def over_either(first_leads, one, other):
    shape = one[0].shape
    unit = jnp.ones(shape, jnp.float32)
    scale_one = jnp.where(first_leads, unit, other[0])
    scale_other = jnp.where(first_leads, one[0], unit)
    return [one[0] * other[0]] + [scale_one * a + scale_other * b for a, b in zip(one[1:], other[1:])]


def far_kernel(parts, split, low, high, flip_ref, vector_ref, weight_ref, *refs):
    heads, body, refs = refs[:parts], refs[parts], refs[parts + 1 :]
    rest, refs = (refs[0], refs[2:]) if low else (None, refs)
    states, out_ref, picture_ref, ends_ref, sems = refs[:5]
    cell_refs, mixed_refs = refs[5:7], refs[7:]
    channels, rows, cols = out_ref.shape[1:]
    cells = cell_refs[0].shape[1]
    passes = vector_ref.shape[0]
    flip = flip_ref[0]
    me = lax.axis_index("depth")
    places = far_places(cells, rows, parts, split, heads[-1], body, rest)
    fill_ends(parts, cells, rows, heads, ends_ref)
    tiles = range(low // SUB, high // SUB)

    def prepare(base, slot):
        return prepare_steps(
            parts - 1, range(cells), places, body, base, cells, rows, parts, cols, ends_ref, weight_ref, cell_refs[slot], mixed_refs[slot]
        )

    def send(index):
        at = pl.ds(pl.multiple_of(index * SUB, SUB), SUB)
        return pltpu.make_async_copy(picture_ref.at[:, :, at, :], out_ref.at[:, :, at, :], sems.at[index])

    def finish(result, index):
        at = pl.ds(pl.multiple_of(index * SUB, SUB), SUB)
        for p in range(passes):
            images = [[states[m, p * channels + j, at, :] for j in range(channels)] for m in range(parts - 1)]
            images.append(result[p])
            bit = 0
            while len(images) > 1:
                leads = ((me >> bit) & 1) == flip
                images = [over_either(leads, images[j], images[j + 1]) for j in range(0, len(images), 2)]
                bit += 1
            for channel in range(3):
                picture_ref[p, channel, at, :] = images[0][channel + 1]
            picture_ref[p, 3, at, :] = 1.0 - images[0][0]
        send(index).start()

    def unit(index, slot, beside):
        finish(march_unit(flip, vector_ref, range(cells), cells, cell_refs[slot], mixed_refs[slot], beside), index)

    march_tiles(len(tiles), tiles[0], prepare, unit)
    for index in tiles:
        send(index).wait()


def swap_pairs(block, axis, start):
    pairs = [(i, i + 1) for i in range(start, lax.axis_size(axis) - 1, 2)]
    return lax.ppermute(block, axis, pairs + [(j, i) for i, j in pairs])


def swap_along(block, axis, mask):
    return lax.ppermute(block, axis, [(i, i ^ mask) for i in range(lax.axis_size(axis))])


def estimate(micros):
    return pl.CostEstimate(flops=int(micros * 1_000_000_000), transcendentals=0, bytes_accessed=0)


def on_device(field, light_vectors, transfer, light_index, flips):
    parts = lax.axis_size("depth")
    cells, all_rows, cols = field.shape
    rows = all_rows // parts
    passes = light_index.shape[0]
    channels, knots = transfer.shape[1:]
    tiles = rows // SUB
    values = passes * channels
    in_vmem = pl.BlockSpec(memory_space=VMEM)
    in_smem = pl.BlockSpec(memory_space=SMEM)
    in_any = pl.BlockSpec(memory_space=pl.ANY)
    in_hbm = pl.BlockSpec(memory_space=pltpu.HBM)

    def array(*shape):
        return jax.ShapeDtypeStruct(shape, jnp.float32)

    def settings(mib, micros):
        return dict(
            compiler_params=pltpu.CompilerParams(vmem_limit_bytes=mib * MIB),
            cost_estimate=pl.CostEstimate(flops=int(micros * 1e9), transcendentals=0, bytes_accessed=0),
        )

    near_rows = 2 * cells + cells * rows
    head_rows = 2 * cells + 2 * rows
    skip = rows // parts
    split = rows - rows // parts
    body_rows = skip + (cells - 2) * split + cells
    rest_rows = (cells - 2) * (rows - split) + 2 * SUB
    *packed, far_head = pl.pallas_call(
        functools.partial(pack_kernel, parts),
        out_shape=[array(near_rows, cols)] * (parts - 2) + [array(head_rows, cols)],
        in_specs=[in_hbm],
        out_specs=[in_vmem] * (parts - 1),
        scratch_shapes=[VMEM((parts - 1, 2, cells, SUB, cols), jnp.float32), pltpu.SemaphoreType.DMA((6, parts - 1))],
        name="pack",
        **settings(8, 1),
    )(pltpu.with_memory_space_constraint(field, pltpu.HBM))
    near = [swap_along(packed[m - 1], "depth", m) for m in range(1, parts - 1)]

    far_head = swap_along(far_head, "depth", parts - 1)

    edges, own, far_body, far_rest = pl.pallas_call(
        functools.partial(edge_kernel, parts, split),
        out_shape=[array(rows, cols), array(near_rows, cols), array(body_rows, cols), array(rest_rows, cols)],
        in_specs=[in_vmem, in_any],
        out_specs=[in_vmem] * 4,
        name="edges",
        **settings(8, 1),
    )(field, packed[0])
    sides = pl.pallas_call(
        functools.partial(side_kernel, parts),
        out_shape=[array(skip, cols)] * parts,
        in_specs=[in_vmem] * 2 + [in_any],
        out_specs=[in_vmem] * parts,
        name="sides",
        **settings(4, 0.1),
    )(swap_pairs(edges, "tile", 0), swap_pairs(edges, "tile", 1), far_head)
    laterals = [swap_along(sides[m], "depth", m) for m in range(1, parts - 1)]
    far_body = swap_along(lax.dynamic_update_slice(far_body, sides[-1], (0, 0)), "depth", parts - 1)
    *laterals, far_rest = lax.optimization_barrier((*laterals, far_rest))
    far_rest = swap_along(far_rest, "depth", parts - 1)

    cell_shape = VMEM((3, cells, SUB, cols), jnp.float32)
    mixed_shape = VMEM((cells, values * SUB, cols), jnp.float32)
    ends_shape = VMEM((parts + 2, 2, rows, cols), jnp.float32)
    weight_shape = jax.ShapeDtypeStruct((values * SUB, 3 * knots * SUB), jnp.bfloat16)
    vectors, weights, mixed = pl.pallas_call(
        functools.partial(mix_kernel, parts),
        out_shape=[array(passes, 3, SUB, cols), weight_shape, array(tiles, cells, values * SUB, cols)],
        in_specs=[in_smem] * 2 + [in_vmem] * 2,
        out_specs=[in_vmem] * 3,
        name="mix",
        **settings(8, 0.01),
    )(light_index, light_vectors, transfer, own)
    inner = pl.pallas_call(
        functools.partial(own_kernel, parts),
        out_shape=array(values, rows, cols),
        in_specs=[in_smem] + [in_vmem] * 4,
        out_specs=in_vmem,
        scratch_shapes=[cell_shape] * 2,
        name="own",
        **settings(8, 4),
    )(flips, vectors, own, mixed, sides[0])
    states = pl.pallas_call(
        functools.partial(near_kernel, parts),
        out_shape=array(parts - 1, values, rows, cols),
        in_specs=[in_smem] + [in_vmem] * (2 * parts + 2),
        out_specs=in_vmem,
        scratch_shapes=[ends_shape] + [cell_shape] * (parts - 1) + [mixed_shape] * (parts - 1),
        name="near",
        **settings(16, 60),
    )(flips, vectors, weights, inner, own, *near, far_head, sides[0], *laterals)
    picture = None
    for low, high in ((0, split), (split, rows)):
        late = [far_rest, picture] if low else []
        picture = pl.pallas_call(
            functools.partial(far_kernel, parts, split, low, high),
            out_shape=array(passes, channels, rows, cols),
            in_specs=[in_smem] + [in_vmem] * (parts + 3) + [in_vmem, in_any][: len(late)] + [in_vmem],
            out_specs=in_any,
            scratch_shapes=[
                VMEM((passes, channels, rows, cols), jnp.float32),
                ends_shape,
                pltpu.SemaphoreType.DMA((tiles,)),
            ]
            + [cell_shape] * 2
            + [mixed_shape] * 2,
            input_output_aliases={parts + 5: 0} if low else {},
            name="late" if low else "far",
            **settings(16, 2),
        )(flips, vectors, weights, own, *near, far_head, far_body, *late, states)
    return picture


def solution(mesh):
    in_specs = (P("depth", None, "tile"), P(), P(), P(), P("tile"))
    out_specs = P(None, None, "depth", "tile")
    return jax.shard_map(
        on_device, mesh=mesh, in_specs=in_specs, out_specs=out_specs, check_vma=False
    )
```

```python
import functools

import jax
import jax.numpy as jnp
from jax import lax
from jax.experimental import pallas as pl
from jax.experimental.pallas import tpu as pltpu
from jax.sharding import PartitionSpec as P

AMBIENT = 0.3
OPACITY = 2.0
SUB = 8
GROUP = 4
VMEM = pltpu.VMEM
SMEM = pltpu.SMEM
MIB = 1 << 20
FINE = 49152.0
WHOLE = 12582912.0


def pack_kernel(parts, field_ref, *refs):
    outs, (rim_ref, sems) = refs[: parts - 1], refs[parts - 1 :]
    cells, all_rows, cols = field_ref.shape
    rows = all_rows // parts
    me = lax.axis_index("depth")
    copies, rims = [], []
    for j, out in enumerate(outs):
        low = pl.multiple_of((me ^ (j + 1)) * rows, SUB)
        before = pl.multiple_of(jnp.maximum(low - SUB, 0), SUB)
        after = pl.multiple_of(jnp.minimum(low + rows, all_rows - SUB), SUB)
        for side, start in enumerate((before, after)):
            source = field_ref.at[:, pl.ds(start, SUB), :]
            rims.append(pltpu.make_async_copy(source, rim_ref.at[j, side], sems.at[side, j]))
        block = field_ref.at[:, pl.ds(low, rows), :]
        if j < parts - 2:
            centre = out.at[pl.ds(cells, cells * rows), :].reshape(cells, rows, cols)
            quarter = cells // 4
            for q in range(4):
                layers = pl.ds(q * quarter, quarter)
                copies.append(pltpu.make_async_copy(block.at[layers], centre.at[layers], sems.at[2 + q, j]))
        else:
            for side in range(2):
                layer = out.at[pl.ds(cells + side * rows, rows), :]
                copies.append(pltpu.make_async_copy(block.at[side * (cells - 1)], layer, sems.at[2 + side, j]))
    for copy in rims + copies:
        copy.start()
    for copy in rims:
        copy.wait()
    for j, out in enumerate(outs):
        part = me ^ (j + 1)
        above = jnp.where(part > 0, 1.0, 0.0)
        below = jnp.where(part < parts - 1, 1.0, 0.0)
        for z in range(cells):
            out[z : z + 1, :] = rim_ref[j, 0, z, SUB - 1 : SUB, :] * above
            below_at = out.shape[0] - cells + z
            out[below_at : below_at + 1, :] = rim_ref[j, 1, z, 0:1, :] * below
    for copy in copies:
        copy.wait()


def edge_kernel(parts, split, source_ref, _, edge_ref, own_ref, body_ref, rest_ref, field_ref, sems):
    cells, all_rows, cols = field_ref.shape
    rows = all_rows // parts
    me = lax.axis_index("depth")
    quarter = cells // 4
    copies = []
    for q in range(4):
        layers = pl.ds(q * quarter, quarter)
        copies.append(pltpu.make_async_copy(source_ref.at[layers], field_ref.at[layers], sems.at[q]))
        copies[-1].start()
    lane_pair = lax.broadcasted_iota(jnp.int32, (SUB, cols), 1) // 2

    def tile(i, carry):
        acc = jnp.zeros((SUB, cols), jnp.float32)
        for part in range(parts):
            for z in range(cells):
                slot = part * cells + z
                start = pl.multiple_of(part * rows + i * SUB, SUB)
                value = field_ref[z, pl.ds(start, SUB), :]
                moved = pltpu.roll(value, (2 * slot + 1) % cols, 1)
                acc = jnp.where(lane_pair == slot, moved, acc)
        edge_ref[pl.ds(pl.multiple_of(i * SUB, SUB), SUB), :] = acc
        return carry

    low = pl.multiple_of(me * rows, SUB)
    above = jnp.where(me > 0, 1.0, 0.0)
    below = jnp.where(me < parts - 1, 1.0, 0.0)
    for z in range(cells):
        if z % quarter == 0:
            copies[z // quarter].wait()
        own_ref[z : z + 1, :] = field_ref[z, pl.ds(jnp.maximum(low - 1, 0), 1), :] * above
        below_at = cells + cells * rows + z
        own_ref[below_at : below_at + 1, :] = field_ref[z, pl.ds(jnp.minimum(low + rows, all_rows - 1), 1), :] * below
    far_low = pl.multiple_of((me ^ (parts - 1)) * rows, SUB)
    own_places, _, _ = near_places(cells, rows, own_ref)
    for z in range(cells):
        ref, start = own_places[z]
        ref[start : start + rows, :] = field_ref[z, pl.ds(low, rows), :]
    skip, more = rows // parts, rows - split
    for z in range(1, cells - 1):
        at = skip + (z - 1) * split
        body_ref[at : at + split, :] = field_ref[z, pl.ds(far_low, split), :]
        next_row = skip + (cells - 2) * split + z - 1
        body_ref[next_row : next_row + 1, :] = field_ref[z, pl.ds(far_low + split, 1), :]
        at = SUB + (z - 1) * more
        rest_ref[at : at + more, :] = field_ref[z, pl.ds(far_low + split, more), :]
    lax.fori_loop(0, rows // SUB, tile, 0)


def side_kernel(parts, even_ref, odd_ref, _, *outs):
    rows, cols = even_ref.shape
    group = rows // parts
    width = cols // parts
    me = lax.axis_index("depth")
    lane = lax.broadcasted_iota(jnp.int32, (rows, cols), 1)
    tile = lax.axis_index("tile")
    sides = jnp.where((lane + tile) % 2 == 1, even_ref[...], odd_ref[...])
    for m in range(parts):
        acc = jnp.zeros((group, cols), jnp.float32)
        for j in range(parts):
            moved = pltpu.roll(sides[j * group : (j + 1) * group], (j - (me ^ m) + parts) * width % cols, 1)
            acc = jnp.where(lane[:group] // width == j, moved, acc)
        outs[m][...] = acc


def near_places(cells, rows, head):
    count = head.shape[0]
    places = [(head, cells + z * rows) for z in range(cells)]
    tops = [(0, head, z) for z in range(cells)]
    bottoms = [(rows - SUB, head, count - cells + z) for z in range(cells)]
    return places, tops, bottoms


def far_places(cells, rows, parts, split, head, body, rest=None):
    skip, more = rows // parts, rows - split
    places, tops, bottoms = near_places(cells, rows, head)
    places[0], places[-1] = (head, cells), (head, cells + rows)
    for z in range(1, cells - 1):
        if rest is None:
            places[z] = (body, skip + (z - 1) * split)
            bottoms[z] = (split - SUB, body, skip + (cells - 2) * split + z - 1)
        else:
            places[z] = (rest, SUB + (z - 1) * more - split)
            tops[z] = (split, body, skip + z * split - 1)
    return places, tops, bottoms


def fill_ends(parts, cells, rows, heads, ends_ref):
    me = lax.axis_index("depth")
    ends_ref[0, 1] = jnp.zeros_like(ends_ref[0, 1])
    ends_ref[parts + 1, 0] = jnp.zeros_like(ends_ref[0, 0])
    for m in range(parts):
        last = (cells - 1) * rows if m < parts - 1 else rows
        ends_ref[(me ^ m) + 1, 0] = heads[m][cells : cells + rows, :]
        ends_ref[(me ^ m) + 1, 1] = heads[m][cells + last : cells + last + rows, :]


def fill_weights(index_ref, curves_ref, scale, weight_ref):
    passes = index_ref.shape[0]
    channels, knots = curves_ref.shape[1:]
    width = weight_ref.shape[1]
    block = knots * SUB
    points = jnp.concatenate([curves_ref[index_ref[p]] for p in range(passes)], axis=0)
    channel = lax.broadcasted_iota(jnp.int32, points.shape, 0) % channels
    points = jnp.where(channel == channels - 1, points * scale, points)
    knot = lax.broadcasted_iota(jnp.int32, (knots, width), 0)
    lane = lax.broadcasted_iota(jnp.int32, (knots, width), 1)
    target = lane // SUB % knots
    here = jnp.where(knot == target, 1.0, 0.0)
    after = jnp.where(knot == target + 1, 1.0, 0.0)
    is_slope = jnp.logical_and(lane >= block, lane < 2 * block)
    spread = jnp.where(is_slope, after - here, here)
    values = jnp.dot(points, spread, precision=lax.Precision.HIGHEST, preferred_element_type=jnp.float32)
    shape = (2 * SUB, width)
    row = lax.broadcasted_iota(jnp.int32, shape, 0)
    lane = lax.broadcasted_iota(jnp.int32, shape, 1)
    on_row = lane % SUB == row % SUB
    for pair in range(passes * channels // 2):
        upper, lower = [jnp.broadcast_to(values[2 * pair + j : 2 * pair + j + 1], shape) for j in range(2)]
        value = jnp.where(on_row, jnp.where(row < SUB, upper, lower), 0.0)
        coarse = value.astype(jnp.bfloat16).astype(jnp.float32)
        value = jnp.where(lane < 2 * block, value, value - coarse)
        weight_ref[2 * pair * SUB : 2 * (pair + 1) * SUB, :] = value.astype(jnp.bfloat16)


def mix_steps(zs, places, base, cols, weight_ref, mixed_ref):
    knots = weight_ref.shape[1] // (3 * SUB)
    half = 0.5 * (knots - 1)
    row = lax.broadcasted_iota(jnp.int32, (2 * SUB, cols), 0)
    knot_at = [jnp.where(row < SUB, 0.0 + k, 1.0 + k).astype(jnp.bfloat16) for k in range(0, knots, 2)]
    zero = jnp.zeros((2 * SUB, cols), jnp.bfloat16)

    def twice(value):
        return jnp.concatenate([value, value], axis=0).astype(jnp.bfloat16)

    def basis(z):
        ref, low = places[z]
        scaled = half * jnp.tanh(0.5 * ref[pl.ds(low + base, SUB), :])
        position = scaled + half
        segment = ((scaled + (half - 0.5)) + WHOLE) - WHOLE
        coarse = (position + FINE) - FINE
        right = coarse - segment
        left, right, rest = twice(1.0 - right), twice(right), twice(position - coarse)
        here = twice(segment)
        after = twice(segment + 1.0)
        tents, rests = [], []
        for at in knot_at:
            is_here = here == at
            tents.append(jnp.where(is_here, left, jnp.where(after == at, right, zero)))
            rests.append(jnp.where(is_here, rest, zero))
        return [jnp.concatenate(part, axis=0) for part in (tents, rests)]

    def several(group):
        tents, rests = [jnp.concatenate(parts, axis=1) for parts in zip(*[basis(z) for z in group])]
        right = jnp.concatenate([tents, rests, tents], axis=0)
        mixed = jnp.dot(weight_ref[...], right, preferred_element_type=jnp.float32)
        for j, z in enumerate(group):
            mixed_ref[z] = mixed[:, j * cols : (j + 1) * cols]

    zs = list(zs)
    return [functools.partial(several, zs[i : i + GROUP]) for i in range(0, len(zs), GROUP)]


def slope_steps(m, zs, where, lateral, base, cells, rows, parts, cols, ends_ref, cell_ref):
    places, tops, bottoms = where
    me = lax.axis_index("depth")
    part = me ^ m
    at = pl.ds(base, SUB)
    lane = lax.broadcasted_iota(jnp.int32, (SUB, cols), 1)
    sublane = lax.broadcasted_iota(jnp.int32, (SUB, cols), 0)
    is_first = lane == 0
    is_last = lane == cols - 1
    is_top = {low: jnp.logical_and(sublane == 0, base == low) for low in sorted({top[0] for top in tops})}
    is_bottom = {
        low: jnp.logical_and(sublane == SUB - 1, base == low) for low in sorted({bottom[0] for bottom in bottoms})
    }
    group = rows // parts
    got = lateral[pl.ds(pl.multiple_of(base % group, SUB), SUB), :]
    sides = pltpu.roll(got, (2 * cols - 1 - base // group * (cols // parts)) % cols, 1)

    def layer(z):
        if z < 0:
            return ends_ref[part, 1, at, :]
        if z == cells:
            return ends_ref[part + 2, 0, at, :]
        ref, low = places[z]
        return ref[pl.ds(low + base, SUB), :]

    def step(z):
        ref, low = places[z]
        here = layer(z)
        top_at, top_ref, top = tops[z]
        bottom_at, bottom_ref, bottom = bottoms[z]
        upper = jnp.where(is_top[top_at], top_ref[top : top + 1, :], ref[pl.ds(low + base - 1, SUB), :])
        lower = jnp.where(is_bottom[bottom_at], bottom_ref[bottom : bottom + 1, :], ref[pl.ds(low + base + 1, SUB), :])
        edge = pltpu.roll(sides, (cols - 2 * z) % cols, 1) if z else sides
        grad_x = pltpu.roll(jnp.where(is_first, edge, here), cols - 1, 1) - pltpu.roll(
            jnp.where(is_last, edge, here), 1, 1
        )
        grad_y = lower - upper
        grad_z = layer(z + 1) - layer(z - 1)
        inverse = lax.rsqrt(grad_x * grad_x + grad_y * grad_y + grad_z * grad_z + 4.0)
        cell_ref[0, z] = grad_x * inverse
        cell_ref[1, z] = grad_y * inverse
        cell_ref[2, z] = grad_z * inverse

    return [functools.partial(step, z) for z in zs]


def prepare_steps(m, zs, where, lateral, base, cells, rows, parts, cols, ends_ref, weight_ref, cell_ref, mixed_ref):
    slopes = slope_steps(m, zs, where, lateral, base, cells, rows, parts, cols, ends_ref, cell_ref)
    mixes = mix_steps(zs, where[0], base, cols, weight_ref, mixed_ref)

    def both(i):
        mixes[i]()
        for step in slopes[GROUP * i : GROUP * (i + 1)]:
            step()

    return [functools.partial(both, i) for i in range(len(mixes))]


def march_unit(flip, vector_ref, zs, cells, cell_ref, mixed_ref, beside, inner=None):
    passes = vector_ref.shape[0]
    channels = mixed_ref.shape[1] // (passes * SUB)
    shape = vector_ref.shape[2:]
    vectors = [[vector_ref[p, axis] for axis in range(3)] for p in range(passes)]
    state = [(jnp.ones(shape, jnp.float32), [jnp.zeros(shape, jnp.float32)] * 3)] * passes
    count = len(beside)
    for u, spot in enumerate(zs):
        for step in beside[u * count // len(zs) : (u + 1) * count // len(zs)]:
            step()
        z = spot + flip * (cells - 1 - 2 * spot)
        normal = [cell_ref[axis, z] for axis in range(3)]
        for p in range(passes):
            keep, sums = state[p]
            mixed = [mixed_ref[z, (p * channels + c) * SUB : (p * channels + c + 1) * SUB, :] for c in range(channels)]
            facing = normal[0] * vectors[p][0] + normal[1] * vectors[p][1] + normal[2] * vectors[p][2]
            taken = keep * mixed[3]
            weight = taken * (AMBIENT + jnp.abs(facing))
            sums = [total + weight * tint for total, tint in zip(sums, mixed)]
            keep = keep - taken
            if inner is not None and u == 0:
                keep, sums = keep * inner(p, 0), [total + keep * inner(p, j + 1) for j, total in enumerate(sums)]
            state[p] = (keep, sums)
    return [[keep] + sums for keep, sums in state]


def march_tiles(count, start, prepare, unit):
    def ahead(index, slot):
        return prepare(pl.multiple_of((index + 1) * SUB, SUB), 1 - slot)

    for step in prepare(start * SUB, 0):
        step()

    def pair(i, carry):
        for slot in range(2):
            index = start + 2 * i + slot
            unit(index, slot, ahead(index, slot))
        return carry

    lax.fori_loop(0, count // 2 - 1, pair, 0)
    unit(start + count - 2, 0, ahead(start + count - 2, 0))
    unit(start + count - 1, 1, [])


def mix_kernel(parts, index_ref, lights_ref, curves_ref, own_ref, vector_ref, weight_ref, mixed_ref):
    tiles, cells, _, cols = mixed_ref.shape
    passes = index_ref.shape[0]
    for p in range(passes):
        for axis in range(3):
            vector_ref[p, axis] = jnp.full((SUB, cols), lights_ref[index_ref[p], axis])
    fill_weights(index_ref, curves_ref, OPACITY / (parts * cells), weight_ref)
    places, _, _ = near_places(cells, tiles * SUB, own_ref)

    def tile(i, carry):
        base = pl.multiple_of(i * SUB, SUB)
        for step in mix_steps(range(1, cells - 1), places, base, cols, weight_ref, mixed_ref.at[i]):
            step()
        return carry

    lax.fori_loop(0, tiles, tile, 0)


def own_kernel(parts, flip_ref, vector_ref, own_ref, mixed_ref, lateral_ref, out_ref, *cell_refs):
    rows, cols = out_ref.shape[1:]
    passes = vector_ref.shape[0]
    channels = out_ref.shape[0] // passes
    cells = cell_refs[0].shape[1]
    flip = flip_ref[0]
    inner = range(1, cells - 1)
    where = near_places(cells, rows, own_ref)

    def prepare(base, slot):
        return slope_steps(0, inner, where, lateral_ref, base, cells, rows, parts, cols, None, cell_refs[slot])

    def unit(index, slot, beside):
        base = pl.multiple_of(index * SUB, SUB)
        result = march_unit(flip, vector_ref, inner, cells, cell_refs[slot], mixed_ref.at[index], beside)
        for p in range(passes):
            for j in range(channels):
                out_ref[p * channels + j, pl.ds(base, SUB), :] = result[p][j]

    march_tiles(rows // SUB, 0, prepare, unit)


def near_kernel(parts, flip_ref, vector_ref, weight_ref, inner_ref, *refs):
    count = parts - 1
    heads, laterals, out_ref, ends_ref = refs[:parts], refs[parts : 2 * parts - 1], refs[2 * parts - 1], refs[2 * parts]
    cell_refs, mixed_refs = refs[2 * parts + 1 : 2 * parts + 1 + 2 * count], refs[2 * parts + 1 + 2 * count :]
    rows, cols = out_ref.shape[2:]
    cells = cell_refs[0].shape[1]
    passes = vector_ref.shape[0]
    channels = inner_ref.shape[0] // passes
    flip = flip_ref[0]
    tiles = rows // SUB
    zs = [(0, cells - 1)] + [range(cells)] * (count - 1)
    places = [near_places(cells, rows, head) for head in heads[:count]]
    fill_ends(parts, cells, rows, heads, ends_ref)

    def prepare(m, base, slot):
        spot = slot * count + m
        return prepare_steps(
            m, zs[m], places[m], laterals[m], base, cells, rows, parts, cols, ends_ref, weight_ref, cell_refs[spot], mixed_refs[spot]
        )

    marches = [len(z) for z in zs]
    ends = [sum(marches[: m + 1]) for m in range(count)]

    def unit(index, slot, beside):
        base = pl.multiple_of(index * SUB, SUB)
        at = pl.ds(base, SUB)
        cuts = [0] + [len(beside) * end // ends[-1] for end in ends]
        for m in range(count):
            inner = (lambda p, j: inner_ref[p * channels + j, at, :]) if m == 0 else None
            mine = beside[cuts[m] : cuts[m + 1]]
            spot = slot * count + m
            result = march_unit(flip, vector_ref, zs[m], cells, cell_refs[spot], mixed_refs[spot], mine, inner)
            for p in range(passes):
                for j in range(channels):
                    out_ref[m, p * channels + j, at, :] = result[p][j]

    def prepare_all(base, slot):
        return [step for m in range(count) for step in prepare(m, base, slot)]

    march_tiles(tiles, 0, prepare_all, unit)


def over_either(first_leads, one, other):
    shape = one[0].shape
    unit = jnp.ones(shape, jnp.float32)
    scale_one = jnp.where(first_leads, unit, other[0])
    scale_other = jnp.where(first_leads, one[0], unit)
    return [one[0] * other[0]] + [scale_one * a + scale_other * b for a, b in zip(one[1:], other[1:])]


def far_kernel(parts, split, low, high, flip_ref, vector_ref, weight_ref, *refs):
    heads, body, refs = refs[:parts], refs[parts], refs[parts + 1 :]
    rest, refs = (refs[0], refs[2:]) if low else (None, refs)
    states, out_ref, picture_ref, ends_ref, sems = refs[:5]
    cell_refs, mixed_refs = refs[5:7], refs[7:]
    channels, rows, cols = out_ref.shape[1:]
    cells = cell_refs[0].shape[1]
    passes = vector_ref.shape[0]
    flip = flip_ref[0]
    me = lax.axis_index("depth")
    places = far_places(cells, rows, parts, split, heads[-1], body, rest)
    fill_ends(parts, cells, rows, heads, ends_ref)
    tiles = range(low // SUB, high // SUB)

    def prepare(base, slot):
        return prepare_steps(
            parts - 1, range(cells), places, body, base, cells, rows, parts, cols, ends_ref, weight_ref, cell_refs[slot], mixed_refs[slot]
        )

    def send(index):
        at = pl.ds(pl.multiple_of(index * SUB, SUB), SUB)
        return pltpu.make_async_copy(picture_ref.at[:, :, at, :], out_ref.at[:, :, at, :], sems.at[index])

    def finish(result, index):
        at = pl.ds(pl.multiple_of(index * SUB, SUB), SUB)
        for p in range(passes):
            images = [[states[m, p * channels + j, at, :] for j in range(channels)] for m in range(parts - 1)]
            images.append(result[p])
            bit = 0
            while len(images) > 1:
                leads = ((me >> bit) & 1) == flip
                images = [over_either(leads, images[j], images[j + 1]) for j in range(0, len(images), 2)]
                bit += 1
            for channel in range(3):
                picture_ref[p, channel, at, :] = images[0][channel + 1]
            picture_ref[p, 3, at, :] = 1.0 - images[0][0]
        send(index).start()

    def unit(index, slot, beside):
        finish(march_unit(flip, vector_ref, range(cells), cells, cell_refs[slot], mixed_refs[slot], beside), index)

    march_tiles(len(tiles), tiles[0], prepare, unit)
    for index in tiles:
        send(index).wait()


def swap_pairs(block, axis, start):
    pairs = [(i, i + 1) for i in range(start, lax.axis_size(axis) - 1, 2)]
    return lax.ppermute(block, axis, pairs + [(j, i) for i, j in pairs])


def swap_along(block, axis, mask):
    return lax.ppermute(block, axis, [(i, i ^ mask) for i in range(lax.axis_size(axis))])


def estimate(micros):
    return pl.CostEstimate(flops=int(micros * 1_000_000_000), transcendentals=0, bytes_accessed=0)


def on_device(field, light_vectors, transfer, light_index, flips):
    parts = lax.axis_size("depth")
    cells, all_rows, cols = field.shape
    rows = all_rows // parts
    passes = light_index.shape[0]
    channels, knots = transfer.shape[1:]
    tiles = rows // SUB
    values = passes * channels
    in_vmem = pl.BlockSpec(memory_space=VMEM)
    in_smem = pl.BlockSpec(memory_space=SMEM)
    in_any = pl.BlockSpec(memory_space=pl.ANY)
    in_hbm = pl.BlockSpec(memory_space=pltpu.HBM)

    def array(*shape):
        return jax.ShapeDtypeStruct(shape, jnp.float32)

    def settings(mib, micros):
        return dict(
            compiler_params=pltpu.CompilerParams(vmem_limit_bytes=mib * MIB),
            cost_estimate=pl.CostEstimate(flops=int(micros * 1e9), transcendentals=0, bytes_accessed=0),
        )

    near_rows = 2 * cells + cells * rows
    head_rows = 2 * cells + 2 * rows
    skip = rows // parts
    split = rows // 2
    body_rows = skip + (cells - 2) * split + cells
    rest_rows = (cells - 2) * (rows - split) + 2 * SUB
    *packed, far_head = pl.pallas_call(
        functools.partial(pack_kernel, parts),
        out_shape=[array(near_rows, cols)] * (parts - 2) + [array(head_rows, cols)],
        in_specs=[in_hbm],
        out_specs=[in_vmem] * (parts - 1),
        scratch_shapes=[VMEM((parts - 1, 2, cells, SUB, cols), jnp.float32), pltpu.SemaphoreType.DMA((6, parts - 1))],
        name="pack",
        **settings(8, 1),
    )(pltpu.with_memory_space_constraint(field, pltpu.HBM))
    near = [swap_along(packed[m - 1], "depth", m) for m in range(1, parts - 1)]

    far_head = swap_along(far_head, "depth", parts - 1)

    edges, own, far_body, far_rest = pl.pallas_call(
        functools.partial(edge_kernel, parts, split),
        out_shape=[array(rows, cols), array(near_rows, cols), array(body_rows, cols), array(rest_rows, cols)],
        in_specs=[in_hbm, in_any],
        out_specs=[in_vmem] * 4,
        scratch_shapes=[VMEM(field.shape, jnp.float32), pltpu.SemaphoreType.DMA((4,))],
        name="edges",
        **settings(8, 1),
    )(pltpu.with_memory_space_constraint(field, pltpu.HBM), packed[0])
    sides = pl.pallas_call(
        functools.partial(side_kernel, parts),
        out_shape=[array(skip, cols)] * parts,
        in_specs=[in_vmem] * 2 + [in_any],
        out_specs=[in_vmem] * parts,
        name="sides",
        **settings(4, 0.1),
    )(swap_pairs(edges, "tile", 0), swap_pairs(edges, "tile", 1), far_head)
    laterals = [swap_along(sides[m], "depth", m) for m in range(1, parts - 1)]
    far_body = swap_along(lax.dynamic_update_slice(far_body, sides[-1], (0, 0)), "depth", parts - 1)
    *laterals, far_rest = lax.optimization_barrier((*laterals, far_rest))
    far_rest = swap_along(far_rest, "depth", parts - 1)

    cell_shape = VMEM((3, cells, SUB, cols), jnp.float32)
    mixed_shape = VMEM((cells, values * SUB, cols), jnp.float32)
    ends_shape = VMEM((parts + 2, 2, rows, cols), jnp.float32)
    weight_shape = jax.ShapeDtypeStruct((values * SUB, 3 * knots * SUB), jnp.bfloat16)
    vectors, weights, mixed = pl.pallas_call(
        functools.partial(mix_kernel, parts),
        out_shape=[array(passes, 3, SUB, cols), weight_shape, array(tiles, cells, values * SUB, cols)],
        in_specs=[in_smem] * 2 + [in_vmem] * 2,
        out_specs=[in_vmem] * 3,
        name="mix",
        **settings(8, 0.01),
    )(light_index, light_vectors, transfer, own)
    inner = pl.pallas_call(
        functools.partial(own_kernel, parts),
        out_shape=array(values, rows, cols),
        in_specs=[in_smem] + [in_vmem] * 4,
        out_specs=in_vmem,
        scratch_shapes=[cell_shape] * 2,
        name="own",
        **settings(8, 4),
    )(flips, vectors, own, mixed, sides[0])
    states = pl.pallas_call(
        functools.partial(near_kernel, parts),
        out_shape=array(parts - 1, values, rows, cols),
        in_specs=[in_smem] + [in_vmem] * (2 * parts + 2),
        out_specs=in_vmem,
        scratch_shapes=[ends_shape] + [cell_shape] * (2 * parts - 2) + [mixed_shape] * (2 * parts - 2),
        name="near",
        **settings(20, 60),
    )(flips, vectors, weights, inner, own, *near, far_head, sides[0], *laterals)
    picture = None
    for low, high in ((0, split), (split, rows)):
        late = [far_rest, picture] if low else []
        picture = pl.pallas_call(
            functools.partial(far_kernel, parts, split, low, high),
            out_shape=array(passes, channels, rows, cols),
            in_specs=[in_smem] + [in_vmem] * (parts + 3) + [in_vmem, in_any][: len(late)] + [in_vmem],
            out_specs=in_any,
            scratch_shapes=[
                VMEM((passes, channels, rows, cols), jnp.float32),
                ends_shape,
                pltpu.SemaphoreType.DMA((tiles,)),
            ]
            + [cell_shape] * 2
            + [mixed_shape] * 2,
            input_output_aliases={parts + 5: 0} if low else {},
            name="late" if low else "far",
            **settings(16, 2),
        )(flips, vectors, weights, own, *near, far_head, far_body, *late, states)
    return picture


def solution(mesh):
    in_specs = (P("depth", None, "tile"), P(), P(), P(), P("tile"))
    out_specs = P(None, None, "depth", "tile")
    return jax.shard_map(
        on_device, mesh=mesh, in_specs=in_specs, out_specs=out_specs, check_vma=False
    )
```

```python
import functools

import jax
import jax.numpy as jnp
from jax import lax
from jax.experimental import pallas as pl
from jax.experimental.pallas import tpu as pltpu
from jax.sharding import PartitionSpec as P

AMBIENT = 0.3
OPACITY = 2.0
SUB = 8
VMEM = pltpu.VMEM
SMEM = pltpu.SMEM
MIB = 1 << 20
FINE = 49152.0


def pack_kernel(parts, field_ref, *refs):
    outs, (rim_ref, sems) = refs[: parts - 1], refs[parts - 1 :]
    cells, all_rows, cols = field_ref.shape
    rows = all_rows // parts
    me = lax.axis_index("depth")
    copies, rims = [], []
    for j, out in enumerate(outs):
        low = pl.multiple_of((me ^ (j + 1)) * rows, SUB)
        before = jnp.maximum(low - 1, 0)
        after = jnp.minimum(low + rows, all_rows - 1)
        for side, start in enumerate((before, after)):
            source = field_ref.at[:, pl.ds(start, 1), :]
            rims.append(pltpu.make_async_copy(source, rim_ref.at[j, side], sems.at[side, j]))
        block = field_ref.at[:, pl.ds(low, rows), :]
        if j < parts - 2:
            centre = out.at[pl.ds(cells, cells * rows), :].reshape(cells, rows, cols)
            quarter = cells // 4
            for q in range(4):
                layers = pl.ds(q * quarter, quarter)
                copies.append(pltpu.make_async_copy(block.at[layers], centre.at[layers], sems.at[2 + q, j]))
        else:
            for side in range(2):
                layer = out.at[pl.ds(cells + side * rows, rows), :]
                copies.append(pltpu.make_async_copy(block.at[side * (cells - 1)], layer, sems.at[2 + side, j]))
    for copy in rims + copies:
        copy.start()
    for copy in rims:
        copy.wait()
    for j, out in enumerate(outs):
        part = me ^ (j + 1)
        above = jnp.where(part > 0, 1.0, 0.0)
        below = jnp.where(part < parts - 1, 1.0, 0.0)
        for z in range(cells):
            out[z : z + 1, :] = rim_ref[j, 0, z, 0:1, :] * above
            below_at = out.shape[0] - cells + z
            out[below_at : below_at + 1, :] = rim_ref[j, 1, z, 0:1, :] * below
    for copy in copies:
        copy.wait()


def edge_kernel(parts, split, field_ref, _, edge_ref, own_ref, body_ref, rest_ref):
    cells, all_rows, cols = field_ref.shape
    rows = all_rows // parts
    me = lax.axis_index("depth")
    lane_pair = lax.broadcasted_iota(jnp.int32, (SUB, cols), 1) // 2

    def tile(i, carry):
        acc = jnp.zeros((SUB, cols), jnp.float32)
        for part in range(parts):
            for z in range(cells):
                slot = part * cells + z
                start = pl.multiple_of(part * rows + i * SUB, SUB)
                value = field_ref[z, pl.ds(start, SUB), :]
                moved = pltpu.roll(value, (2 * slot + 1) % cols, 1)
                acc = jnp.where(lane_pair == slot, moved, acc)
        edge_ref[pl.ds(pl.multiple_of(i * SUB, SUB), SUB), :] = acc
        return carry

    lax.fori_loop(0, rows // SUB, tile, 0)
    low = pl.multiple_of(me * rows, SUB)
    above = jnp.where(me > 0, 1.0, 0.0)
    below = jnp.where(me < parts - 1, 1.0, 0.0)
    for z in range(cells):
        own_ref[z : z + 1, :] = field_ref[z, pl.ds(jnp.maximum(low - 1, 0), 1), :] * above
        below_at = cells + cells * rows + z
        own_ref[below_at : below_at + 1, :] = field_ref[z, pl.ds(jnp.minimum(low + rows, all_rows - 1), 1), :] * below
    far_low = pl.multiple_of((me ^ (parts - 1)) * rows, SUB)
    own_places, _, _ = near_places(cells, rows, own_ref)
    for z in range(cells):
        ref, start = own_places[z]
        ref[start : start + rows, :] = field_ref[z, pl.ds(low, rows), :]
    skip, more = rows // parts, rows - split
    for z in range(1, cells - 1):
        at = skip + (z - 1) * split
        body_ref[at : at + split, :] = field_ref[z, pl.ds(far_low, split), :]
        next_row = skip + (cells - 2) * split + z - 1
        body_ref[next_row : next_row + 1, :] = field_ref[z, pl.ds(far_low + split, 1), :]
        at = SUB + (z - 1) * more
        rest_ref[at : at + more, :] = field_ref[z, pl.ds(far_low + split, more), :]


def side_kernel(parts, even_ref, odd_ref, _, *outs):
    rows, cols = even_ref.shape
    group = rows // parts
    width = cols // parts
    me = lax.axis_index("depth")
    lane = lax.broadcasted_iota(jnp.int32, (rows, cols), 1)
    tile = lax.axis_index("tile")
    sides = jnp.where((lane + tile) % 2 == 1, even_ref[...], odd_ref[...])
    for m in range(parts):
        acc = jnp.zeros((group, cols), jnp.float32)
        for j in range(parts):
            moved = pltpu.roll(sides[j * group : (j + 1) * group], (j - (me ^ m) + parts) * width % cols, 1)
            acc = jnp.where(lane[:group] // width == j, moved, acc)
        outs[m][...] = acc


def near_places(cells, rows, head):
    count = head.shape[0]
    places = [(head, cells + z * rows) for z in range(cells)]
    tops = [(0, head, z) for z in range(cells)]
    bottoms = [(rows - SUB, head, count - cells + z) for z in range(cells)]
    return places, tops, bottoms


def far_places(cells, rows, parts, split, head, body, rest=None):
    skip, more = rows // parts, rows - split
    places, tops, bottoms = near_places(cells, rows, head)
    places[0], places[-1] = (head, cells), (head, cells + rows)
    for z in range(1, cells - 1):
        if rest is None:
            places[z] = (body, skip + (z - 1) * split)
            bottoms[z] = (split - SUB, body, skip + (cells - 2) * split + z - 1)
        else:
            places[z] = (rest, SUB + (z - 1) * more - split)
            tops[z] = (split, body, skip + z * split - 1)
    return places, tops, bottoms


def fill_ends(parts, cells, rows, heads, ends_ref):
    me = lax.axis_index("depth")
    ends_ref[0, 1] = jnp.zeros_like(ends_ref[0, 1])
    ends_ref[parts + 1, 0] = jnp.zeros_like(ends_ref[0, 0])
    for m in range(parts):
        last = (cells - 1) * rows if m < parts - 1 else rows
        ends_ref[(me ^ m) + 1, 0] = heads[m][cells : cells + rows, :]
        ends_ref[(me ^ m) + 1, 1] = heads[m][cells + last : cells + last + rows, :]


def fill_weights(index_ref, curves_ref, scale, weight_ref):
    passes = index_ref.shape[0]
    channels, knots = curves_ref.shape[1:]
    width = weight_ref.shape[1]
    block = knots * SUB
    points = jnp.concatenate([curves_ref[index_ref[p]] for p in range(passes)], axis=0)
    channel = lax.broadcasted_iota(jnp.int32, points.shape, 0) % channels
    points = jnp.where(channel == channels - 1, points * scale, points)
    knot = lax.broadcasted_iota(jnp.int32, (knots, width), 0)
    lane = lax.broadcasted_iota(jnp.int32, (knots, width), 1)
    target = lane // SUB % knots
    here = jnp.where(knot == target, 1.0, 0.0)
    after = jnp.where(knot == target + 1, 1.0, 0.0)
    is_slope = jnp.logical_and(lane >= block, lane < 2 * block)
    spread = jnp.where(is_slope, after - here, here)
    values = jnp.dot(points, spread, precision=lax.Precision.HIGHEST, preferred_element_type=jnp.float32)
    shape = (2 * SUB, width)
    row = lax.broadcasted_iota(jnp.int32, shape, 0)
    lane = lax.broadcasted_iota(jnp.int32, shape, 1)
    on_row = lane % SUB == row % SUB
    for pair in range(passes * channels // 2):
        upper, lower = [jnp.broadcast_to(values[2 * pair + j : 2 * pair + j + 1], shape) for j in range(2)]
        value = jnp.where(on_row, jnp.where(row < SUB, upper, lower), 0.0)
        coarse = value.astype(jnp.bfloat16).astype(jnp.float32)
        value = jnp.where(lane < 2 * block, value, value - coarse)
        weight_ref[2 * pair * SUB : 2 * (pair + 1) * SUB, :] = value.astype(jnp.bfloat16)


def prepare_steps(m, zs, where, lateral, base, cells, rows, parts, cols, ends_ref, weight_ref, cell_ref, mixed_ref):
    me = lax.axis_index("depth")
    part = me ^ m
    at = pl.ds(base, SUB)
    lane = lax.broadcasted_iota(jnp.int32, (SUB, cols), 1)
    sublane = lax.broadcasted_iota(jnp.int32, (SUB, cols), 0)
    is_first = lane == 0
    is_last = lane == cols - 1
    places, tops, bottoms = where
    group = rows // parts
    got = lateral[pl.ds(pl.multiple_of(base % group, SUB), SUB), :]
    sides = pltpu.roll(got, (2 * cols - 1 - base // group * (cols // parts)) % cols, 1)

    def layer(z):
        if z < 0:
            return ends_ref[part, 1, at, :]
        if z == cells:
            return ends_ref[part + 2, 0, at, :]
        ref, low = places[z]
        return ref[pl.ds(low + base, SUB), :]

    def step(z):
        ref, low = places[z]
        here = layer(z)
        top_at, top_ref, top = tops[z]
        bottom_at, bottom_ref, bottom = bottoms[z]
        is_top = jnp.logical_and(sublane == 0, base == top_at)
        is_bottom = jnp.logical_and(sublane == SUB - 1, base == bottom_at)
        upper = jnp.where(is_top, top_ref[top : top + 1, :], ref[pl.ds(low + base - 1, SUB), :])
        lower = jnp.where(is_bottom, bottom_ref[bottom : bottom + 1, :], ref[pl.ds(low + base + 1, SUB), :])
        edge = pltpu.roll(sides, (cols - 2 * z) % cols, 1) if z else sides
        grad_x = pltpu.roll(jnp.where(is_first, edge, here), cols - 1, 1) - pltpu.roll(
            jnp.where(is_last, edge, here), 1, 1
        )
        grad_y = lower - upper
        grad_z = layer(z + 1) - layer(z - 1)
        inverse = lax.rsqrt(grad_x * grad_x + grad_y * grad_y + grad_z * grad_z + 4.0)
        cell_ref[0, z] = grad_x * inverse
        cell_ref[1, z] = grad_y * inverse
        cell_ref[2, z] = grad_z * inverse
        half = 0.5 * (knots - 1)
        position = half + half * jnp.tanh(0.5 * here)
        coarse = (position + FINE) - FINE
        segment = jnp.minimum(jnp.floor(position), knots - 2.0)
        rest = position - coarse
        right = coarse - segment
        left = 1.0 - right
        twice = lambda value: jnp.concatenate([value, value], axis=0).astype(jnp.bfloat16)
        left, right, rest, segment = twice(left), twice(right), twice(rest), twice(segment)
        zero = jnp.zeros_like(left)
        tents, rests = [], []
        for k in range(0, knots, 2):
            is_here = segment == pair_at + k
            is_before = segment == pair_at + (k - 1)
            tents.append(jnp.where(is_here, left, jnp.where(is_before, right, zero)))
            rests.append(jnp.where(is_here, rest, zero))
        return [jnp.concatenate(part, axis=0) for part in (tents, rests)]

    def two(first, second):
        tents, rests = [jnp.concatenate(both, axis=1) for both in zip(step(first), step(second))]
        right = jnp.concatenate([tents, rests, tents], axis=0)
        mixed = jnp.dot(weight_ref[...], right, preferred_element_type=jnp.float32)
        mixed_ref[first] = mixed[:, :cols]
        mixed_ref[second] = mixed[:, cols:]

    knots = weight_ref.shape[1] // (3 * SUB)
    pair_at = jnp.where(lax.broadcasted_iota(jnp.int32, (2 * SUB, cols), 0) < SUB, 0.0, 1.0).astype(jnp.bfloat16)
    zs = list(zs)
    return [functools.partial(two, *zs[i : i + 2]) for i in range(0, len(zs), 2)]


def march_unit(flip, vector_ref, zs, cells, cell_ref, mixed_ref, beside, inner=None):
    passes = vector_ref.shape[0]
    channels = mixed_ref.shape[1] // (passes * SUB)
    shape = vector_ref.shape[2:]
    vectors = [[vector_ref[p, axis] for axis in range(3)] for p in range(passes)]
    state = [(jnp.ones(shape, jnp.float32), [jnp.zeros(shape, jnp.float32)] * 3)] * passes
    count = len(beside)
    for u, spot in enumerate(zs):
        for step in beside[u * count // len(zs) : (u + 1) * count // len(zs)]:
            step()
        z = spot + flip * (cells - 1 - 2 * spot)
        normal = [cell_ref[axis, z] for axis in range(3)]
        for p in range(passes):
            keep, sums = state[p]
            mixed = [mixed_ref[z, (p * channels + c) * SUB : (p * channels + c + 1) * SUB, :] for c in range(channels)]
            facing = normal[0] * vectors[p][0] + normal[1] * vectors[p][1] + normal[2] * vectors[p][2]
            taken = keep * mixed[3]
            weight = taken * (AMBIENT + jnp.abs(facing))
            sums = [total + weight * tint for total, tint in zip(sums, mixed)]
            keep = keep - taken
            if inner is not None and u == 0:
                keep, sums = keep * inner(p, 0), [total + keep * inner(p, j + 1) for j, total in enumerate(sums)]
            state[p] = (keep, sums)
    return [[keep] + sums for keep, sums in state]


def march_tiles(count, start, prepare, unit):
    def ahead(index, slot):
        return prepare(pl.multiple_of((index + 1) * SUB, SUB), 1 - slot)

    for step in prepare(start * SUB, 0):
        step()

    def pair(i, carry):
        for slot in range(2):
            index = start + 2 * i + slot
            unit(index, slot, ahead(index, slot))
        return carry

    lax.fori_loop(0, count // 2 - 1, pair, 0)
    unit(start + count - 2, 0, ahead(start + count - 2, 0))
    unit(start + count - 1, 1, [])


def own_kernel(parts, index_ref, flip_ref, lights_ref, curves_ref, own_ref, lateral_ref, out_ref, vector_ref, weight_ref, *refs):
    cell_refs, mixed_refs = refs[:2], refs[2:]
    rows, cols = out_ref.shape[1:]
    channels = curves_ref.shape[1]
    passes = index_ref.shape[0]
    cells = cell_refs[0].shape[1]
    flip = flip_ref[0]
    tiles = rows // SUB
    inner = range(1, cells - 1)
    for p in range(passes):
        for axis in range(3):
            vector_ref[p, axis] = jnp.full((SUB, cols), lights_ref[index_ref[p], axis])
    fill_weights(index_ref, curves_ref, OPACITY / (parts * cells), weight_ref)
    places = near_places(cells, rows, own_ref)

    def prepare(base, slot):
        return prepare_steps(
            0, inner, places, lateral_ref, base, cells, rows, parts, cols, None, weight_ref, cell_refs[slot], mixed_refs[slot]
        )

    def unit(index, slot, beside):
        base = pl.multiple_of(index * SUB, SUB)
        result = march_unit(flip, vector_ref, inner, cells, cell_refs[slot], mixed_refs[slot], beside)
        for p in range(passes):
            for j in range(channels):
                out_ref[p * channels + j, pl.ds(base, SUB), :] = result[p][j]

    march_tiles(tiles, 0, prepare, unit)


def near_kernel(parts, flip_ref, vector_ref, weight_ref, inner_ref, *refs):
    count = parts - 1
    heads, laterals, out_ref, ends_ref = refs[:parts], refs[parts : 2 * parts - 1], refs[2 * parts - 1], refs[2 * parts]
    cell_refs, mixed_refs = refs[2 * parts + 1 : 2 * parts + 1 + count], refs[2 * parts + 1 + count :]
    rows, cols = out_ref.shape[2:]
    cells = cell_refs[0].shape[1]
    passes = vector_ref.shape[0]
    channels = inner_ref.shape[0] // passes
    flip = flip_ref[0]
    tiles = rows // SUB
    zs = [(0, cells - 1)] + [range(cells)] * (count - 1)
    places = [near_places(cells, rows, head) for head in heads[:count]]
    fill_ends(parts, cells, rows, heads, ends_ref)

    def prepare(m, base):
        return prepare_steps(
            m, zs[m], places[m], laterals[m], base, cells, rows, parts, cols, ends_ref, weight_ref, cell_refs[m], mixed_refs[m]
        )

    for step in prepare(0, 0):
        step()

    def tile(i, carry):
        base = pl.multiple_of(i * SUB, SUB)
        after = pl.multiple_of(jnp.minimum(i + 1, tiles - 1) * SUB, SUB)
        at = pl.ds(base, SUB)
        for m in range(count):
            beside = prepare(m + 1, base) if m + 1 < count else prepare(0, after)
            inner = (lambda p, j: inner_ref[p * channels + j, at, :]) if m == 0 else None
            result = march_unit(flip, vector_ref, zs[m], cells, cell_refs[m], mixed_refs[m], beside, inner)
            for p in range(passes):
                for j in range(channels):
                    out_ref[m, p * channels + j, at, :] = result[p][j]
        return carry

    lax.fori_loop(0, tiles, tile, 0)


def over_either(first_leads, one, other):
    shape = one[0].shape
    unit = jnp.ones(shape, jnp.float32)
    scale_one = jnp.where(first_leads, unit, other[0])
    scale_other = jnp.where(first_leads, one[0], unit)
    return [one[0] * other[0]] + [scale_one * a + scale_other * b for a, b in zip(one[1:], other[1:])]


def far_kernel(parts, split, low, high, flip_ref, vector_ref, weight_ref, *refs):
    heads, body, refs = refs[:parts], refs[parts], refs[parts + 1 :]
    rest, refs = (refs[0], refs[2:]) if low else (None, refs)
    states, out_ref, picture_ref, ends_ref, sems = refs[:5]
    cell_refs, mixed_refs = refs[5:7], refs[7:]
    channels, rows, cols = out_ref.shape[1:]
    cells = cell_refs[0].shape[1]
    passes = vector_ref.shape[0]
    flip = flip_ref[0]
    me = lax.axis_index("depth")
    places = far_places(cells, rows, parts, split, heads[-1], body, rest)
    fill_ends(parts, cells, rows, heads, ends_ref)
    tiles = range(low // SUB, high // SUB)

    def prepare(base, slot):
        return prepare_steps(
            parts - 1, range(cells), places, body, base, cells, rows, parts, cols, ends_ref, weight_ref, cell_refs[slot], mixed_refs[slot]
        )

    def send(index):
        at = pl.ds(pl.multiple_of(index * SUB, SUB), SUB)
        return pltpu.make_async_copy(picture_ref.at[:, :, at, :], out_ref.at[:, :, at, :], sems.at[index])

    def finish(result, index):
        at = pl.ds(pl.multiple_of(index * SUB, SUB), SUB)
        for p in range(passes):
            images = [[states[m, p * channels + j, at, :] for j in range(channels)] for m in range(parts - 1)]
            images.append(result[p])
            bit = 0
            while len(images) > 1:
                leads = ((me >> bit) & 1) == flip
                images = [over_either(leads, images[j], images[j + 1]) for j in range(0, len(images), 2)]
                bit += 1
            for channel in range(3):
                picture_ref[p, channel, at, :] = images[0][channel + 1]
            picture_ref[p, 3, at, :] = 1.0 - images[0][0]
        send(index).start()

    def unit(index, slot, beside):
        finish(march_unit(flip, vector_ref, range(cells), cells, cell_refs[slot], mixed_refs[slot], beside), index)

    march_tiles(len(tiles), tiles[0], prepare, unit)
    for index in tiles:
        send(index).wait()


def swap_pairs(block, axis, start):
    pairs = [(i, i + 1) for i in range(start, lax.axis_size(axis) - 1, 2)]
    return lax.ppermute(block, axis, pairs + [(j, i) for i, j in pairs])


def swap_along(block, axis, mask):
    return lax.ppermute(block, axis, [(i, i ^ mask) for i in range(lax.axis_size(axis))])


def estimate(micros):
    return pl.CostEstimate(flops=int(micros * 1_000_000_000), transcendentals=0, bytes_accessed=0)


def on_device(field, light_vectors, transfer, light_index, flips):
    parts = lax.axis_size("depth")
    cells, all_rows, cols = field.shape
    rows = all_rows // parts
    passes = light_index.shape[0]
    channels, knots = transfer.shape[1:]
    tiles = rows // SUB
    values = passes * channels
    in_vmem = pl.BlockSpec(memory_space=VMEM)
    in_smem = pl.BlockSpec(memory_space=SMEM)
    in_any = pl.BlockSpec(memory_space=pl.ANY)
    in_hbm = pl.BlockSpec(memory_space=pltpu.HBM)

    def array(*shape):
        return jax.ShapeDtypeStruct(shape, jnp.float32)

    def settings(mib, micros):
        return dict(
            compiler_params=pltpu.CompilerParams(vmem_limit_bytes=mib * MIB),
            cost_estimate=pl.CostEstimate(flops=int(micros * 1e9), transcendentals=0, bytes_accessed=0),
        )

    near_rows = 2 * cells + cells * rows
    head_rows = 2 * cells + 2 * rows
    skip = rows // parts
    split = rows - rows // parts
    body_rows = skip + (cells - 2) * split + cells
    rest_rows = (cells - 2) * (rows - split) + 2 * SUB
    *packed, far_head = pl.pallas_call(
        functools.partial(pack_kernel, parts),
        out_shape=[array(near_rows, cols)] * (parts - 2) + [array(head_rows, cols)],
        in_specs=[in_hbm],
        out_specs=[in_vmem] * (parts - 1),
        scratch_shapes=[VMEM((parts - 1, 2, cells, 1, cols), jnp.float32), pltpu.SemaphoreType.DMA((6, parts - 1))],
        name="pack",
        **settings(8, 1),
    )(pltpu.with_memory_space_constraint(field, pltpu.HBM))
    near = [swap_along(packed[m - 1], "depth", m) for m in range(1, parts - 1)]

    far_head = swap_along(far_head, "depth", parts - 1)

    edges, own, far_body, far_rest = pl.pallas_call(
        functools.partial(edge_kernel, parts, split),
        out_shape=[array(rows, cols), array(near_rows, cols), array(body_rows, cols), array(rest_rows, cols)],
        in_specs=[in_vmem, in_any],
        out_specs=[in_vmem] * 4,
        name="edges",
        **settings(8, 1),
    )(field, packed[0])
    sides = pl.pallas_call(
        functools.partial(side_kernel, parts),
        out_shape=[array(skip, cols)] * parts,
        in_specs=[in_vmem] * 2 + [in_any],
        out_specs=[in_vmem] * parts,
        name="sides",
        **settings(4, 0.1),
    )(swap_pairs(edges, "tile", 0), swap_pairs(edges, "tile", 1), far_head)
    laterals = [swap_along(sides[m], "depth", m) for m in range(1, parts - 1)]
    far_body = swap_along(lax.dynamic_update_slice(far_body, sides[-1], (0, 0)), "depth", parts - 1)
    *laterals, far_rest = lax.optimization_barrier((*laterals, far_rest))
    far_rest = swap_along(far_rest, "depth", parts - 1)

    cell_shape = VMEM((3, cells, SUB, cols), jnp.float32)
    mixed_shape = VMEM((cells, values * SUB, cols), jnp.float32)
    ends_shape = VMEM((parts + 2, 2, rows, cols), jnp.float32)
    weight_shape = jax.ShapeDtypeStruct((values * SUB, 3 * knots * SUB), jnp.bfloat16)
    inner, vectors, weights = pl.pallas_call(
        functools.partial(own_kernel, parts),
        out_shape=[array(values, rows, cols), array(passes, 3, SUB, cols), weight_shape],
        in_specs=[in_smem] * 3 + [in_vmem] * 3,
        out_specs=[in_vmem] * 3,
        scratch_shapes=[cell_shape] * 2 + [mixed_shape] * 2,
        name="own",
        **settings(12, 4),
    )(light_index, flips, light_vectors, transfer, own, sides[0])
    states = pl.pallas_call(
        functools.partial(near_kernel, parts),
        out_shape=array(parts - 1, values, rows, cols),
        in_specs=[in_smem] + [in_vmem] * (2 * parts + 2),
        out_specs=in_vmem,
        scratch_shapes=[ends_shape] + [cell_shape] * (parts - 1) + [mixed_shape] * (parts - 1),
        name="near",
        **settings(16, 60),
    )(flips, vectors, weights, inner, own, *near, far_head, sides[0], *laterals)
    picture = None
    for low, high in ((0, split), (split, rows)):
        late = [far_rest, picture] if low else []
        picture = pl.pallas_call(
            functools.partial(far_kernel, parts, split, low, high),
            out_shape=array(passes, channels, rows, cols),
            in_specs=[in_smem] + [in_vmem] * (parts + 3) + [in_vmem, in_any][: len(late)] + [in_vmem],
            out_specs=in_any,
            scratch_shapes=[
                VMEM((passes, channels, rows, cols), jnp.float32),
                ends_shape,
                pltpu.SemaphoreType.DMA((tiles,)),
            ]
            + [cell_shape] * 2
            + [mixed_shape] * 2,
            input_output_aliases={parts + 5: 0} if low else {},
            name="late" if low else "far",
            **settings(16, 2),
        )(flips, vectors, weights, own, *near, far_head, far_body, *late, states)
    return picture


def solution(mesh):
    in_specs = (P("depth", None, "tile"), P(), P(), P(), P("tile"))
    out_specs = P(None, None, "depth", "tile")
    return jax.shard_map(
        on_device, mesh=mesh, in_specs=in_specs, out_specs=out_specs, check_vma=False
    )
```

```python
import functools

import jax
import jax.numpy as jnp
from jax import lax
from jax.experimental import pallas as pl
from jax.experimental.pallas import tpu as pltpu
from jax.sharding import PartitionSpec as P

AMBIENT = 0.3
OPACITY = 2.0
SUB = 8
VMEM = pltpu.VMEM
SMEM = pltpu.SMEM
MIB = 1 << 20
FINE = 49152.0


def pack_kernel(parts, field_ref, *refs):
    outs, (rim_ref, sems) = refs[: parts - 1], refs[parts - 1 :]
    cells, all_rows, cols = field_ref.shape
    rows = all_rows // parts
    me = lax.axis_index("depth")
    copies, rims = [], []
    for j, out in enumerate(outs):
        low = pl.multiple_of((me ^ (j + 1)) * rows, SUB)
        before = pl.multiple_of(jnp.maximum(low - SUB, 0), SUB)
        after = pl.multiple_of(jnp.minimum(low + rows, all_rows - SUB), SUB)
        for side, start in enumerate((before, after)):
            source = field_ref.at[:, pl.ds(start, SUB), :]
            rims.append(pltpu.make_async_copy(source, rim_ref.at[j, side], sems.at[side, j]))
        block = field_ref.at[:, pl.ds(low, rows), :]
        if j < parts - 2:
            centre = out.at[pl.ds(cells, cells * rows), :].reshape(cells, rows, cols)
            quarter = cells // 4
            for q in range(4):
                layers = pl.ds(q * quarter, quarter)
                copies.append(pltpu.make_async_copy(block.at[layers], centre.at[layers], sems.at[2 + q, j]))
        else:
            for side in range(2):
                layer = out.at[pl.ds(cells + side * rows, rows), :]
                copies.append(pltpu.make_async_copy(block.at[side * (cells - 1)], layer, sems.at[2 + side, j]))
    for copy in rims + copies:
        copy.start()
    for copy in rims:
        copy.wait()
    for j, out in enumerate(outs):
        part = me ^ (j + 1)
        above = jnp.where(part > 0, 1.0, 0.0)
        below = jnp.where(part < parts - 1, 1.0, 0.0)
        for z in range(cells):
            out[z : z + 1, :] = rim_ref[j, 0, z, SUB - 1 : SUB, :] * above
            below_at = out.shape[0] - cells + z
            out[below_at : below_at + 1, :] = rim_ref[j, 1, z, 0:1, :] * below
    for copy in copies:
        copy.wait()


def edge_kernel(parts, split, field_ref, _, edge_ref, own_ref, body_ref, rest_ref):
    cells, all_rows, cols = field_ref.shape
    rows = all_rows // parts
    me = lax.axis_index("depth")
    lane_pair = lax.broadcasted_iota(jnp.int32, (SUB, cols), 1) // 2

    def tile(i, carry):
        acc = jnp.zeros((SUB, cols), jnp.float32)
        for part in range(parts):
            for z in range(cells):
                slot = part * cells + z
                start = pl.multiple_of(part * rows + i * SUB, SUB)
                value = field_ref[z, pl.ds(start, SUB), :]
                moved = pltpu.roll(value, (2 * slot + 1) % cols, 1)
                acc = jnp.where(lane_pair == slot, moved, acc)
        edge_ref[pl.ds(pl.multiple_of(i * SUB, SUB), SUB), :] = acc
        return carry

    lax.fori_loop(0, rows // SUB, tile, 0)
    low = pl.multiple_of(me * rows, SUB)
    above = jnp.where(me > 0, 1.0, 0.0)
    below = jnp.where(me < parts - 1, 1.0, 0.0)
    for z in range(cells):
        own_ref[z : z + 1, :] = field_ref[z, pl.ds(jnp.maximum(low - 1, 0), 1), :] * above
        below_at = cells + cells * rows + z
        own_ref[below_at : below_at + 1, :] = field_ref[z, pl.ds(jnp.minimum(low + rows, all_rows - 1), 1), :] * below
    far_low = pl.multiple_of((me ^ (parts - 1)) * rows, SUB)
    own_places, _, _ = near_places(cells, rows, own_ref)
    for z in range(cells):
        ref, start = own_places[z]
        ref[start : start + rows, :] = field_ref[z, pl.ds(low, rows), :]
    skip, more = rows // parts, rows - split
    for z in range(1, cells - 1):
        at = skip + (z - 1) * split
        body_ref[at : at + split, :] = field_ref[z, pl.ds(far_low, split), :]
        next_row = skip + (cells - 2) * split + z - 1
        body_ref[next_row : next_row + 1, :] = field_ref[z, pl.ds(far_low + split, 1), :]
        at = SUB + (z - 1) * more
        rest_ref[at : at + more, :] = field_ref[z, pl.ds(far_low + split, more), :]


def side_kernel(parts, even_ref, odd_ref, _, *outs):
    rows, cols = even_ref.shape
    group = rows // parts
    width = cols // parts
    me = lax.axis_index("depth")
    lane = lax.broadcasted_iota(jnp.int32, (rows, cols), 1)
    tile = lax.axis_index("tile")
    sides = jnp.where((lane + tile) % 2 == 1, even_ref[...], odd_ref[...])
    for m in range(parts):
        acc = jnp.zeros((group, cols), jnp.float32)
        for j in range(parts):
            moved = pltpu.roll(sides[j * group : (j + 1) * group], (j - (me ^ m) + parts) * width % cols, 1)
            acc = jnp.where(lane[:group] // width == j, moved, acc)
        outs[m][...] = acc


def near_places(cells, rows, head):
    count = head.shape[0]
    places = [(head, cells + z * rows) for z in range(cells)]
    tops = [(0, head, z) for z in range(cells)]
    bottoms = [(rows - SUB, head, count - cells + z) for z in range(cells)]
    return places, tops, bottoms


def far_places(cells, rows, parts, split, head, body, rest=None):
    skip, more = rows // parts, rows - split
    places, tops, bottoms = near_places(cells, rows, head)
    places[0], places[-1] = (head, cells), (head, cells + rows)
    for z in range(1, cells - 1):
        if rest is None:
            places[z] = (body, skip + (z - 1) * split)
            bottoms[z] = (split - SUB, body, skip + (cells - 2) * split + z - 1)
        else:
            places[z] = (rest, SUB + (z - 1) * more - split)
            tops[z] = (split, body, skip + z * split - 1)
    return places, tops, bottoms


def fill_ends(parts, cells, rows, heads, ends_ref):
    me = lax.axis_index("depth")
    ends_ref[0, 1] = jnp.zeros_like(ends_ref[0, 1])
    ends_ref[parts + 1, 0] = jnp.zeros_like(ends_ref[0, 0])
    for m in range(parts):
        last = (cells - 1) * rows if m < parts - 1 else rows
        ends_ref[(me ^ m) + 1, 0] = heads[m][cells : cells + rows, :]
        ends_ref[(me ^ m) + 1, 1] = heads[m][cells + last : cells + last + rows, :]


def fill_weights(index_ref, curves_ref, scale, weight_ref):
    passes = index_ref.shape[0]
    channels, knots = curves_ref.shape[1:]
    width = weight_ref.shape[1]
    block = knots * SUB
    points = jnp.concatenate([curves_ref[index_ref[p]] for p in range(passes)], axis=0)
    channel = lax.broadcasted_iota(jnp.int32, points.shape, 0) % channels
    points = jnp.where(channel == channels - 1, points * scale, points)
    knot = lax.broadcasted_iota(jnp.int32, (knots, width), 0)
    lane = lax.broadcasted_iota(jnp.int32, (knots, width), 1)
    target = lane // SUB % knots
    here = jnp.where(knot == target, 1.0, 0.0)
    after = jnp.where(knot == target + 1, 1.0, 0.0)
    is_slope = jnp.logical_and(lane >= block, lane < 2 * block)
    spread = jnp.where(is_slope, after - here, here)
    values = jnp.dot(points, spread, precision=lax.Precision.HIGHEST, preferred_element_type=jnp.float32)
    shape = (2 * SUB, width)
    row = lax.broadcasted_iota(jnp.int32, shape, 0)
    lane = lax.broadcasted_iota(jnp.int32, shape, 1)
    on_row = lane % SUB == row % SUB
    for pair in range(passes * channels // 2):
        upper, lower = [jnp.broadcast_to(values[2 * pair + j : 2 * pair + j + 1], shape) for j in range(2)]
        value = jnp.where(on_row, jnp.where(row < SUB, upper, lower), 0.0)
        coarse = value.astype(jnp.bfloat16).astype(jnp.float32)
        value = jnp.where(lane < 2 * block, value, value - coarse)
        weight_ref[2 * pair * SUB : 2 * (pair + 1) * SUB, :] = value.astype(jnp.bfloat16)


def prepare_steps(m, zs, where, lateral, base, cells, rows, parts, cols, ends_ref, weight_ref, cell_ref, mixed_ref):
    me = lax.axis_index("depth")
    part = me ^ m
    at = pl.ds(base, SUB)
    lane = lax.broadcasted_iota(jnp.int32, (SUB, cols), 1)
    sublane = lax.broadcasted_iota(jnp.int32, (SUB, cols), 0)
    is_first = lane == 0
    is_last = lane == cols - 1
    places, tops, bottoms = where
    group = rows // parts
    got = lateral[pl.ds(pl.multiple_of(base % group, SUB), SUB), :]
    sides = pltpu.roll(got, (2 * cols - 1 - base // group * (cols // parts)) % cols, 1)

    def layer(z):
        if z < 0:
            return ends_ref[part, 1, at, :]
        if z == cells:
            return ends_ref[part + 2, 0, at, :]
        ref, low = places[z]
        return ref[pl.ds(low + base, SUB), :]

    def step(z):
        ref, low = places[z]
        here = layer(z)
        top_at, top_ref, top = tops[z]
        bottom_at, bottom_ref, bottom = bottoms[z]
        is_top = jnp.logical_and(sublane == 0, base == top_at)
        is_bottom = jnp.logical_and(sublane == SUB - 1, base == bottom_at)
        upper = jnp.where(is_top, top_ref[top : top + 1, :], ref[pl.ds(low + base - 1, SUB), :])
        lower = jnp.where(is_bottom, bottom_ref[bottom : bottom + 1, :], ref[pl.ds(low + base + 1, SUB), :])
        edge = pltpu.roll(sides, (cols - 2 * z) % cols, 1) if z else sides
        grad_x = pltpu.roll(jnp.where(is_first, edge, here), cols - 1, 1) - pltpu.roll(
            jnp.where(is_last, edge, here), 1, 1
        )
        grad_y = lower - upper
        grad_z = layer(z + 1) - layer(z - 1)
        inverse = lax.rsqrt(grad_x * grad_x + grad_y * grad_y + grad_z * grad_z + 4.0)
        cell_ref[0, z] = grad_x * inverse
        cell_ref[1, z] = grad_y * inverse
        cell_ref[2, z] = grad_z * inverse
        half = 0.5 * (knots - 1)
        position = half + half * jnp.tanh(0.5 * here)
        coarse = (position + FINE) - FINE
        segment = jnp.minimum(jnp.floor(position), knots - 2.0)
        rest = position - coarse
        right = coarse - segment
        left = 1.0 - right
        twice = lambda value: jnp.concatenate([value, value], axis=0).astype(jnp.bfloat16)
        left, right, rest, segment = twice(left), twice(right), twice(rest), twice(segment)
        zero = jnp.zeros_like(left)
        tents, rests = [], []
        for k in range(0, knots, 2):
            is_here = segment == pair_at + k
            is_before = segment == pair_at + (k - 1)
            tents.append(jnp.where(is_here, left, jnp.where(is_before, right, zero)))
            rests.append(jnp.where(is_here, rest, zero))
        return [jnp.concatenate(part, axis=0) for part in (tents, rests)]

    def two(first, second):
        tents, rests = [jnp.concatenate(both, axis=1) for both in zip(step(first), step(second))]
        right = jnp.concatenate([tents, rests, tents], axis=0)
        mixed = jnp.dot(weight_ref[...], right, preferred_element_type=jnp.float32)
        mixed_ref[first] = mixed[:, :cols]
        mixed_ref[second] = mixed[:, cols:]

    knots = weight_ref.shape[1] // (3 * SUB)
    pair_at = jnp.where(lax.broadcasted_iota(jnp.int32, (2 * SUB, cols), 0) < SUB, 0.0, 1.0).astype(jnp.bfloat16)
    zs = list(zs)
    return [functools.partial(two, *zs[i : i + 2]) for i in range(0, len(zs), 2)]


def march_unit(flip, vector_ref, zs, cells, cell_ref, mixed_ref, beside, inner=None):
    passes = vector_ref.shape[0]
    channels = mixed_ref.shape[1] // (passes * SUB)
    shape = vector_ref.shape[2:]
    vectors = [[vector_ref[p, axis] for axis in range(3)] for p in range(passes)]
    state = [(jnp.ones(shape, jnp.float32), [jnp.zeros(shape, jnp.float32)] * 3)] * passes
    count = len(beside)
    for u, spot in enumerate(zs):
        for step in beside[u * count // len(zs) : (u + 1) * count // len(zs)]:
            step()
        z = spot + flip * (cells - 1 - 2 * spot)
        normal = [cell_ref[axis, z] for axis in range(3)]
        for p in range(passes):
            keep, sums = state[p]
            mixed = [mixed_ref[z, (p * channels + c) * SUB : (p * channels + c + 1) * SUB, :] for c in range(channels)]
            facing = normal[0] * vectors[p][0] + normal[1] * vectors[p][1] + normal[2] * vectors[p][2]
            taken = keep * mixed[3]
            weight = taken * (AMBIENT + jnp.abs(facing))
            sums = [total + weight * tint for total, tint in zip(sums, mixed)]
            keep = keep - taken
            if inner is not None and u == 0:
                keep, sums = keep * inner(p, 0), [total + keep * inner(p, j + 1) for j, total in enumerate(sums)]
            state[p] = (keep, sums)
    return [[keep] + sums for keep, sums in state]


def march_tiles(count, start, prepare, unit):
    def ahead(index, slot):
        return prepare(pl.multiple_of((index + 1) * SUB, SUB), 1 - slot)

    for step in prepare(start * SUB, 0):
        step()

    def pair(i, carry):
        for slot in range(2):
            index = start + 2 * i + slot
            unit(index, slot, ahead(index, slot))
        return carry

    lax.fori_loop(0, count // 2 - 1, pair, 0)
    unit(start + count - 2, 0, ahead(start + count - 2, 0))
    unit(start + count - 1, 1, [])


def own_kernel(parts, index_ref, flip_ref, lights_ref, curves_ref, own_ref, lateral_ref, out_ref, vector_ref, weight_ref, *refs):
    cell_refs, mixed_refs = refs[:2], refs[2:]
    rows, cols = out_ref.shape[1:]
    channels = curves_ref.shape[1]
    passes = index_ref.shape[0]
    cells = cell_refs[0].shape[1]
    flip = flip_ref[0]
    tiles = rows // SUB
    inner = range(1, cells - 1)
    for p in range(passes):
        for axis in range(3):
            vector_ref[p, axis] = jnp.full((SUB, cols), lights_ref[index_ref[p], axis])
    fill_weights(index_ref, curves_ref, OPACITY / (parts * cells), weight_ref)
    places = near_places(cells, rows, own_ref)

    def prepare(base, slot):
        return prepare_steps(
            0, inner, places, lateral_ref, base, cells, rows, parts, cols, None, weight_ref, cell_refs[slot], mixed_refs[slot]
        )

    def unit(index, slot, beside):
        base = pl.multiple_of(index * SUB, SUB)
        result = march_unit(flip, vector_ref, inner, cells, cell_refs[slot], mixed_refs[slot], beside)
        for p in range(passes):
            for j in range(channels):
                out_ref[p * channels + j, pl.ds(base, SUB), :] = result[p][j]

    march_tiles(tiles, 0, prepare, unit)


def near_kernel(parts, flip_ref, vector_ref, weight_ref, inner_ref, *refs):
    count = parts - 1
    heads, laterals, out_ref, ends_ref = refs[:parts], refs[parts : 2 * parts - 1], refs[2 * parts - 1], refs[2 * parts]
    cell_refs, mixed_refs = refs[2 * parts + 1 : 2 * parts + 1 + count], refs[2 * parts + 1 + count :]
    rows, cols = out_ref.shape[2:]
    cells = cell_refs[0].shape[1]
    passes = vector_ref.shape[0]
    channels = inner_ref.shape[0] // passes
    flip = flip_ref[0]
    tiles = rows // SUB
    zs = [(0, cells - 1)] + [range(cells)] * (count - 1)
    places = [near_places(cells, rows, head) for head in heads[:count]]
    fill_ends(parts, cells, rows, heads, ends_ref)

    def prepare(m, base):
        return prepare_steps(
            m, zs[m], places[m], laterals[m], base, cells, rows, parts, cols, ends_ref, weight_ref, cell_refs[m], mixed_refs[m]
        )

    def others(base):
        return [step for m in range(count - 1) for step in prepare(m, base)]

    def unit(i, ahead):
        base = pl.multiple_of(i * SUB, SUB)
        at = pl.ds(base, SUB)
        last = prepare(count - 1, base)
        lengths = [len(z) for z in zs[:-1]]
        cuts = [len(last) * sum(lengths[:m]) // sum(lengths) for m in range(count)]
        for m in range(count):
            beside = ahead if m == count - 1 else last[cuts[m] : cuts[m + 1]]
            inner = (lambda p, j: inner_ref[p * channels + j, at, :]) if m == 0 else None
            result = march_unit(flip, vector_ref, zs[m], cells, cell_refs[m], mixed_refs[m], beside, inner)
            for p in range(passes):
                for j in range(channels):
                    out_ref[m, p * channels + j, at, :] = result[p][j]

    def tile(i, carry):
        unit(i, others(pl.multiple_of((i + 1) * SUB, SUB)))
        return carry

    for step in others(0):
        step()
    lax.fori_loop(0, tiles - 1, tile, 0)
    unit(tiles - 1, [])


def over_either(first_leads, one, other):
    shape = one[0].shape
    unit = jnp.ones(shape, jnp.float32)
    scale_one = jnp.where(first_leads, unit, other[0])
    scale_other = jnp.where(first_leads, one[0], unit)
    return [one[0] * other[0]] + [scale_one * a + scale_other * b for a, b in zip(one[1:], other[1:])]


def far_kernel(parts, split, low, high, flip_ref, vector_ref, weight_ref, *refs):
    heads, body, refs = refs[:parts], refs[parts], refs[parts + 1 :]
    rest, refs = (refs[0], refs[2:]) if low else (None, refs)
    states, out_ref, picture_ref, ends_ref, sems = refs[:5]
    cell_refs, mixed_refs = refs[5:7], refs[7:]
    channels, rows, cols = out_ref.shape[1:]
    cells = cell_refs[0].shape[1]
    passes = vector_ref.shape[0]
    flip = flip_ref[0]
    me = lax.axis_index("depth")
    places = far_places(cells, rows, parts, split, heads[-1], body, rest)
    fill_ends(parts, cells, rows, heads, ends_ref)
    tiles = range(low // SUB, high // SUB)

    def prepare(base, slot):
        return prepare_steps(
            parts - 1, range(cells), places, body, base, cells, rows, parts, cols, ends_ref, weight_ref, cell_refs[slot], mixed_refs[slot]
        )

    def send(index):
        at = pl.ds(pl.multiple_of(index * SUB, SUB), SUB)
        return pltpu.make_async_copy(picture_ref.at[:, :, at, :], out_ref.at[:, :, at, :], sems.at[index])

    def finish(result, index):
        at = pl.ds(pl.multiple_of(index * SUB, SUB), SUB)
        for p in range(passes):
            images = [[states[m, p * channels + j, at, :] for j in range(channels)] for m in range(parts - 1)]
            images.append(result[p])
            bit = 0
            while len(images) > 1:
                leads = ((me >> bit) & 1) == flip
                images = [over_either(leads, images[j], images[j + 1]) for j in range(0, len(images), 2)]
                bit += 1
            for channel in range(3):
                picture_ref[p, channel, at, :] = images[0][channel + 1]
            picture_ref[p, 3, at, :] = 1.0 - images[0][0]
        send(index).start()

    def unit(index, slot, beside):
        finish(march_unit(flip, vector_ref, range(cells), cells, cell_refs[slot], mixed_refs[slot], beside), index)

    march_tiles(len(tiles), tiles[0], prepare, unit)
    for index in tiles:
        send(index).wait()


def swap_pairs(block, axis, start):
    pairs = [(i, i + 1) for i in range(start, lax.axis_size(axis) - 1, 2)]
    return lax.ppermute(block, axis, pairs + [(j, i) for i, j in pairs])


def swap_along(block, axis, mask):
    return lax.ppermute(block, axis, [(i, i ^ mask) for i in range(lax.axis_size(axis))])


def estimate(micros):
    return pl.CostEstimate(flops=int(micros * 1_000_000_000), transcendentals=0, bytes_accessed=0)


def on_device(field, light_vectors, transfer, light_index, flips):
    parts = lax.axis_size("depth")
    cells, all_rows, cols = field.shape
    rows = all_rows // parts
    passes = light_index.shape[0]
    channels, knots = transfer.shape[1:]
    tiles = rows // SUB
    values = passes * channels
    in_vmem = pl.BlockSpec(memory_space=VMEM)
    in_smem = pl.BlockSpec(memory_space=SMEM)
    in_any = pl.BlockSpec(memory_space=pl.ANY)
    in_hbm = pl.BlockSpec(memory_space=pltpu.HBM)

    def array(*shape):
        return jax.ShapeDtypeStruct(shape, jnp.float32)

    def settings(mib, micros):
        return dict(
            compiler_params=pltpu.CompilerParams(vmem_limit_bytes=mib * MIB),
            cost_estimate=pl.CostEstimate(flops=int(micros * 1e9), transcendentals=0, bytes_accessed=0),
        )

    near_rows = 2 * cells + cells * rows
    head_rows = 2 * cells + 2 * rows
    skip = rows // parts
    split = rows // 2
    body_rows = skip + (cells - 2) * split + cells
    rest_rows = (cells - 2) * (rows - split) + 2 * SUB
    *packed, far_head = pl.pallas_call(
        functools.partial(pack_kernel, parts),
        out_shape=[array(near_rows, cols)] * (parts - 2) + [array(head_rows, cols)],
        in_specs=[in_hbm],
        out_specs=[in_vmem] * (parts - 1),
        scratch_shapes=[VMEM((parts - 1, 2, cells, SUB, cols), jnp.float32), pltpu.SemaphoreType.DMA((6, parts - 1))],
        name="pack",
        **settings(8, 1),
    )(pltpu.with_memory_space_constraint(field, pltpu.HBM))
    near = [swap_along(packed[m - 1], "depth", m) for m in range(1, parts - 1)]

    far_head = swap_along(far_head, "depth", parts - 1)

    edges, own, far_body, far_rest = pl.pallas_call(
        functools.partial(edge_kernel, parts, split),
        out_shape=[array(rows, cols), array(near_rows, cols), array(body_rows, cols), array(rest_rows, cols)],
        in_specs=[in_vmem, in_any],
        out_specs=[in_vmem] * 4,
        name="edges",
        **settings(8, 1),
    )(field, packed[0])
    sides = pl.pallas_call(
        functools.partial(side_kernel, parts),
        out_shape=[array(skip, cols)] * parts,
        in_specs=[in_vmem] * 2 + [in_any],
        out_specs=[in_vmem] * parts,
        name="sides",
        **settings(4, 0.1),
    )(swap_pairs(edges, "tile", 0), swap_pairs(edges, "tile", 1), far_head)
    laterals = [swap_along(sides[m], "depth", m) for m in range(1, parts - 1)]
    far_body = swap_along(lax.dynamic_update_slice(far_body, sides[-1], (0, 0)), "depth", parts - 1)
    *laterals, far_rest = lax.optimization_barrier((*laterals, far_rest))
    far_rest = swap_along(far_rest, "depth", parts - 1)

    cell_shape = VMEM((3, cells, SUB, cols), jnp.float32)
    mixed_shape = VMEM((cells, values * SUB, cols), jnp.float32)
    ends_shape = VMEM((parts + 2, 2, rows, cols), jnp.float32)
    weight_shape = jax.ShapeDtypeStruct((values * SUB, 3 * knots * SUB), jnp.bfloat16)
    inner, vectors, weights = pl.pallas_call(
        functools.partial(own_kernel, parts),
        out_shape=[array(values, rows, cols), array(passes, 3, SUB, cols), weight_shape],
        in_specs=[in_smem] * 3 + [in_vmem] * 3,
        out_specs=[in_vmem] * 3,
        scratch_shapes=[cell_shape] * 2 + [mixed_shape] * 2,
        name="own",
        **settings(12, 4),
    )(light_index, flips, light_vectors, transfer, own, sides[0])
    states = pl.pallas_call(
        functools.partial(near_kernel, parts),
        out_shape=array(parts - 1, values, rows, cols),
        in_specs=[in_smem] + [in_vmem] * (2 * parts + 2),
        out_specs=in_vmem,
        scratch_shapes=[ends_shape] + [cell_shape] * (parts - 1) + [mixed_shape] * (parts - 1),
        name="near",
        **settings(16, 60),
    )(flips, vectors, weights, inner, own, *near, far_head, sides[0], *laterals)
    picture = None
    for low, high in ((0, split), (split, rows)):
        late = [far_rest, picture] if low else []
        picture = pl.pallas_call(
            functools.partial(far_kernel, parts, split, low, high),
            out_shape=array(passes, channels, rows, cols),
            in_specs=[in_smem] + [in_vmem] * (parts + 3) + [in_vmem, in_any][: len(late)] + [in_vmem],
            out_specs=in_any,
            scratch_shapes=[
                VMEM((passes, channels, rows, cols), jnp.float32),
                ends_shape,
                pltpu.SemaphoreType.DMA((tiles,)),
            ]
            + [cell_shape] * 2
            + [mixed_shape] * 2,
            input_output_aliases={parts + 5: 0} if low else {},
            name="late" if low else "far",
            **settings(16, 2),
        )(flips, vectors, weights, own, *near, far_head, far_body, *late, states)
    return picture


def solution(mesh):
    in_specs = (P("depth", None, "tile"), P(), P(), P(), P("tile"))
    out_specs = P(None, None, "depth", "tile")
    return jax.shard_map(
        on_device, mesh=mesh, in_specs=in_specs, out_specs=out_specs, check_vma=False
    )
```

```python
import functools

import jax
import jax.numpy as jnp
from jax import lax
from jax.experimental import pallas as pl
from jax.experimental.pallas import tpu as pltpu
from jax.sharding import PartitionSpec as P

AMBIENT = 0.3
OPACITY = 2.0
SUB = 8
VMEM = pltpu.VMEM
SMEM = pltpu.SMEM
MIB = 1 << 20
FINE = 49152.0


def pack_kernel(parts, field_ref, *refs):
    outs, (rim_ref, sems) = refs[: parts - 1], refs[parts - 1 :]
    cells, all_rows, cols = field_ref.shape
    rows = all_rows // parts
    me = lax.axis_index("depth")
    copies, rims = [], []
    for j, out in enumerate(outs):
        low = pl.multiple_of((me ^ (j + 1)) * rows, SUB)
        before = pl.multiple_of(jnp.maximum(low - SUB, 0), SUB)
        after = pl.multiple_of(jnp.minimum(low + rows, all_rows - SUB), SUB)
        for side, start in enumerate((before, after)):
            source = field_ref.at[:, pl.ds(start, SUB), :]
            rims.append(pltpu.make_async_copy(source, rim_ref.at[j, side], sems.at[side, j]))
        block = field_ref.at[:, pl.ds(low, rows), :]
        if j < parts - 2:
            centre = out.at[pl.ds(cells, cells * rows), :].reshape(cells, rows, cols)
            quarter = cells // 4
            for q in range(4):
                layers = pl.ds(q * quarter, quarter)
                copies.append(pltpu.make_async_copy(block.at[layers], centre.at[layers], sems.at[2 + q, j]))
        else:
            for side in range(2):
                layer = out.at[pl.ds(cells + side * rows, rows), :]
                copies.append(pltpu.make_async_copy(block.at[side * (cells - 1)], layer, sems.at[2 + side, j]))
    for copy in rims + copies:
        copy.start()
    for copy in rims:
        copy.wait()
    for j, out in enumerate(outs):
        part = me ^ (j + 1)
        above = jnp.where(part > 0, 1.0, 0.0)
        below = jnp.where(part < parts - 1, 1.0, 0.0)
        for z in range(cells):
            out[z : z + 1, :] = rim_ref[j, 0, z, SUB - 1 : SUB, :] * above
            below_at = out.shape[0] - cells + z
            out[below_at : below_at + 1, :] = rim_ref[j, 1, z, 0:1, :] * below
    for copy in copies:
        copy.wait()


def edge_kernel(parts, split, field_ref, _, edge_ref, own_ref, body_ref, rest_ref):
    cells, all_rows, cols = field_ref.shape
    rows = all_rows // parts
    me = lax.axis_index("depth")
    lane_pair = lax.broadcasted_iota(jnp.int32, (SUB, cols), 1) // 2

    def tile(i, carry):
        acc = jnp.zeros((SUB, cols), jnp.float32)
        for part in range(parts):
            for z in range(cells):
                slot = part * cells + z
                start = pl.multiple_of(part * rows + i * SUB, SUB)
                value = field_ref[z, pl.ds(start, SUB), :]
                moved = pltpu.roll(value, (2 * slot + 1) % cols, 1)
                acc = jnp.where(lane_pair == slot, moved, acc)
        edge_ref[pl.ds(pl.multiple_of(i * SUB, SUB), SUB), :] = acc
        return carry

    lax.fori_loop(0, rows // SUB, tile, 0)
    low = pl.multiple_of(me * rows, SUB)
    above = jnp.where(me > 0, 1.0, 0.0)
    below = jnp.where(me < parts - 1, 1.0, 0.0)
    for z in range(cells):
        own_ref[z : z + 1, :] = field_ref[z, pl.ds(jnp.maximum(low - 1, 0), 1), :] * above
        below_at = cells + cells * rows + z
        own_ref[below_at : below_at + 1, :] = field_ref[z, pl.ds(jnp.minimum(low + rows, all_rows - 1), 1), :] * below
    far_low = pl.multiple_of((me ^ (parts - 1)) * rows, SUB)
    own_places, _, _ = near_places(cells, rows, own_ref)
    for z in range(cells):
        ref, start = own_places[z]
        ref[start : start + rows, :] = field_ref[z, pl.ds(low, rows), :]
    skip, more = rows // parts, rows - split
    for z in range(1, cells - 1):
        at = skip + (z - 1) * split
        body_ref[at : at + split, :] = field_ref[z, pl.ds(far_low, split), :]
        next_row = skip + (cells - 2) * split + z - 1
        body_ref[next_row : next_row + 1, :] = field_ref[z, pl.ds(far_low + split, 1), :]
        at = SUB + (z - 1) * more
        rest_ref[at : at + more, :] = field_ref[z, pl.ds(far_low + split, more), :]


def side_kernel(parts, even_ref, odd_ref, _, *outs):
    rows, cols = even_ref.shape
    group = rows // parts
    width = cols // parts
    me = lax.axis_index("depth")
    lane = lax.broadcasted_iota(jnp.int32, (rows, cols), 1)
    tile = lax.axis_index("tile")
    sides = jnp.where((lane + tile) % 2 == 1, even_ref[...], odd_ref[...])
    for m in range(parts):
        acc = jnp.zeros((group, cols), jnp.float32)
        for j in range(parts):
            moved = pltpu.roll(sides[j * group : (j + 1) * group], (j - (me ^ m) + parts) * width % cols, 1)
            acc = jnp.where(lane[:group] // width == j, moved, acc)
        outs[m][...] = acc


def near_places(cells, rows, head):
    count = head.shape[0]
    places = [(head, cells + z * rows) for z in range(cells)]
    tops = [(0, head, z) for z in range(cells)]
    bottoms = [(rows - SUB, head, count - cells + z) for z in range(cells)]
    return places, tops, bottoms


def far_places(cells, rows, parts, split, head, body, rest=None):
    skip, more = rows // parts, rows - split
    places, tops, bottoms = near_places(cells, rows, head)
    places[0], places[-1] = (head, cells), (head, cells + rows)
    for z in range(1, cells - 1):
        if rest is None:
            places[z] = (body, skip + (z - 1) * split)
            bottoms[z] = (split - SUB, body, skip + (cells - 2) * split + z - 1)
        else:
            places[z] = (rest, SUB + (z - 1) * more - split)
            tops[z] = (split, body, skip + z * split - 1)
    return places, tops, bottoms


def fill_ends(parts, cells, rows, heads, ends_ref):
    me = lax.axis_index("depth")
    ends_ref[0, 1] = jnp.zeros_like(ends_ref[0, 1])
    ends_ref[parts + 1, 0] = jnp.zeros_like(ends_ref[0, 0])
    for m in range(parts):
        last = (cells - 1) * rows if m < parts - 1 else rows
        ends_ref[(me ^ m) + 1, 0] = heads[m][cells : cells + rows, :]
        ends_ref[(me ^ m) + 1, 1] = heads[m][cells + last : cells + last + rows, :]


def fill_weights(index_ref, curves_ref, scale, weight_ref):
    passes = index_ref.shape[0]
    channels, knots = curves_ref.shape[1:]
    width = weight_ref.shape[1]
    block = knots * SUB
    points = jnp.concatenate([curves_ref[index_ref[p]] for p in range(passes)], axis=0)
    channel = lax.broadcasted_iota(jnp.int32, points.shape, 0) % channels
    points = jnp.where(channel == channels - 1, points * scale, points)
    knot = lax.broadcasted_iota(jnp.int32, (knots, width), 0)
    lane = lax.broadcasted_iota(jnp.int32, (knots, width), 1)
    target = lane // SUB % knots
    here = jnp.where(knot == target, 1.0, 0.0)
    after = jnp.where(knot == target + 1, 1.0, 0.0)
    is_slope = jnp.logical_and(lane >= block, lane < 2 * block)
    spread = jnp.where(is_slope, after - here, here)
    values = jnp.dot(points, spread, precision=lax.Precision.HIGHEST, preferred_element_type=jnp.float32)
    shape = (2 * SUB, width)
    row = lax.broadcasted_iota(jnp.int32, shape, 0)
    lane = lax.broadcasted_iota(jnp.int32, shape, 1)
    on_row = lane % SUB == row % SUB
    for pair in range(passes * channels // 2):
        upper, lower = [jnp.broadcast_to(values[2 * pair + j : 2 * pair + j + 1], shape) for j in range(2)]
        value = jnp.where(on_row, jnp.where(row < SUB, upper, lower), 0.0)
        coarse = value.astype(jnp.bfloat16).astype(jnp.float32)
        value = jnp.where(lane < 2 * block, value, value - coarse)
        weight_ref[2 * pair * SUB : 2 * (pair + 1) * SUB, :] = value.astype(jnp.bfloat16)


def prepare_steps(m, zs, where, lateral, base, cells, rows, parts, cols, ends_ref, weight_ref, cell_ref, mixed_ref):
    me = lax.axis_index("depth")
    part = me ^ m
    at = pl.ds(base, SUB)
    lane = lax.broadcasted_iota(jnp.int32, (SUB, cols), 1)
    sublane = lax.broadcasted_iota(jnp.int32, (SUB, cols), 0)
    is_first = lane == 0
    is_last = lane == cols - 1
    places, tops, bottoms = where
    group = rows // parts
    got = lateral[pl.ds(pl.multiple_of(base % group, SUB), SUB), :]
    sides = pltpu.roll(got, (2 * cols - 1 - base // group * (cols // parts)) % cols, 1)

    def layer(z):
        if z < 0:
            return ends_ref[part, 1, at, :]
        if z == cells:
            return ends_ref[part + 2, 0, at, :]
        ref, low = places[z]
        return ref[pl.ds(low + base, SUB), :]

    def step(z):
        ref, low = places[z]
        here = layer(z)
        top_at, top_ref, top = tops[z]
        bottom_at, bottom_ref, bottom = bottoms[z]
        is_top = jnp.logical_and(sublane == 0, base == top_at)
        is_bottom = jnp.logical_and(sublane == SUB - 1, base == bottom_at)
        upper = jnp.where(is_top, top_ref[top : top + 1, :], ref[pl.ds(low + base - 1, SUB), :])
        lower = jnp.where(is_bottom, bottom_ref[bottom : bottom + 1, :], ref[pl.ds(low + base + 1, SUB), :])
        edge = pltpu.roll(sides, (cols - 2 * z) % cols, 1) if z else sides
        grad_x = pltpu.roll(jnp.where(is_first, edge, here), cols - 1, 1) - pltpu.roll(
            jnp.where(is_last, edge, here), 1, 1
        )
        grad_y = lower - upper
        grad_z = layer(z + 1) - layer(z - 1)
        inverse = lax.rsqrt(grad_x * grad_x + grad_y * grad_y + grad_z * grad_z + 4.0)
        cell_ref[0, z] = grad_x * inverse
        cell_ref[1, z] = grad_y * inverse
        cell_ref[2, z] = grad_z * inverse
        half = 0.5 * (knots - 1)
        position = half + half * jnp.tanh(0.5 * here)
        coarse = (position + FINE) - FINE
        segment = jnp.minimum(jnp.floor(position), knots - 2.0)
        rest = position - coarse
        right = coarse - segment
        left = 1.0 - right
        twice = lambda value: jnp.concatenate([value, value], axis=0).astype(jnp.bfloat16)
        left, right, rest, segment = twice(left), twice(right), twice(rest), twice(segment)
        zero = jnp.zeros_like(left)
        tents, rests = [], []
        for k in range(0, knots, 2):
            is_here = segment == pair_at + k
            is_before = segment == pair_at + (k - 1)
            tents.append(jnp.where(is_here, left, jnp.where(is_before, right, zero)))
            rests.append(jnp.where(is_here, rest, zero))
        return [jnp.concatenate(part, axis=0) for part in (tents, rests)]

    def two(first, second):
        tents, rests = [jnp.concatenate(both, axis=1) for both in zip(step(first), step(second))]
        right = jnp.concatenate([tents, rests, tents], axis=0)
        mixed = jnp.dot(weight_ref[...], right, preferred_element_type=jnp.float32)
        mixed_ref[first] = mixed[:, :cols]
        mixed_ref[second] = mixed[:, cols:]

    knots = weight_ref.shape[1] // (3 * SUB)
    pair_at = jnp.where(lax.broadcasted_iota(jnp.int32, (2 * SUB, cols), 0) < SUB, 0.0, 1.0).astype(jnp.bfloat16)
    zs = list(zs)
    return [functools.partial(two, *zs[i : i + 2]) for i in range(0, len(zs), 2)]


def march_unit(flip, vector_ref, zs, cells, cell_ref, mixed_ref, beside, inner=None):
    passes = vector_ref.shape[0]
    channels = mixed_ref.shape[1] // (passes * SUB)
    shape = vector_ref.shape[2:]
    vectors = [[vector_ref[p, axis] for axis in range(3)] for p in range(passes)]
    state = [(jnp.ones(shape, jnp.float32), [jnp.zeros(shape, jnp.float32)] * 3)] * passes
    count = len(beside)
    for u, spot in enumerate(zs):
        for step in beside[u * count // len(zs) : (u + 1) * count // len(zs)]:
            step()
        z = spot + flip * (cells - 1 - 2 * spot)
        normal = [cell_ref[axis, z] for axis in range(3)]
        for p in range(passes):
            keep, sums = state[p]
            mixed = [mixed_ref[z, (p * channels + c) * SUB : (p * channels + c + 1) * SUB, :] for c in range(channels)]
            facing = normal[0] * vectors[p][0] + normal[1] * vectors[p][1] + normal[2] * vectors[p][2]
            taken = keep * mixed[3]
            weight = taken * (AMBIENT + jnp.abs(facing))
            sums = [total + weight * tint for total, tint in zip(sums, mixed)]
            keep = keep - taken
            if inner is not None and u == 0:
                keep, sums = keep * inner(p, 0), [total + keep * inner(p, j + 1) for j, total in enumerate(sums)]
            state[p] = (keep, sums)
    return [[keep] + sums for keep, sums in state]


def march_tiles(count, start, prepare, unit):
    def ahead(index, slot):
        return prepare(pl.multiple_of((index + 1) * SUB, SUB), 1 - slot)

    for step in prepare(start * SUB, 0):
        step()

    def pair(i, carry):
        for slot in range(2):
            index = start + 2 * i + slot
            unit(index, slot, ahead(index, slot))
        return carry

    lax.fori_loop(0, count // 2 - 1, pair, 0)
    unit(start + count - 2, 0, ahead(start + count - 2, 0))
    unit(start + count - 1, 1, [])


def own_kernel(parts, index_ref, flip_ref, lights_ref, curves_ref, own_ref, lateral_ref, out_ref, vector_ref, weight_ref, *refs):
    cell_refs, mixed_refs = refs[:2], refs[2:]
    rows, cols = out_ref.shape[1:]
    channels = curves_ref.shape[1]
    passes = index_ref.shape[0]
    cells = cell_refs[0].shape[1]
    flip = flip_ref[0]
    tiles = rows // SUB
    inner = range(1, cells - 1)
    for p in range(passes):
        for axis in range(3):
            vector_ref[p, axis] = jnp.full((SUB, cols), lights_ref[index_ref[p], axis])
    fill_weights(index_ref, curves_ref, OPACITY / (parts * cells), weight_ref)
    places = near_places(cells, rows, own_ref)

    def prepare(base, slot):
        return prepare_steps(
            0, inner, places, lateral_ref, base, cells, rows, parts, cols, None, weight_ref, cell_refs[slot], mixed_refs[slot]
        )

    def unit(index, slot, beside):
        base = pl.multiple_of(index * SUB, SUB)
        result = march_unit(flip, vector_ref, inner, cells, cell_refs[slot], mixed_refs[slot], beside)
        for p in range(passes):
            for j in range(channels):
                out_ref[p * channels + j, pl.ds(base, SUB), :] = result[p][j]

    march_tiles(tiles, 0, prepare, unit)


def near_kernel(parts, flip_ref, vector_ref, weight_ref, inner_ref, *refs):
    count = parts - 1
    heads, laterals, out_ref, ends_ref = refs[:parts], refs[parts : 2 * parts - 1], refs[2 * parts - 1], refs[2 * parts]
    cell_refs, mixed_refs = refs[2 * parts + 1 : 2 * parts + 1 + count], refs[2 * parts + 1 + count :]
    rows, cols = out_ref.shape[2:]
    cells = cell_refs[0].shape[1]
    passes = vector_ref.shape[0]
    channels = inner_ref.shape[0] // passes
    flip = flip_ref[0]
    tiles = rows // SUB
    zs = [(0, cells - 1)] + [range(cells)] * (count - 1)
    places = [near_places(cells, rows, head) for head in heads[:count]]
    fill_ends(parts, cells, rows, heads, ends_ref)

    def prepare(m, base):
        return prepare_steps(
            m, zs[m], places[m], laterals[m], base, cells, rows, parts, cols, ends_ref, weight_ref, cell_refs[m], mixed_refs[m]
        )

    for step in prepare(0, 0):
        step()

    def tile(i, carry):
        base = pl.multiple_of(i * SUB, SUB)
        after = pl.multiple_of(jnp.minimum(i + 1, tiles - 1) * SUB, SUB)
        at = pl.ds(base, SUB)
        for m in range(count):
            beside = prepare(m + 1, base) if m + 1 < count else prepare(0, after)
            inner = (lambda p, j: inner_ref[p * channels + j, at, :]) if m == 0 else None
            result = march_unit(flip, vector_ref, zs[m], cells, cell_refs[m], mixed_refs[m], beside, inner)
            for p in range(passes):
                for j in range(channels):
                    out_ref[m, p * channels + j, at, :] = result[p][j]
        return carry

    lax.fori_loop(0, tiles, tile, 0)


def over_either(first_leads, one, other):
    shape = one[0].shape
    unit = jnp.ones(shape, jnp.float32)
    scale_one = jnp.where(first_leads, unit, other[0])
    scale_other = jnp.where(first_leads, one[0], unit)
    return [one[0] * other[0]] + [scale_one * a + scale_other * b for a, b in zip(one[1:], other[1:])]


def far_kernel(parts, split, low, high, flip_ref, vector_ref, weight_ref, *refs):
    heads, body, refs = refs[:parts], refs[parts], refs[parts + 1 :]
    rest, refs = (refs[0], refs[2:]) if low else (None, refs)
    states, out_ref, picture_ref, ends_ref, sems = refs[:5]
    cell_refs, mixed_refs = refs[5:7], refs[7:]
    channels, rows, cols = out_ref.shape[1:]
    cells = cell_refs[0].shape[1]
    passes = vector_ref.shape[0]
    flip = flip_ref[0]
    me = lax.axis_index("depth")
    places = far_places(cells, rows, parts, split, heads[-1], body, rest)
    fill_ends(parts, cells, rows, heads, ends_ref)
    tiles = range(low // SUB, high // SUB)

    def prepare(base, slot):
        return prepare_steps(
            parts - 1, range(cells), places, body, base, cells, rows, parts, cols, ends_ref, weight_ref, cell_refs[slot], mixed_refs[slot]
        )

    def send(index):
        at = pl.ds(pl.multiple_of(index * SUB, SUB), SUB)
        return pltpu.make_async_copy(picture_ref.at[:, :, at, :], out_ref.at[:, :, at, :], sems.at[index])

    def finish(result, index):
        at = pl.ds(pl.multiple_of(index * SUB, SUB), SUB)
        for p in range(passes):
            images = [[states[m, p * channels + j, at, :] for j in range(channels)] for m in range(parts - 1)]
            images.append(result[p])
            bit = 0
            while len(images) > 1:
                leads = ((me >> bit) & 1) == flip
                images = [over_either(leads, images[j], images[j + 1]) for j in range(0, len(images), 2)]
                bit += 1
            for channel in range(3):
                picture_ref[p, channel, at, :] = images[0][channel + 1]
            picture_ref[p, 3, at, :] = 1.0 - images[0][0]
        send(index).start()

    def unit(index, slot, beside):
        finish(march_unit(flip, vector_ref, range(cells), cells, cell_refs[slot], mixed_refs[slot], beside), index)

    march_tiles(len(tiles), tiles[0], prepare, unit)
    for index in tiles:
        send(index).wait()


def swap_pairs(block, axis, start):
    pairs = [(i, i + 1) for i in range(start, lax.axis_size(axis) - 1, 2)]
    return lax.ppermute(block, axis, pairs + [(j, i) for i, j in pairs])


def swap_along(block, axis, mask):
    return lax.ppermute(block, axis, [(i, i ^ mask) for i in range(lax.axis_size(axis))])


def estimate(micros):
    return pl.CostEstimate(flops=int(micros * 1_000_000_000), transcendentals=0, bytes_accessed=0)


def on_device(field, light_vectors, transfer, light_index, flips):
    parts = lax.axis_size("depth")
    cells, all_rows, cols = field.shape
    rows = all_rows // parts
    passes = light_index.shape[0]
    channels, knots = transfer.shape[1:]
    tiles = rows // SUB
    values = passes * channels
    in_vmem = pl.BlockSpec(memory_space=VMEM)
    in_smem = pl.BlockSpec(memory_space=SMEM)
    in_any = pl.BlockSpec(memory_space=pl.ANY)
    in_hbm = pl.BlockSpec(memory_space=pltpu.HBM)

    def array(*shape):
        return jax.ShapeDtypeStruct(shape, jnp.float32)

    def settings(mib, micros):
        return dict(
            compiler_params=pltpu.CompilerParams(vmem_limit_bytes=mib * MIB),
            cost_estimate=pl.CostEstimate(flops=int(micros * 1e9), transcendentals=0, bytes_accessed=0),
        )

    near_rows = 2 * cells + cells * rows
    head_rows = 2 * cells + 2 * rows
    skip = rows // parts
    split = rows // 2
    body_rows = skip + (cells - 2) * split + cells
    rest_rows = (cells - 2) * (rows - split) + 2 * SUB
    *packed, far_head = pl.pallas_call(
        functools.partial(pack_kernel, parts),
        out_shape=[array(near_rows, cols)] * (parts - 2) + [array(head_rows, cols)],
        in_specs=[in_hbm],
        out_specs=[in_vmem] * (parts - 1),
        scratch_shapes=[VMEM((parts - 1, 2, cells, SUB, cols), jnp.float32), pltpu.SemaphoreType.DMA((6, parts - 1))],
        name="pack",
        **settings(8, 1),
    )(pltpu.with_memory_space_constraint(field, pltpu.HBM))
    near = [swap_along(packed[m - 1], "depth", m) for m in range(1, parts - 1)]

    far_head = swap_along(far_head, "depth", parts - 1)

    edges, own, far_body, far_rest = pl.pallas_call(
        functools.partial(edge_kernel, parts, split),
        out_shape=[array(rows, cols), array(near_rows, cols), array(body_rows, cols), array(rest_rows, cols)],
        in_specs=[in_vmem, in_any],
        out_specs=[in_vmem] * 4,
        name="edges",
        **settings(8, 1),
    )(field, packed[0])
    sides = pl.pallas_call(
        functools.partial(side_kernel, parts),
        out_shape=[array(skip, cols)] * parts,
        in_specs=[in_vmem] * 2 + [in_any],
        out_specs=[in_vmem] * parts,
        name="sides",
        **settings(4, 0.1),
    )(swap_pairs(edges, "tile", 0), swap_pairs(edges, "tile", 1), far_head)
    laterals = [swap_along(sides[m], "depth", m) for m in range(1, parts - 1)]
    far_body = swap_along(lax.dynamic_update_slice(far_body, sides[-1], (0, 0)), "depth", parts - 1)
    *laterals, far_rest = lax.optimization_barrier((*laterals, far_rest))
    far_rest = swap_along(far_rest, "depth", parts - 1)

    cell_shape = VMEM((3, cells, SUB, cols), jnp.float32)
    mixed_shape = VMEM((cells, values * SUB, cols), jnp.float32)
    ends_shape = VMEM((parts + 2, 2, rows, cols), jnp.float32)
    weight_shape = jax.ShapeDtypeStruct((values * SUB, 3 * knots * SUB), jnp.bfloat16)
    inner, vectors, weights = pl.pallas_call(
        functools.partial(own_kernel, parts),
        out_shape=[array(values, rows, cols), array(passes, 3, SUB, cols), weight_shape],
        in_specs=[in_smem] * 3 + [in_vmem] * 3,
        out_specs=[in_vmem] * 3,
        scratch_shapes=[cell_shape] * 2 + [mixed_shape] * 2,
        name="own",
        **settings(12, 4),
    )(light_index, flips, light_vectors, transfer, own, sides[0])
    states = pl.pallas_call(
        functools.partial(near_kernel, parts),
        out_shape=array(parts - 1, values, rows, cols),
        in_specs=[in_smem] + [in_vmem] * (2 * parts + 2),
        out_specs=in_vmem,
        scratch_shapes=[ends_shape] + [cell_shape] * (parts - 1) + [mixed_shape] * (parts - 1),
        name="near",
        **settings(16, 60),
    )(flips, vectors, weights, inner, own, *near, far_head, sides[0], *laterals)
    picture = None
    for low, high in ((0, split), (split, rows)):
        late = [far_rest, picture] if low else []
        picture = pl.pallas_call(
            functools.partial(far_kernel, parts, split, low, high),
            out_shape=array(passes, channels, rows, cols),
            in_specs=[in_smem] + [in_vmem] * (parts + 3) + [in_vmem, in_any][: len(late)] + [in_vmem],
            out_specs=in_any,
            scratch_shapes=[
                VMEM((passes, channels, rows, cols), jnp.float32),
                ends_shape,
                pltpu.SemaphoreType.DMA((tiles,)),
            ]
            + [cell_shape] * 2
            + [mixed_shape] * 2,
            input_output_aliases={parts + 5: 0} if low else {},
            name="late" if low else "far",
            **settings(16, 2),
        )(flips, vectors, weights, own, *near, far_head, far_body, *late, states)
    return picture


def solution(mesh):
    in_specs = (P("depth", None, "tile"), P(), P(), P(), P("tile"))
    out_specs = P(None, None, "depth", "tile")
    return jax.shard_map(
        on_device, mesh=mesh, in_specs=in_specs, out_specs=out_specs, check_vma=False
    )
```
